512 devices in a mesh: frame: 64 (over y, z), band: 8 (over x, core).
Axes of the slice: x: 4, y: 8, z: 8, core: 2. Of those that a mesh axis runs over, the one named last changes fastest.
Arguments:
- tokens: bfloat16 [8192, 3072], P(('frame', 'band')), may hold values from -6 to 6
- qkv_weight: bfloat16 [3072, 3, 2048], P('frame', None, 'band'), may hold values from -1 to 1, as said below
- out_weight: bfloat16 [2048, 3072], P('frame', 'band'), may hold values from -0.125 to 0.125
- head_kind: int32 [16], P('band'), may hold values from 0 to 1
Outputs:
- attended: bfloat16 [8192, 3072], P(('frame', 'band'))
The draws below stay inside these ranges and needn't reach their ends.
Inputs may be any that keep to these rules, and one draw needn't show every extreme that they name: `head_kind`: 0 marks a spatial head, 1 a temporal head. `qkv_weight`: entries lie within 4 * 3072^-0.5 in magnitude.
All inputs are finite; a program needn't handle non-finite values.
Results may differ from the reference program's by a relative error of at most 0.022.
Values may be sent and summed in bfloat16 or wider, within the bound.
A program may use at most 64 MiB of HBM per device.

```python
import jax
import jax.numpy as jnp
from jax import lax

D = 3072
HEAD = 128
HEAD_DEV = 2
HEADS = 16
POSITIONS = 128
FRAMES = 64
TOKENS = 8192
N_BAND = 8


def draw_tokens(key, part):
    key = jax.random.fold_in(key, 11)
    rest_key = jax.random.fold_in(key, 4)
    return jax.random.truncated_normal(rest_key, -6.0, 6.0, (TOKENS, D), jnp.float32).astype(jnp.bfloat16)


def draw_qkv_weight(key, part):
    key = jax.random.fold_in(key, 23)
    query_key, second_key, value_key = jax.random.split(key, 3)
    spread = D ** (-0.5)
    query_part = spread * jax.random.truncated_normal(query_key, -4.0, 4.0, (D, HEADS * HEAD), jnp.float32)
    value_part = spread * jax.random.truncated_normal(value_key, -4.0, 4.0, (D, HEADS * HEAD), jnp.float32)
    key_part = spread * jax.random.truncated_normal(second_key, -4.0, 4.0, (D, HEADS * HEAD), jnp.float32)
    return jnp.stack([query_part, key_part, value_part], axis=1).astype(jnp.bfloat16)


def plant(drawn, key, low, high):
    shape = drawn.shape
    spot = [jax.random.randint(jax.random.fold_in(key, axis), (), 0, shape[axis]) for axis in range(len(shape))]
    drawn = drawn.at[tuple(spot)].set(low)
    longest = shape.index(max(shape))
    spot[longest] = (spot[longest] + 1) % shape[longest]
    return drawn.at[tuple(spot)].set(high)


def levels(rng, dims, pieces, least, top_value):
    def one(dim, blocks):
        heights = jax.random.uniform(jax.random.fold_in(jax.random.fold_in(rng, 6), dim), (blocks,), jnp.float32, least / len(pieces), top_value / len(pieces))
        return jnp.repeat(jnp.exp(heights), dims[dim] // blocks).reshape((-1,) + (1,) * (len(dims) - dim - 1))

    loudness = one(*pieces[0])
    for cut in pieces[1:]:
        loudness = loudness * one(*cut)
    return loudness


def noise(key, dims, width, bound, cuts=(), kind=jnp.bfloat16):
    factor_of = levels(key, dims, cuts, -0.22, 0.18) if cuts else 1.0
    result = jax.random.normal(key, dims, jnp.float32) * width * factor_of
    return jnp.minimum(jnp.maximum(result, -bound), bound).astype(kind)


def setup_inputs(seed: int = 0) -> dict:
    key_of = jax.random.split(jax.random.key(seed), 5)
    tokens = draw_tokens(jax.random.fold_in(key_of[4], 71), 0)
    qkv_weight = draw_qkv_weight(jax.random.fold_in(key_of[4], 71), 0)
    out_weight = noise(key_of[2], (HEADS * HEAD, D), (HEADS * HEAD) ** -0.5, 0.125, ((0, 64), (1, 8)))
    head_kind = plant(jax.random.randint(key_of[3], (HEADS,), 0, 2), jax.random.fold_in(key_of[3], 1), 0, 1).astype(jnp.int32)
    return {"tokens": tokens, "qkv_weight": qkv_weight, "out_weight": out_weight, "head_kind": head_kind}


def softmax_rows(scores):
    largest = jnp.max(scores, axis=-1, keepdims=True)
    raised = jnp.exp(scores - largest)
    return (raised / jnp.sum(raised, axis=-1, keepdims=True)).astype(jnp.bfloat16)


def reference(tokens, qkv_weight, out_weight, head_kind):
    scale_factor = HEAD ** -0.5
    summed = jnp.dot(tokens, qkv_weight.reshape(D, 3 * HEADS * HEAD), preferred_element_type=jnp.float32)
    projected = summed.astype(jnp.bfloat16).reshape(FRAMES, POSITIONS, 3, HEADS, HEAD)

    def one_head(head_index):
        picked = lax.dynamic_index_in_dim(projected, head_index, axis=3, keepdims=False)
        queries = picked[:, :, 0].astype(jnp.float32)
        keys_all = picked[:, :, 1].astype(jnp.float32)
        values_all = picked[:, :, 2].astype(jnp.float32)
        space_scores = jnp.einsum("fpe,fqe->fpq", queries, keys_all) * scale_factor
        space_probs = softmax_rows(space_scores).astype(jnp.float32)
        spatial = jnp.einsum("fpq,fqe->fpe", space_probs, values_all).astype(jnp.bfloat16)
        time_scores = jnp.einsum("fpe,gpe->pfg", queries, keys_all) * scale_factor
        time_probs = softmax_rows(time_scores).astype(jnp.float32)
        temporal = jnp.einsum("pfg,gpe->fpe", time_probs, values_all).astype(jnp.bfloat16)
        return jnp.where(head_kind[head_index] == 1, temporal, spatial)

    heads_out = lax.map(one_head, jnp.arange(HEADS, dtype=jnp.int32))
    chosen = heads_out.transpose(1, 2, 0, 3).reshape(FRAMES * POSITIONS, N_BAND, HEAD_DEV * HEAD)
    grouped = out_weight.reshape(N_BAND, HEAD_DEV * HEAD, D)

    def add_group(running, group_index):
        columns = lax.dynamic_index_in_dim(chosen, group_index, axis=1, keepdims=False)
        rows_w = lax.dynamic_index_in_dim(grouped, group_index, axis=0, keepdims=False)
        partial_sum = jnp.dot(columns, rows_w, preferred_element_type=jnp.float32).astype(jnp.bfloat16)
        partial_sum = lax.optimization_barrier(partial_sum)
        return running + partial_sum.astype(jnp.float32), None

    running, unused = lax.scan(add_group, jnp.zeros((FRAMES * POSITIONS, D), jnp.float32), jnp.arange(N_BAND, dtype=jnp.int32))
    return running.astype(jnp.bfloat16)
```

```python
import jax
import jax.numpy as jnp
from jax import lax
from jax.experimental import pallas as pl
from jax.experimental.pallas import tpu as pltpu
from jax.sharding import PartitionSpec as P

MESH = pl.DeviceIdType.MESH
NX = 4
NY = 8
NZ = 8
PAIRS = NZ // 2
BANDS = 2 * NX
PEERS = NY * PAIRS
HEAD = 128
POSITIONS = 128
ROWS = 2 * POSITIONS
SHARE = POSITIONS // PEERS
DEPTH = 48
WIDTH = 384


def remote(src, dst, send_sem, recv_sem, device):
    return pltpu.make_async_remote_copy(
        src_ref=src,
        dst_ref=dst,
        send_sem=send_sem,
        recv_sem=recv_sem,
        device_id=device,
        device_id_type=MESH,
    )


def await_bytes(ref, sem):
    pltpu.make_async_copy(ref, ref, sem).wait()


def attend(queries, keys, values, bias):
    scores = lax.dot_general(
        queries, keys, (((1,), (1,)), ((), ())), preferred_element_type=jnp.float32
    ) * (HEAD**-0.5)
    if bias is not None:
        scores = scores + bias
    raised = jnp.exp(scores - jnp.max(scores, axis=-1, keepdims=True))
    probs = (raised / jnp.sum(raised, axis=-1, keepdims=True)).astype(jnp.bfloat16)
    return jnp.dot(probs, values, preferred_element_type=jnp.float32)


def wrap(value, size):
    return lax.rem(value + 8 * size, size)


def hops(size):
    return (size // 2, (size - 1) // 2)


def wander(place):
    if isinstance(place, int):
        return (place + 1) // 2 * (2 * (place % 2) - 1)
    return lax.div(place + 1, 2) * (2 * lax.rem(place, 2) - 1)


class Grid:
    def __init__(self, block, device, here, sizes, sign, sems):
        self.block = block
        self.device = device
        self.first, self.second = here
        self.n_first, self.n_second = sizes
        self.sign = sign
        self.send, self.recv1, self.recv2 = sems

    def turn(self, way):
        return self.sign if way == 0 else -self.sign

    def to_second(self, block, way, step, place):
        there = wrap(self.second + self.turn(way), self.n_second)
        remote(
            block,
            block,
            self.send.at[1, way],
            self.recv2.at[way, step, place],
            self.device(self.first, there),
        ).start()

    def begin(self, part):
        own = part(self.first, self.second)
        for way in range(2):
            if hops(self.n_second)[way]:
                self.to_second(own, way, 0, 0)

        for place in range(1, self.n_first // 2 + 1):
            self.to_first(own, place, self.sign * wander(place))

    def to_first(self, block, place, by):
        there = wrap(self.first + by, self.n_first)
        remote(
            block,
            block,
            self.send.at[0, 0],
            self.recv1.at[place],
            self.device(there, self.second),
        ).start()

    def along_first(self, place):
        block = self.block(
            wrap(self.first - self.sign * wander(place), self.n_first), self.second
        )
        await_bytes(block, self.recv1.at[place])
        half = self.n_first // 4
        if isinstance(place, int) and place == 2 * half - 1:
            self.to_first(block, self.n_first - 1, self.sign * half)
            if half > 1:
                self.to_first(block, self.n_first - 3, self.sign)
        if isinstance(place, int) and place == 2 * half and half > 1:
            self.to_first(block, self.n_first - 2, -self.sign)
        for way in range(2):
            if hops(self.n_second)[way]:
                self.to_second(block, way, 0, place)

    def along_second(self, step, place):
        for way in range(2):
            count = hops(self.n_second)[way]
            if step > count:
                continue
            block = self.block(
                wrap(self.first - self.sign * wander(place), self.n_first),
                wrap(self.second - self.turn(way) * step, self.n_second),
            )
            await_bytes(block, self.recv2.at[way, step - 1, place])
            if step < count:
                self.to_second(block, way, step, place)


def kernel(
    tokens,
    qkv,
    out_weight,
    kind_hbm,
    out,
    wbuf,
    obuf,
    tbuf,
    msg,
    fin,
    rmsg,
    rfin,
    cbuf,
    mbuf,
    sbuf,
    qkv_sum,
    total,
    by_peer,
    by_frame,
    bias,
    kind,
    own_sem,
    z_send,
    z_recv,
    w_send,
    w_recv1,
    w_recv2,
    o_send,
    o_recv1,
    o_recv2,
    t_send,
    t_recv,
    s_send,
    s_recv,
    a_send,
    a_recv,
    m_send,
    m_recv,
    n_send,
    n_recv,
    f_send,
    f_recv,
):
    frame = lax.axis_index("frame")
    band = lax.axis_index("band")
    y, z = lax.div(frame, NZ), lax.rem(frame, NZ)
    x, core = lax.div(band, 2), lax.rem(band, 2)
    across = z + (y - z) * core
    along = y + (z - y) * core
    pair, odd = lax.div(across, 2), lax.rem(across, 2)
    other = 1 - odd
    sign = 1 - 2 * core
    sibling_band = 2 * x + 1 - core
    sibling = (frame, sibling_band)
    sibling_odd = lax.rem(y + (z - y) * core, 2)
    me = along * PAIRS + pair

    def frame_at(along_there, across_there):
        return along_there * (NZ - (NZ - 1) * core) + across_there * (1 + (NZ - 1) * core)

    beside = frame_at(along, 2 * pair + other)

    def band_at(step):
        return 2 * wrap(x + step, NX) + core

    def peer(index):
        return (frame_at(lax.div(index, PAIRS), 2 * lax.rem(index, PAIRS) + odd), band)

    barrier = pltpu.get_barrier_semaphore()

    def greet(device):
        pl.semaphore_signal(barrier, inc=1, device_id=device, device_id_type=MESH)

    greet(sibling)
    greet((beside, sibling_band))
    for step in (1, -1):
        greet((y * NZ + wrap(z + step, NZ), band))
        greet((wrap(y + step, NY) * NZ + z, band))
        greet((frame_at(along, 2 * wrap(pair + step, PAIRS) + odd), band))
    for step in range(1, NX):
        greet((frame, band_at(step)))

    def head_columns(which):
        return qkv.at[:, :, pl.ds(pl.multiple_of(which * HEAD, HEAD), HEAD)]

    own = [
        pltpu.make_async_copy(head_columns(odd), wbuf.at[:, along, pair, odd], own_sem.at[0]),
        pltpu.make_async_copy(out_weight.at[0:16], obuf.at[0, y, z], own_sem.at[1]),
        pltpu.make_async_copy(out_weight.at[16:32], obuf.at[1, z, y], own_sem.at[2]),
        pltpu.make_async_copy(tokens, tbuf.at[odd, band], own_sem.at[3]),
        pltpu.make_async_copy(kind_hbm, kind, own_sem.at[4]),
    ]
    for copy in own:
        copy.start()
    pl.semaphore_wait(barrier, 8 + NX - 1)

    remote(
        head_columns(other), wbuf.at[:, along, pair, odd], z_send.at[0], z_recv.at[0], (beside, band)
    ).start()
    beside_z = y * NZ + z + 1 - 2 * lax.rem(z, 2)
    beside_y = (y + 1 - 2 * lax.rem(y, 2)) * NZ + z
    remote(
        tokens, tbuf.at[lax.rem(z, 2), band], z_send.at[1], z_recv.at[1 + core], (beside_z, 2 * x)
    ).start()
    remote(
        tokens, tbuf.at[lax.rem(y, 2), band], z_send.at[2], z_recv.at[1 + core], (beside_y, 2 * x + 1)
    ).start()

    grid = Grid(
        lambda first, second: wbuf.at[:, second, first],
        lambda first, second: (frame_at(second, 2 * first + odd), band),
        (pair, along),
        (PAIRS, NY),
        sign,
        (w_send, w_recv1, w_recv2),
    )

    def begin(which):
        grid.begin(lambda first, second: wbuf.at[:, second, first, which])

    def token_along_x(which, block):
        for step in (1, NX - 1, 2):
            remote(
                block, block, t_send.at[which, step], t_recv.at[which, step], (frame, band_at(step))
            ).start()

    for copy in own:
        copy.wait()
    begin(odd)
    token_along_x(0, tbuf.at[odd, band])
    remote(
        tbuf.at[odd, band], tbuf.at[sibling_odd, band], s_send.at[0], s_recv.at[0], sibling
    ).start()

    tall = lax.broadcasted_iota(jnp.int32, (ROWS, ROWS), 0)
    wide = lax.broadcasted_iota(jnp.int32, (ROWS, ROWS), 1)

    def origin(row):
        return (
            lax.rem(lax.div(row, SHARE), 2) * POSITIONS
            + lax.div(row, 2 * SHARE) * SHARE
            + lax.rem(row, SHARE)
        )

    qkv_sum[...] = jnp.zeros_like(qkv_sum)
    by_peer[...] = jnp.where(wide == origin(tall), 1.0, 0.0).astype(jnp.bfloat16)
    by_frame[...] = jnp.where(tall == origin(wide), 1.0, 0.0).astype(jnp.bfloat16)
    bias[...] = jnp.where(lax.rem(tall, SHARE) == lax.rem(wide, SHARE), 0.0, -1e30)

    await_bytes(wbuf.at[:, along, pair, other], z_recv.at[0])
    begin(other)
    for which in range(2):
        await_bytes(tbuf.at[other, 2 * x + which], z_recv.at[1 + which])
        token_along_x(1 + which, tbuf.at[other, 2 * x + which])

    def out_block(half, first, second):
        return obuf.at[half, second, first]

    def out_here(half):
        return (z, y) if half == 0 else (y, z)

    def out_device(half, first, second):
        return (second * NZ + first if half == 0 else first * NZ + second, band)

    def turn(way):
        return sign if way == 0 else -sign

    def out_send1(half, way, step, block):
        first, second = out_here(half)
        there = wrap(first + turn(way), NY)
        remote(
            block,
            block,
            o_send.at[half, 0, way],
            o_recv1.at[half, way, step],
            out_device(half, there, second),
        ).start()

    def out_send2(half, way, step, chunk):
        first, second = out_here(half)
        there = wrap(second + turn(way), NY)
        remote(
            chunk,
            chunk,
            o_send.at[half, 1, way],
            o_recv2.at[half, way, step],
            out_device(half, first, there),
        ).start()

    def out_along_first(step):
        for half in range(2):
            first, second = out_here(half)
            for way in range(2):
                if step > hops(NY)[way]:
                    continue
                block = obuf.at[half, second, wrap(first - turn(way) * step, NY)]
                if step:
                    await_bytes(block, o_recv1.at[half, way, step - 1])
                if step < hops(NY)[way]:
                    out_send1(half, way, step, block)

    def out_along_second(step):
        for half in range(2):
            first, second = out_here(half)
            for way in range(2):
                if step > hops(NY)[way]:
                    continue
                chunk = obuf.at[half, wrap(second - turn(way) * step, NY)]
                if step:
                    await_bytes(chunk, o_recv2.at[half, way, step - 1])
                if step < hops(NY)[way]:
                    out_send2(half, way, step, chunk)

    out_along_first(0)
    for place in range(1, PAIRS):
        grid.along_first(place)

    def ring_step(step):
        def one(place, carry):
            grid.along_second(step, place)
            return carry

        lax.fori_loop(0, PAIRS, one, 0)

    ring_step(1)
    out_along_first(1)
    for hop in (1, NX - 1, 2):
        from_band = band_at(-hop)
        await_bytes(tbuf.at[odd, from_band], t_recv.at[0, hop])
        remote(
            tbuf.at[odd, from_band],
            tbuf.at[sibling_odd, from_band],
            s_send.at[hop],
            s_recv.at[hop],
            sibling,
        ).start()
    ring_step(2)
    out_along_first(2)
    ring_step(3)
    out_along_first(3)
    out_along_first(4)
    out_along_second(0)
    for hop in range(NX):
        from_band = 2 * wrap(x - hop, NX) + 1 - core
        await_bytes(tbuf.at[odd, from_band], s_recv.at[hop])
        if hop:
            for which in range(2):
                await_bytes(
                    tbuf.at[other, 2 * wrap(x - hop, NX) + which], t_recv.at[1 + which, hop]
                )
    ring_step(4)

    chunk = 2 * NZ * DEPTH

    def project(step, right):
        at = pl.ds(pl.multiple_of(step * chunk, HEAD), chunk)
        qkv_sum[...] += jnp.dot(
            tbuf[:, :, :, at].reshape(ROWS, chunk),
            jnp.concatenate([right(slot) for slot in range(3)], axis=1),
            preferred_element_type=jnp.float32,
        )

    @pl.when(core == 0)
    def _():
        def one(step, carry):
            project(step, lambda slot: wbuf[slot, pl.ds(2 * step, 2)].reshape(chunk, HEAD))
            return carry

        lax.fori_loop(0, NY // 2, one, 0)

    @pl.when(core == 1)
    def _():
        def one(step, carry):
            project(
                step,
                lambda slot: jnp.concatenate(
                    [
                        wbuf[slot, :, step, parity].reshape(chunk // 2, HEAD)
                        for parity in range(2)
                    ],
                    axis=0,
                ),
            )
            return carry

        lax.fori_loop(0, NY // 2, one, 0)

    rounded = qkv_sum[...].astype(jnp.bfloat16)

    msg[...] = (
        jnp.dot(by_peer[...], rounded, preferred_element_type=jnp.float32)
        .reshape(msg.shape)
        .astype(jnp.bfloat16)
    )

    def exchange(stage, source, target):
        def send(step, carry):
            there = lax.rem(me + step, PEERS)
            remote(
                source.at[there], target.at[me], a_send.at[stage], a_recv.at[stage], peer(there)
            ).start()
            return carry

        pltpu.make_async_copy(source.at[me], target.at[me], a_recv.at[stage]).start()
        lax.fori_loop(1, PEERS, send, 0)

    exchange(0, msg, fin)
    out_along_second(1)
    spatial = jnp.concatenate(
        [
            attend(
                rounded[at : at + POSITIONS, :HEAD],
                rounded[at : at + POSITIONS, HEAD : 2 * HEAD],
                rounded[at : at + POSITIONS, 2 * HEAD :],
                None,
            )
            for at in (0, POSITIONS)
        ],
        axis=0,
    ).astype(jnp.bfloat16)
    await_bytes(wbuf.at[:, 0, 0, 0], z_send.at[0])
    await_bytes(tbuf.at[0, 0], z_send.at[1])
    await_bytes(tbuf.at[0, 0], z_send.at[2])
    await_bytes(wbuf.at[:, 0, 0 : PAIRS - 1], w_send.at[0, 0])
    for way in range(2):
        await_bytes(wbuf.at[:, 0 : hops(NY)[way]], w_send.at[1, way])
        for half in range(2):
            await_bytes(obuf.at[half, 0, 0 : hops(NY)[way]], o_send.at[half, 0, way])
    for hop in range(NX):
        await_bytes(tbuf.at[0, 0], s_send.at[hop])
        if hop:
            for which in range(3):
                await_bytes(tbuf.at[0, 0], t_send.at[which, hop])
    await_bytes(fin, a_recv.at[0])
    out_along_second(2)
    laid = fin[...].reshape(ROWS, 3 * HEAD)
    mixed = attend(laid[:, :HEAD], laid[:, HEAD : 2 * HEAD], laid[:, 2 * HEAD :], bias[...])
    rmsg[...] = mixed.reshape(rmsg.shape).astype(jnp.bfloat16)
    exchange(1, rmsg, rfin)
    await_bytes(msg.at[0 : PEERS - 1], a_send.at[0])
    await_bytes(rfin, a_recv.at[1])
    out_along_second(3)
    back = jnp.dot(
        by_frame[...], rfin[...].reshape(ROWS, HEAD), preferred_element_type=jnp.float32
    ).astype(jnp.bfloat16)
    temporal = jnp.full((ROWS, HEAD), kind[odd], jnp.int32) == 1
    cbuf[...] = jnp.where(temporal, back, spatial).reshape(cbuf.shape)

    for step in (1, NX - 1, 2):
        remote(
            cbuf.at[odd],
            mbuf.at[band, odd],
            m_send.at[0, step],
            m_recv.at[0, step],
            (frame, band_at(step)),
        ).start()
    for step in (1, NX - 1, 2, 0):
        remote(
            cbuf.at[other],
            mbuf.at[band, odd],
            m_send.at[1, step],
            m_recv.at[1, step],
            (beside, band_at(step)),
        ).start()
    remote(
        cbuf.at[odd], mbuf.at[band, odd], n_send.at[0, 0], n_recv.at[0, 0], sibling
    ).start()
    last = pltpu.make_async_copy(cbuf.at[odd], mbuf.at[band, odd], m_recv.at[0, 0])
    last.start()
    for which, hop in ((1, 0), (0, 1), (0, 3), (1, 1), (1, 3), (0, 2), (1, 2)):
        block = mbuf.at[band_at(-hop), odd if which == 0 else other]
        await_bytes(block, m_recv.at[which, hop])
        remote(block, block, n_send.at[which, hop], n_recv.at[which, hop], sibling).start()
    out_along_second(4)
    last.wait()

    def project_out(source):
        left = jnp.concatenate([mbuf[source, 0], mbuf[source, 1]], axis=1)
        right = jnp.stack([obuf[0, source], obuf[1, :, source]], axis=1).reshape(
            2 * HEAD, WIDTH
        )
        return jnp.dot(left, right, preferred_element_type=jnp.float32)

    def own_core(hop, carry):
        total[...] += project_out(band_at(-hop))
        return carry

    def other_core(hop, carry):
        source = 2 * wrap(x - hop, NX) + 1 - core
        for which in range(2):
            await_bytes(
                mbuf.at[source, sibling_odd if which == 0 else 1 - sibling_odd],
                n_recv.at[which, hop],
            )
        total[...] += project_out(source)
        return carry

    total[...] = jnp.zeros_like(total)
    lax.fori_loop(0, NX, own_core, 0)
    lax.fori_loop(0, NX, other_core, 0)
    sbuf[...] = total[...].astype(jnp.bfloat16).reshape(sbuf.shape)

    def columns(which):
        return out.at[:, pl.ds(pl.multiple_of(which * WIDTH, HEAD), WIDTH)]

    for step in range(1, BANDS):
        there = wrap(band + step, BANDS)
        remote(
            sbuf.at[there], columns(band), f_send.at[step], f_recv.at[step], (frame, there)
        ).start()
    last = pltpu.make_async_copy(sbuf.at[band], columns(band), f_send.at[0])
    last.start()
    for step in range(1, BANDS):
        await_bytes(columns(wrap(band - step, BANDS)), f_recv.at[step])
    last.wait()

    await_bytes(rmsg.at[0 : PEERS - 1], a_send.at[1])
    for which in range(2):
        for hop in range(NX):
            if hop or which:
                await_bytes(cbuf.at[0], m_send.at[which, hop])
            await_bytes(cbuf.at[0], n_send.at[which, hop])
    for half in range(2):
        for way in range(2):
            await_bytes(obuf.at[half, 0 : hops(NY)[way]], o_send.at[half, 1, way])
    for step in range(1, BANDS):
        await_bytes(sbuf.at[0], f_send.at[step])


def body(tokens, qkv_weight, out_weight, head_kind):
    bf16 = jnp.bfloat16
    dma = pltpu.SemaphoreType.DMA
    hbm = pl.BlockSpec(memory_space=pltpu.HBM)
    return pl.pallas_call(
        kernel,
        out_shape=jax.ShapeDtypeStruct(tokens.shape, tokens.dtype),
        in_specs=[hbm] * 4,
        out_specs=hbm,
        scratch_shapes=[
            pltpu.VMEM((3, NY, PAIRS, 2, DEPTH, HEAD), bf16),
            pltpu.VMEM((2, 8, 8, 16, WIDTH), bf16),
            pltpu.VMEM((2, BANDS) + tokens.shape, bf16),
            pltpu.VMEM((PEERS, 2 * SHARE, 3 * HEAD), bf16),
            pltpu.VMEM((PEERS, 2 * SHARE, 3 * HEAD), bf16),
            pltpu.VMEM((PEERS, 2 * SHARE, HEAD), bf16),
            pltpu.VMEM((PEERS, 2 * SHARE, HEAD), bf16),
            pltpu.VMEM((2, POSITIONS, HEAD), bf16),
            pltpu.VMEM((BANDS, 2, POSITIONS, HEAD), bf16),
            pltpu.VMEM((BANDS, 16, WIDTH), bf16),
            pltpu.VMEM((ROWS, 3 * HEAD), jnp.float32),
            pltpu.VMEM((POSITIONS, WIDTH), jnp.float32),
            pltpu.VMEM((ROWS, ROWS), bf16),
            pltpu.VMEM((ROWS, ROWS), bf16),
            pltpu.VMEM((ROWS, ROWS), jnp.float32),
            pltpu.SMEM((2,), jnp.int32),
            dma((5,)),
            dma((3,)),
            dma((3,)),
            dma((2, 2)),
            dma((4,)),
            dma((2, 4, 4)),
            dma((2, 2, 2)),
            dma((2, 2, 4)),
            dma((2, 2, 4)),
            dma((3, NX)),
            dma((3, NX)),
            dma((NX,)),
            dma((NX,)),
            dma((2,)),
            dma((2,)),
            dma((2, NX)),
            dma((2, NX)),
            dma((2, NX)),
            dma((2, NX)),
            dma((BANDS,)),
            dma((BANDS,)),
        ],
        compiler_params=pltpu.CompilerParams(
            collective_id=0, has_side_effects=True, vmem_limit_bytes=64 * 1024 * 1024
        ),
    )(tokens, qkv_weight.transpose(1, 0, 2), out_weight, head_kind)


def solution(mesh):
    return jax.shard_map(
        body,
        mesh=mesh,
        in_specs=(
            P(("frame", "band"), None),
            P("frame", None, "band"),
            P("frame", "band"),
            P("band"),
        ),
        out_specs=P(("frame", "band"), None),
        check_vma=False,
    )
```

```python
import jax
import jax.numpy as jnp
from jax import lax
from jax.experimental import pallas as pl
from jax.experimental.pallas import tpu as pltpu
from jax.sharding import PartitionSpec as P

MESH = pl.DeviceIdType.MESH
NX = 4
NY = 8
NZ = 8
PAIRS = NZ // 2
BANDS = 2 * NX
PEERS = NY * PAIRS
HEAD = 128
POSITIONS = 128
ROWS = 2 * POSITIONS
SHARE = POSITIONS // PEERS
DEPTH = 48
WIDTH = 384


def remote(src, dst, send_sem, recv_sem, device):
    return pltpu.make_async_remote_copy(
        src_ref=src,
        dst_ref=dst,
        send_sem=send_sem,
        recv_sem=recv_sem,
        device_id=device,
        device_id_type=MESH,
    )


def await_bytes(ref, sem):
    pltpu.make_async_copy(ref, ref, sem).wait()


def attend(queries, keys, values, bias):
    scores = lax.dot_general(
        queries, keys, (((1,), (1,)), ((), ())), preferred_element_type=jnp.float32
    ) * (HEAD**-0.5)
    if bias is not None:
        scores = scores + bias
    raised = jnp.exp(scores - jnp.max(scores, axis=-1, keepdims=True))
    probs = (raised / jnp.sum(raised, axis=-1, keepdims=True)).astype(jnp.bfloat16)
    return jnp.dot(probs, values, preferred_element_type=jnp.float32)


def wrap(value, size):
    return lax.rem(value + 8 * size, size)


def hops(size):
    return (size // 2, (size - 1) // 2)


def wander(place):
    if isinstance(place, int):
        return (place + 1) // 2 * (2 * (place % 2) - 1)
    return lax.div(place + 1, 2) * (2 * lax.rem(place, 2) - 1)


class Grid:
    def __init__(self, block, device, here, sizes, sign, sems):
        self.block = block
        self.device = device
        self.first, self.second = here
        self.n_first, self.n_second = sizes
        self.sign = sign
        self.send, self.recv1, self.recv2 = sems

    def turn(self, way):
        return self.sign if way == 0 else -self.sign

    def to_second(self, block, way, step, place):
        there = wrap(self.second + self.turn(way), self.n_second)
        remote(
            block,
            block,
            self.send.at[1, way],
            self.recv2.at[way, step, place],
            self.device(self.first, there),
        ).start()

    def begin(self, part):
        own = part(self.first, self.second)
        for way in range(2):
            if hops(self.n_second)[way]:
                self.to_second(own, way, 0, 0)

        for place in range(1, self.n_first // 2 + 1):
            self.to_first(own, place, self.sign * wander(place))

    def to_first(self, block, place, by):
        there = wrap(self.first + by, self.n_first)
        remote(
            block,
            block,
            self.send.at[0, 0],
            self.recv1.at[place],
            self.device(there, self.second),
        ).start()

    def along_first(self, place):
        block = self.block(
            wrap(self.first - self.sign * wander(place), self.n_first), self.second
        )
        await_bytes(block, self.recv1.at[place])
        half = self.n_first // 4
        if isinstance(place, int) and place == 2 * half - 1:
            self.to_first(block, self.n_first - 1, self.sign * half)
            if half > 1:
                self.to_first(block, self.n_first - 3, self.sign)
        if isinstance(place, int) and place == 2 * half and half > 1:
            self.to_first(block, self.n_first - 2, -self.sign)
        for way in range(2):
            if hops(self.n_second)[way]:
                self.to_second(block, way, 0, place)

    def along_second(self, step, place):
        for way in range(2):
            count = hops(self.n_second)[way]
            if step > count:
                continue
            block = self.block(
                wrap(self.first - self.sign * wander(place), self.n_first),
                wrap(self.second - self.turn(way) * step, self.n_second),
            )
            await_bytes(block, self.recv2.at[way, step - 1, place])
            if step < count:
                self.to_second(block, way, step, place)


def kernel(
    tokens,
    qkv,
    out_weight,
    kind_hbm,
    out,
    wbuf,
    obuf,
    tbuf,
    msg,
    fin,
    rmsg,
    rfin,
    cbuf,
    mbuf,
    sbuf,
    qkv_sum,
    total,
    by_peer,
    by_frame,
    bias,
    kind,
    own_sem,
    z_send,
    z_recv,
    w_send,
    w_recv1,
    w_recv2,
    o_send,
    o_recv1,
    o_recv2,
    t_send,
    t_recv,
    s_send,
    s_recv,
    a_send,
    a_recv,
    m_send,
    m_recv,
    n_send,
    n_recv,
    f_send,
    f_recv,
):
    frame = lax.axis_index("frame")
    band = lax.axis_index("band")
    y, z = lax.div(frame, NZ), lax.rem(frame, NZ)
    x, core = lax.div(band, 2), lax.rem(band, 2)
    across = z + (y - z) * core
    along = y + (z - y) * core
    pair, odd = lax.div(across, 2), lax.rem(across, 2)
    other = 1 - odd
    sign = 1 - 2 * core
    sibling_band = 2 * x + 1 - core
    sibling = (frame, sibling_band)
    sibling_odd = lax.rem(y + (z - y) * core, 2)
    me = along * PAIRS + pair

    def frame_at(along_there, across_there):
        return along_there * (NZ - (NZ - 1) * core) + across_there * (1 + (NZ - 1) * core)

    beside = frame_at(along, 2 * pair + other)

    def band_at(step):
        return 2 * wrap(x + step, NX) + core

    def peer(index):
        return (frame_at(lax.div(index, PAIRS), 2 * lax.rem(index, PAIRS) + odd), band)

    barrier = pltpu.get_barrier_semaphore()

    def greet(device):
        pl.semaphore_signal(barrier, inc=1, device_id=device, device_id_type=MESH)

    greet(sibling)
    greet((beside, sibling_band))
    for step in (1, -1):
        greet((y * NZ + wrap(z + step, NZ), band))
        greet((wrap(y + step, NY) * NZ + z, band))
        greet((frame_at(along, 2 * wrap(pair + step, PAIRS) + odd), band))
    for step in range(1, NX):
        greet((frame, band_at(step)))

    def head_columns(which):
        return qkv.at[:, :, pl.ds(pl.multiple_of(which * HEAD, HEAD), HEAD)]

    own = [
        pltpu.make_async_copy(head_columns(odd), wbuf.at[:, along, pair, odd], own_sem.at[0]),
        pltpu.make_async_copy(out_weight.at[0:16], obuf.at[0, y, z], own_sem.at[1]),
        pltpu.make_async_copy(out_weight.at[16:32], obuf.at[1, z, y], own_sem.at[2]),
        pltpu.make_async_copy(tokens, tbuf.at[odd, band], own_sem.at[3]),
        pltpu.make_async_copy(kind_hbm, kind, own_sem.at[4]),
    ]
    for copy in own:
        copy.start()
    pl.semaphore_wait(barrier, 8 + NX - 1)

    remote(
        head_columns(other), wbuf.at[:, along, pair, odd], z_send.at[0], z_recv.at[0], (beside, band)
    ).start()
    beside_z = y * NZ + z + 1 - 2 * lax.rem(z, 2)
    beside_y = (y + 1 - 2 * lax.rem(y, 2)) * NZ + z
    remote(
        tokens, tbuf.at[lax.rem(z, 2), band], z_send.at[1], z_recv.at[1 + core], (beside_z, 2 * x)
    ).start()
    remote(
        tokens, tbuf.at[lax.rem(y, 2), band], z_send.at[2], z_recv.at[1 + core], (beside_y, 2 * x + 1)
    ).start()

    grid = Grid(
        lambda first, second: wbuf.at[:, second, first],
        lambda first, second: (frame_at(second, 2 * first + odd), band),
        (pair, along),
        (PAIRS, NY),
        sign,
        (w_send, w_recv1, w_recv2),
    )

    def begin(which):
        grid.begin(lambda first, second: wbuf.at[:, second, first, which])

    def token_along_x(which, block):
        for step in (1, NX - 1):
            remote(
                block, block, t_send.at[which, step], t_recv.at[which, step], (frame, band_at(step))
            ).start()

    def token_passed_on(which, by):
        if which == 0:
            block = tbuf.at[odd, band_at(-by)]
        else:
            block = tbuf.at[other, 2 * wrap(x - by, NX) + which - 1]
        remote(
            block, block, t_send.at[which, 2], t_recv.at[which, 2], (frame, band_at(by))
        ).start()

    def token_to_sibling(hop):
        from_band = band_at(-hop)
        remote(
            tbuf.at[odd, from_band],
            tbuf.at[sibling_odd, from_band],
            s_send.at[hop],
            s_recv.at[hop],
            sibling,
        ).start()

    for copy in own:
        copy.wait()
    begin(odd)
    token_along_x(0, tbuf.at[odd, band])
    remote(
        tbuf.at[odd, band], tbuf.at[sibling_odd, band], s_send.at[0], s_recv.at[0], sibling
    ).start()

    tall = lax.broadcasted_iota(jnp.int32, (ROWS, ROWS), 0)
    wide = lax.broadcasted_iota(jnp.int32, (ROWS, ROWS), 1)

    def origin(row):
        return (
            lax.rem(lax.div(row, SHARE), 2) * POSITIONS
            + lax.div(row, 2 * SHARE) * SHARE
            + lax.rem(row, SHARE)
        )

    qkv_sum[...] = jnp.zeros_like(qkv_sum)
    by_peer[...] = jnp.where(wide == origin(tall), 1.0, 0.0).astype(jnp.bfloat16)
    by_frame[...] = jnp.where(tall == origin(wide), 1.0, 0.0).astype(jnp.bfloat16)
    bias[...] = jnp.where(lax.rem(tall, SHARE) == lax.rem(wide, SHARE), 0.0, -1e30)

    await_bytes(wbuf.at[:, along, pair, other], z_recv.at[0])
    begin(other)
    for which in range(2):
        await_bytes(tbuf.at[other, 2 * x + which], z_recv.at[1 + which])
        token_along_x(1 + which, tbuf.at[other, 2 * x + which])

    def out_block(half, first, second):
        return obuf.at[half, second, first]

    def out_here(half):
        return (z, y) if half == 0 else (y, z)

    def out_device(half, first, second):
        return (second * NZ + first if half == 0 else first * NZ + second, band)

    def turn(way):
        return sign if way == 0 else -sign

    def out_send1(half, way, step, block):
        first, second = out_here(half)
        there = wrap(first + turn(way), NY)
        remote(
            block,
            block,
            o_send.at[half, 0, way],
            o_recv1.at[half, way, step],
            out_device(half, there, second),
        ).start()

    def out_send2(half, way, step, chunk):
        first, second = out_here(half)
        there = wrap(second + turn(way), NY)
        remote(
            chunk,
            chunk,
            o_send.at[half, 1, way],
            o_recv2.at[half, way, step],
            out_device(half, first, there),
        ).start()

    def out_along_first(step):
        for half in range(2):
            first, second = out_here(half)
            for way in range(2):
                if step > hops(NY)[way]:
                    continue
                block = obuf.at[half, second, wrap(first - turn(way) * step, NY)]
                if step:
                    await_bytes(block, o_recv1.at[half, way, step - 1])
                if step < hops(NY)[way]:
                    out_send1(half, way, step, block)

    def out_along_second(step):
        for half in range(2):
            first, second = out_here(half)
            for way in range(2):
                if step > hops(NY)[way]:
                    continue
                chunk = obuf.at[half, wrap(second - turn(way) * step, NY)]
                if step:
                    await_bytes(chunk, o_recv2.at[half, way, step - 1])
                if step < hops(NY)[way]:
                    out_send2(half, way, step, chunk)

    out_along_first(0)
    for place in range(1, PAIRS):
        grid.along_first(place)

    def ring_step(step):
        def one(place, carry):
            grid.along_second(step, place)
            return carry

        lax.fori_loop(0, PAIRS, one, 0)

    for hop in (1, NX - 1):
        await_bytes(tbuf.at[odd, band_at(-hop)], t_recv.at[0, hop])
    token_passed_on(0, sign)
    token_to_sibling(1)
    token_to_sibling(NX - 1)
    ring_step(1)
    out_along_first(1)
    for which, by in ((1, 1), (2, -1)):
        for hop in (1, NX - 1):
            await_bytes(
                tbuf.at[other, 2 * wrap(x - hop, NX) + which - 1], t_recv.at[which, hop]
            )
        token_passed_on(which, by)
    ring_step(2)
    await_bytes(tbuf.at[odd, band_at(2)], t_recv.at[0, 2])
    token_to_sibling(2)
    out_along_first(2)
    ring_step(3)
    out_along_first(3)
    out_along_first(4)
    out_along_second(0)
    for hop in range(NX):
        from_band = 2 * wrap(x - hop, NX) + 1 - core
        await_bytes(tbuf.at[odd, from_band], s_recv.at[hop])
        if hop == 2:
            for which in range(2):
                await_bytes(
                    tbuf.at[other, 2 * wrap(x - hop, NX) + which], t_recv.at[1 + which, hop]
                )
    ring_step(4)

    chunk = 2 * NZ * DEPTH

    def project(step, right):
        at = pl.ds(pl.multiple_of(step * chunk, HEAD), chunk)
        qkv_sum[...] += jnp.dot(
            tbuf[:, :, :, at].reshape(ROWS, chunk),
            jnp.concatenate([right(slot) for slot in range(3)], axis=1),
            preferred_element_type=jnp.float32,
        )

    @pl.when(core == 0)
    def _():
        def one(step, carry):
            project(step, lambda slot: wbuf[slot, pl.ds(2 * step, 2)].reshape(chunk, HEAD))
            return carry

        lax.fori_loop(0, NY // 2, one, 0)

    @pl.when(core == 1)
    def _():
        def one(step, carry):
            project(
                step,
                lambda slot: jnp.concatenate(
                    [
                        wbuf[slot, :, step, parity].reshape(chunk // 2, HEAD)
                        for parity in range(2)
                    ],
                    axis=0,
                ),
            )
            return carry

        lax.fori_loop(0, NY // 2, one, 0)

    rounded = qkv_sum[...].astype(jnp.bfloat16)

    msg[...] = (
        jnp.dot(by_peer[...], rounded, preferred_element_type=jnp.float32)
        .reshape(msg.shape)
        .astype(jnp.bfloat16)
    )

    def exchange(stage, source, target):
        def send(step, carry):
            there = lax.rem(me + step, PEERS)
            remote(
                source.at[there], target.at[me], a_send.at[stage], a_recv.at[stage], peer(there)
            ).start()
            return carry

        pltpu.make_async_copy(source.at[me], target.at[me], a_recv.at[stage]).start()
        lax.fori_loop(1, PEERS, send, 0)

    exchange(0, msg, fin)
    out_along_second(1)
    spatial = jnp.concatenate(
        [
            attend(
                rounded[at : at + POSITIONS, :HEAD],
                rounded[at : at + POSITIONS, HEAD : 2 * HEAD],
                rounded[at : at + POSITIONS, 2 * HEAD :],
                None,
            )
            for at in (0, POSITIONS)
        ],
        axis=0,
    ).astype(jnp.bfloat16)
    await_bytes(wbuf.at[:, 0, 0, 0], z_send.at[0])
    await_bytes(tbuf.at[0, 0], z_send.at[1])
    await_bytes(tbuf.at[0, 0], z_send.at[2])
    await_bytes(wbuf.at[:, 0, 0 : PAIRS - 1], w_send.at[0, 0])
    for way in range(2):
        await_bytes(wbuf.at[:, 0 : hops(NY)[way]], w_send.at[1, way])
        for half in range(2):
            await_bytes(obuf.at[half, 0, 0 : hops(NY)[way]], o_send.at[half, 0, way])
    for hop in range(NX):
        await_bytes(tbuf.at[0, 0], s_send.at[hop])
        if hop:
            for which in range(3):
                await_bytes(tbuf.at[0, 0], t_send.at[which, hop])
    await_bytes(fin, a_recv.at[0])
    out_along_second(2)
    laid = fin[...].reshape(ROWS, 3 * HEAD)
    mixed = attend(laid[:, :HEAD], laid[:, HEAD : 2 * HEAD], laid[:, 2 * HEAD :], bias[...])
    rmsg[...] = mixed.reshape(rmsg.shape).astype(jnp.bfloat16)
    exchange(1, rmsg, rfin)
    await_bytes(msg.at[0 : PEERS - 1], a_send.at[0])
    await_bytes(rfin, a_recv.at[1])
    out_along_second(3)
    back = jnp.dot(
        by_frame[...], rfin[...].reshape(ROWS, HEAD), preferred_element_type=jnp.float32
    ).astype(jnp.bfloat16)
    temporal = jnp.full((ROWS, HEAD), kind[odd], jnp.int32) == 1
    cbuf[...] = jnp.where(temporal, back, spatial).reshape(cbuf.shape)

    for step in (1, NX - 1, 2):
        remote(
            cbuf.at[odd],
            mbuf.at[band, odd],
            m_send.at[0, step],
            m_recv.at[0, step],
            (frame, band_at(step)),
        ).start()
    for step in (1, NX - 1, 2, 0):
        remote(
            cbuf.at[other],
            mbuf.at[band, odd],
            m_send.at[1, step],
            m_recv.at[1, step],
            (beside, band_at(step)),
        ).start()
    remote(
        cbuf.at[odd], mbuf.at[band, odd], n_send.at[0, 0], n_recv.at[0, 0], sibling
    ).start()
    last = pltpu.make_async_copy(cbuf.at[odd], mbuf.at[band, odd], m_recv.at[0, 0])
    last.start()
    for which, hop in ((1, 0), (0, 1), (0, 3), (1, 1), (1, 3), (0, 2), (1, 2)):
        block = mbuf.at[band_at(-hop), odd if which == 0 else other]
        await_bytes(block, m_recv.at[which, hop])
        remote(block, block, n_send.at[which, hop], n_recv.at[which, hop], sibling).start()
    out_along_second(4)
    last.wait()

    def project_out(source):
        left = jnp.concatenate([mbuf[source, 0], mbuf[source, 1]], axis=1)
        right = jnp.stack([obuf[0, source], obuf[1, :, source]], axis=1).reshape(
            2 * HEAD, WIDTH
        )
        return jnp.dot(left, right, preferred_element_type=jnp.float32)

    def own_core(hop, carry):
        total[...] += project_out(band_at(-hop))
        return carry

    def other_core(hop, carry):
        source = 2 * wrap(x - hop, NX) + 1 - core
        for which in range(2):
            await_bytes(
                mbuf.at[source, sibling_odd if which == 0 else 1 - sibling_odd],
                n_recv.at[which, hop],
            )
        total[...] += project_out(source)
        return carry

    total[...] = jnp.zeros_like(total)
    lax.fori_loop(0, NX, own_core, 0)
    lax.fori_loop(0, NX, other_core, 0)
    sbuf[...] = total[...].astype(jnp.bfloat16).reshape(sbuf.shape)

    def columns(which):
        return out.at[:, pl.ds(pl.multiple_of(which * WIDTH, HEAD), WIDTH)]

    for step in range(1, BANDS):
        there = wrap(band + step, BANDS)
        remote(
            sbuf.at[there], columns(band), f_send.at[step], f_recv.at[step], (frame, there)
        ).start()
    last = pltpu.make_async_copy(sbuf.at[band], columns(band), f_send.at[0])
    last.start()
    for step in range(1, BANDS):
        await_bytes(columns(wrap(band - step, BANDS)), f_recv.at[step])
    last.wait()

    await_bytes(rmsg.at[0 : PEERS - 1], a_send.at[1])
    for which in range(2):
        for hop in range(NX):
            if hop or which:
                await_bytes(cbuf.at[0], m_send.at[which, hop])
            await_bytes(cbuf.at[0], n_send.at[which, hop])
    for half in range(2):
        for way in range(2):
            await_bytes(obuf.at[half, 0 : hops(NY)[way]], o_send.at[half, 1, way])
    for step in range(1, BANDS):
        await_bytes(sbuf.at[0], f_send.at[step])


def body(tokens, qkv_weight, out_weight, head_kind):
    bf16 = jnp.bfloat16
    dma = pltpu.SemaphoreType.DMA
    hbm = pl.BlockSpec(memory_space=pltpu.HBM)
    return pl.pallas_call(
        kernel,
        out_shape=jax.ShapeDtypeStruct(tokens.shape, tokens.dtype),
        in_specs=[hbm] * 4,
        out_specs=hbm,
        scratch_shapes=[
            pltpu.VMEM((3, NY, PAIRS, 2, DEPTH, HEAD), bf16),
            pltpu.VMEM((2, 8, 8, 16, WIDTH), bf16),
            pltpu.VMEM((2, BANDS) + tokens.shape, bf16),
            pltpu.VMEM((PEERS, 2 * SHARE, 3 * HEAD), bf16),
            pltpu.VMEM((PEERS, 2 * SHARE, 3 * HEAD), bf16),
            pltpu.VMEM((PEERS, 2 * SHARE, HEAD), bf16),
            pltpu.VMEM((PEERS, 2 * SHARE, HEAD), bf16),
            pltpu.VMEM((2, POSITIONS, HEAD), bf16),
            pltpu.VMEM((BANDS, 2, POSITIONS, HEAD), bf16),
            pltpu.VMEM((BANDS, 16, WIDTH), bf16),
            pltpu.VMEM((ROWS, 3 * HEAD), jnp.float32),
            pltpu.VMEM((POSITIONS, WIDTH), jnp.float32),
            pltpu.VMEM((ROWS, ROWS), bf16),
            pltpu.VMEM((ROWS, ROWS), bf16),
            pltpu.VMEM((ROWS, ROWS), jnp.float32),
            pltpu.SMEM((2,), jnp.int32),
            dma((5,)),
            dma((3,)),
            dma((3,)),
            dma((2, 2)),
            dma((4,)),
            dma((2, 4, 4)),
            dma((2, 2, 2)),
            dma((2, 2, 4)),
            dma((2, 2, 4)),
            dma((3, NX)),
            dma((3, NX)),
            dma((NX,)),
            dma((NX,)),
            dma((2,)),
            dma((2,)),
            dma((2, NX)),
            dma((2, NX)),
            dma((2, NX)),
            dma((2, NX)),
            dma((BANDS,)),
            dma((BANDS,)),
        ],
        compiler_params=pltpu.CompilerParams(
            collective_id=0, has_side_effects=True, vmem_limit_bytes=64 * 1024 * 1024
        ),
    )(tokens, qkv_weight.transpose(1, 0, 2), out_weight, head_kind)


def solution(mesh):
    return jax.shard_map(
        body,
        mesh=mesh,
        in_specs=(
            P(("frame", "band"), None),
            P("frame", None, "band"),
            P("frame", "band"),
            P("band"),
        ),
        out_specs=P(("frame", "band"), None),
        check_vma=False,
    )
```

```python
import jax
import jax.numpy as jnp
from jax import lax
from jax.experimental import pallas as pl
from jax.experimental.pallas import tpu as pltpu
from jax.sharding import PartitionSpec as P

MESH = pl.DeviceIdType.MESH
NX = 4
NY = 8
NZ = 8
PAIRS = NZ // 2
BANDS = 2 * NX
PEERS = NY * PAIRS
HEAD = 128
POSITIONS = 128
ROWS = 2 * POSITIONS
SHARE = POSITIONS // PEERS
DEPTH = 48
WIDTH = 384


def remote(src, dst, send_sem, recv_sem, device):
    return pltpu.make_async_remote_copy(
        src_ref=src,
        dst_ref=dst,
        send_sem=send_sem,
        recv_sem=recv_sem,
        device_id=device,
        device_id_type=MESH,
    )


def await_bytes(ref, sem):
    pltpu.make_async_copy(ref, ref, sem).wait()


def attend(queries, keys, values, bias):
    scores = lax.dot_general(
        queries, keys, (((1,), (1,)), ((), ())), preferred_element_type=jnp.float32
    ) * (HEAD**-0.5)
    if bias is not None:
        scores = scores + bias
    raised = jnp.exp(scores - jnp.max(scores, axis=-1, keepdims=True))
    probs = (raised / jnp.sum(raised, axis=-1, keepdims=True)).astype(jnp.bfloat16)
    return jnp.dot(probs, values, preferred_element_type=jnp.float32)


def wrap(value, size):
    return lax.rem(value + 8 * size, size)


def hops(size):
    return (size // 2, (size - 1) // 2)


def wander(place):
    if isinstance(place, int):
        return (place + 1) // 2 * (2 * (place % 2) - 1)
    return lax.div(place + 1, 2) * (2 * lax.rem(place, 2) - 1)


class Grid:
    def __init__(self, block, device, here, sizes, sign, sems):
        self.block = block
        self.device = device
        self.first, self.second = here
        self.n_first, self.n_second = sizes
        self.sign = sign
        self.send, self.recv1, self.recv2 = sems

    def turn(self, way):
        return self.sign if way == 0 else -self.sign

    def to_second(self, block, way, step, place):
        there = wrap(self.second + self.turn(way), self.n_second)
        remote(
            block,
            block,
            self.send.at[1, way],
            self.recv2.at[way, step, place],
            self.device(self.first, there),
        ).start()

    def begin(self, src, dst, device):
        for way in range(2):
            there = wrap(self.second + self.turn(way), self.n_second)
            remote(
                src,
                dst,
                self.send.at[1, way],
                self.recv2.at[way, 0, 0],
                device(self.first, there),
            ).start()
        for place in range(1, self.n_first):
            there = wrap(self.first + self.sign * wander(place), self.n_first)
            remote(
                src,
                dst,
                self.send.at[0, 0],
                self.recv1.at[place],
                device(there, self.second),
            ).start()

    def along_first(self, place):
        block = self.block(
            wrap(self.first - self.sign * wander(place), self.n_first), self.second
        )
        await_bytes(block, self.recv1.at[place])
        for way in range(2):
            self.to_second(block, way, 0, place)

    def along_second(self, step, place):
        for way in range(2):
            count = hops(self.n_second)[way]
            if step > count:
                continue
            block = self.block(
                wrap(self.first - self.sign * wander(place), self.n_first),
                wrap(self.second - self.turn(way) * step, self.n_second),
            )
            await_bytes(block, self.recv2.at[way, step - 1, place])
            if step < count:
                self.to_second(block, way, step, place)


def kernel(
    tokens,
    qkv,
    out_weight,
    kind_hbm,
    out,
    wbuf,
    obuf,
    tbuf,
    msg,
    fin,
    rmsg,
    rfin,
    cbuf,
    mbuf,
    sbuf,
    qkv_sum,
    total,
    by_peer,
    by_frame,
    bias,
    kind,
    cross,
    own_sem,
    z_send,
    z_recv,
    w_send,
    w_recv1,
    w_recv2,
    o_send,
    o_recv1,
    o_recv2,
    t_send,
    t_recv,
    s_send,
    s_recv,
    a_send,
    a_recv,
    m_send,
    m_recv,
    n_send,
    n_recv,
    f_send,
    f_recv,
):
    frame = lax.axis_index("frame")
    band = lax.axis_index("band")
    y, z = lax.div(frame, NZ), lax.rem(frame, NZ)
    x, core = lax.div(band, 2), lax.rem(band, 2)
    across = z + (y - z) * core
    along = y + (z - y) * core
    pair, odd = lax.div(across, 2), lax.rem(across, 2)
    other = 1 - odd
    sign = 1 - 2 * core
    sibling_band = 2 * x + 1 - core
    sibling = (frame, sibling_band)
    sibling_odd = lax.rem(y + (z - y) * core, 2)
    me = along * PAIRS + pair

    def frame_at(along_there, across_there):
        return along_there * (NZ - (NZ - 1) * core) + across_there * (1 + (NZ - 1) * core)

    beside = frame_at(along, 2 * pair + other)

    def band_at(step):
        return 2 * wrap(x + step, NX) + core

    def peer(index):
        return (frame_at(lax.div(index, PAIRS), 2 * lax.rem(index, PAIRS) + odd), band)

    barrier = pltpu.get_barrier_semaphore()

    def greet(device):
        pl.semaphore_signal(barrier, inc=1, device_id=device, device_id_type=MESH)

    greet(sibling)
    greet((beside, sibling_band))
    for step in range(1, NY):
        greet((y * NZ + wrap(z + step, NZ), band))
        greet((wrap(y + step, NY) * NZ + z, band))
    for step in (1, -1):
        greet((frame_at(wrap(along + step, NY), 2 * pair + other), band))
    for step in range(1, NX):
        greet((frame, band_at(step)))

    def head_columns(which):
        return qkv.at[:, :, pl.ds(pl.multiple_of(which * HEAD, HEAD), HEAD)]

    own = [
        pltpu.make_async_copy(head_columns(odd), wbuf.at[:, along, pair, odd], own_sem.at[0]),
        pltpu.make_async_copy(out_weight.at[0:16], obuf.at[0, y, z], own_sem.at[1]),
        pltpu.make_async_copy(out_weight.at[16:32], obuf.at[1, z, y], own_sem.at[2]),
        pltpu.make_async_copy(tokens, tbuf.at[odd, band], own_sem.at[3]),
        pltpu.make_async_copy(kind_hbm, kind, own_sem.at[4]),
        pltpu.make_async_copy(head_columns(other), cross, own_sem.at[5]),
    ]
    for copy in own:
        copy.start()
    pl.semaphore_wait(barrier, 2 + NY - 1 + NZ - 1 + 2 + NX - 1)

    for copy in own:
        copy.wait()

    grid = Grid(
        lambda first, second: wbuf.at[:, second, first],
        lambda first, second: (frame_at(second, 2 * first + odd), band),
        (pair, along),
        (PAIRS, NY),
        sign,
        (w_send, w_recv1, w_recv2),
    )

    def token_along_x(which, block):
        for step in (1, NX - 1):
            remote(
                block, block, t_send.at[which, step], t_recv.at[which, step], (frame, band_at(step))
            ).start()

    def token_passed_on(which, by):
        if which == 0:
            block = tbuf.at[odd, band_at(-by)]
        else:
            block = tbuf.at[other, 2 * wrap(x - by, NX) + which - 1]
        remote(
            block, block, t_send.at[which, 2], t_recv.at[which, 2], (frame, band_at(by))
        ).start()

    def token_to_sibling(hop):
        from_band = band_at(-hop)
        remote(
            tbuf.at[odd, from_band],
            tbuf.at[sibling_odd, from_band],
            s_send.at[hop],
            s_recv.at[hop],
            sibling,
        ).start()

    here = wbuf.at[:, along, pair, odd]
    grid.begin(here, here, grid.device)
    grid.begin(
        cross, here, lambda first, second: (frame_at(second, 2 * first + other), band)
    )
    remote(cross, here, z_send.at[0], z_recv.at[0], (beside, band)).start()
    beside_z = y * NZ + z + 1 - 2 * lax.rem(z, 2)
    beside_y = (y + 1 - 2 * lax.rem(y, 2)) * NZ + z
    remote(
        tokens, tbuf.at[lax.rem(z, 2), band], z_send.at[1], z_recv.at[1 + core], (beside_z, 2 * x)
    ).start()
    remote(
        tokens, tbuf.at[lax.rem(y, 2), band], z_send.at[2], z_recv.at[1 + core], (beside_y, 2 * x + 1)
    ).start()
    token_along_x(0, tbuf.at[odd, band])
    remote(
        tbuf.at[odd, band], tbuf.at[sibling_odd, band], s_send.at[0], s_recv.at[0], sibling
    ).start()

    tall = lax.broadcasted_iota(jnp.int32, (ROWS, ROWS), 0)
    wide = lax.broadcasted_iota(jnp.int32, (ROWS, ROWS), 1)

    def origin(row):
        return (
            lax.rem(lax.div(row, SHARE), 2) * POSITIONS
            + lax.div(row, 2 * SHARE) * SHARE
            + lax.rem(row, SHARE)
        )

    qkv_sum[...] = jnp.zeros_like(qkv_sum)
    by_peer[...] = jnp.where(wide == origin(tall), 1.0, 0.0).astype(jnp.bfloat16)
    by_frame[...] = jnp.where(tall == origin(wide), 1.0, 0.0).astype(jnp.bfloat16)
    bias[...] = jnp.where(lax.rem(tall, SHARE) == lax.rem(wide, SHARE), 0.0, -1e30)

    for which in range(2):
        await_bytes(tbuf.at[other, 2 * x + which], z_recv.at[1 + which])
        token_along_x(1 + which, tbuf.at[other, 2 * x + which])

    def out_here(half):
        return (z, y) if half == 0 else (y, z)

    def out_device(half, first, second):
        return (second * NZ + first if half == 0 else first * NZ + second, band)

    def turn(way):
        return sign if way == 0 else -sign

    def out_send2(half, way, step, chunk):
        first, second = out_here(half)
        there = wrap(second + turn(way), NY)
        remote(
            chunk,
            chunk,
            o_send.at[half, 1, way],
            o_recv2.at[half, way, step],
            out_device(half, first, there),
        ).start()

    def out_along_first():
        for half in range(2):
            first, second = out_here(half)
            block = obuf.at[half, second, first]
            for step in range(1, NY):
                remote(
                    block,
                    block,
                    o_send.at[half, 0, 0],
                    o_recv1.at[half],
                    out_device(half, wrap(first + step, NY), second),
                ).start()

    def out_along_second(step):
        for half in range(2):
            first, second = out_here(half)
            for way in range(2):
                if step > hops(NY)[way]:
                    continue
                chunk = obuf.at[half, wrap(second - turn(way) * step, NY)]
                if step:
                    await_bytes(chunk, o_recv2.at[half, way, step - 1])
                if step < hops(NY)[way]:
                    out_send2(half, way, step, chunk)

    out_along_first()
    for place in range(1, PAIRS):
        grid.along_first(place)

    def ring_step(step):
        def one(place, carry):
            grid.along_second(step, place)
            return carry

        lax.fori_loop(0, PAIRS, one, 0)

    ring_step(1)
    for hop in (1, NX - 1):
        await_bytes(tbuf.at[odd, band_at(-hop)], t_recv.at[0, hop])
    token_passed_on(0, sign)
    token_to_sibling(1)
    token_to_sibling(NX - 1)
    ring_step(2)
    for which, by in ((1, 1), (2, -1)):
        for hop in (1, NX - 1):
            await_bytes(
                tbuf.at[other, 2 * wrap(x - hop, NX) + which - 1], t_recv.at[which, hop]
            )
        token_passed_on(which, by)
    for half in range(2):
        await_bytes(obuf.at[half, out_here(half)[1], 0 : NY - 1], o_recv1.at[half])
    out_along_second(0)
    await_bytes(tbuf.at[odd, band_at(2)], t_recv.at[0, 2])
    token_to_sibling(2)
    ring_step(3)
    for hop in range(NX):
        from_band = 2 * wrap(x - hop, NX) + 1 - core
        await_bytes(tbuf.at[odd, from_band], s_recv.at[hop])
        if hop == 2:
            for which in range(2):
                await_bytes(
                    tbuf.at[other, 2 * wrap(x - hop, NX) + which], t_recv.at[1 + which, hop]
                )
    ring_step(4)
    await_bytes(wbuf.at[:, along, pair, other], z_recv.at[0])
    out_along_second(1)

    chunk = 2 * NZ * DEPTH

    def project(step, right):
        at = pl.ds(pl.multiple_of(step * chunk, HEAD), chunk)
        qkv_sum[...] += jnp.dot(
            tbuf[:, :, :, at].reshape(ROWS, chunk),
            jnp.concatenate([right(slot) for slot in range(3)], axis=1),
            preferred_element_type=jnp.float32,
        )

    @pl.when(core == 0)
    def _():
        def one(step, carry):
            project(step, lambda slot: wbuf[slot, pl.ds(2 * step, 2)].reshape(chunk, HEAD))
            return carry

        lax.fori_loop(0, NY // 2, one, 0)

    @pl.when(core == 1)
    def _():
        def one(step, carry):
            project(
                step,
                lambda slot: jnp.concatenate(
                    [
                        wbuf[slot, :, step, parity].reshape(chunk // 2, HEAD)
                        for parity in range(2)
                    ],
                    axis=0,
                ),
            )
            return carry

        lax.fori_loop(0, NY // 2, one, 0)

    rounded = qkv_sum[...].astype(jnp.bfloat16)

    msg[...] = (
        jnp.dot(by_peer[...], rounded, preferred_element_type=jnp.float32)
        .reshape(msg.shape)
        .astype(jnp.bfloat16)
    )

    def exchange(stage, source, target):
        def send(step, carry):
            there = lax.rem(me + step, PEERS)
            remote(
                source.at[there], target.at[me], a_send.at[stage], a_recv.at[stage], peer(there)
            ).start()
            return carry

        pltpu.make_async_copy(source.at[me], target.at[me], a_recv.at[stage]).start()
        lax.fori_loop(1, PEERS, send, 0)

    exchange(0, msg, fin)
    spatial = jnp.concatenate(
        [
            attend(
                rounded[at : at + POSITIONS, :HEAD],
                rounded[at : at + POSITIONS, HEAD : 2 * HEAD],
                rounded[at : at + POSITIONS, 2 * HEAD :],
                None,
            )
            for at in (0, POSITIONS)
        ],
        axis=0,
    ).astype(jnp.bfloat16)
    await_bytes(wbuf.at[:, 0, 0, 0], z_send.at[0])
    await_bytes(tbuf.at[0, 0], z_send.at[1])
    await_bytes(tbuf.at[0, 0], z_send.at[2])
    await_bytes(wbuf.at[:, 0, 0 : PAIRS - 1], w_send.at[0, 0])
    for way in range(2):
        await_bytes(wbuf.at[:, 0 : hops(NY)[way]], w_send.at[1, way])
        await_bytes(obuf.at[way, 0, 0 : NY - 1], o_send.at[way, 0, 0])
    for hop in range(NX):
        await_bytes(tbuf.at[0, 0], s_send.at[hop])
        if hop:
            for which in range(3):
                await_bytes(tbuf.at[0, 0], t_send.at[which, hop])
    await_bytes(fin, a_recv.at[0])
    out_along_second(2)
    laid = fin[...].reshape(ROWS, 3 * HEAD)
    mixed = attend(laid[:, :HEAD], laid[:, HEAD : 2 * HEAD], laid[:, 2 * HEAD :], bias[...])
    rmsg[...] = mixed.reshape(rmsg.shape).astype(jnp.bfloat16)
    exchange(1, rmsg, rfin)
    await_bytes(msg.at[0 : PEERS - 1], a_send.at[0])
    await_bytes(rfin, a_recv.at[1])
    out_along_second(3)
    back = jnp.dot(
        by_frame[...], rfin[...].reshape(ROWS, HEAD), preferred_element_type=jnp.float32
    ).astype(jnp.bfloat16)
    temporal = jnp.full((ROWS, HEAD), kind[odd], jnp.int32) == 1
    cbuf[...] = jnp.where(temporal, back, spatial).reshape(cbuf.shape)

    for step in (1, NX - 1, 2):
        remote(
            cbuf.at[odd],
            mbuf.at[band, odd],
            m_send.at[0, step],
            m_recv.at[0, step],
            (frame, band_at(step)),
        ).start()
    for step in (1, NX - 1, 2, 0):
        remote(
            cbuf.at[other],
            mbuf.at[band, odd],
            m_send.at[1, step],
            m_recv.at[1, step],
            (beside, band_at(step)),
        ).start()
    remote(
        cbuf.at[odd], mbuf.at[band, odd], n_send.at[0, 0], n_recv.at[0, 0], sibling
    ).start()
    last = pltpu.make_async_copy(cbuf.at[odd], mbuf.at[band, odd], m_recv.at[0, 0])
    last.start()
    for which, hop in ((1, 0), (0, 1), (0, 3), (1, 1), (1, 3), (0, 2), (1, 2)):
        block = mbuf.at[band_at(-hop), odd if which == 0 else other]
        await_bytes(block, m_recv.at[which, hop])
        remote(block, block, n_send.at[which, hop], n_recv.at[which, hop], sibling).start()
    out_along_second(4)
    last.wait()

    def project_out(source):
        left = jnp.concatenate([mbuf[source, 0], mbuf[source, 1]], axis=1)
        right = jnp.stack([obuf[0, source], obuf[1, :, source]], axis=1).reshape(
            2 * HEAD, WIDTH
        )
        return jnp.dot(left, right, preferred_element_type=jnp.float32)

    def own_core(hop, carry):
        total[...] += project_out(band_at(-hop))
        return carry

    def other_core(hop, carry):
        source = 2 * wrap(x - hop, NX) + 1 - core
        for which in range(2):
            await_bytes(
                mbuf.at[source, sibling_odd if which == 0 else 1 - sibling_odd],
                n_recv.at[which, hop],
            )
        total[...] += project_out(source)
        return carry

    total[...] = jnp.zeros_like(total)
    lax.fori_loop(0, NX, own_core, 0)
    lax.fori_loop(0, NX, other_core, 0)
    sbuf[...] = total[...].astype(jnp.bfloat16).reshape(sbuf.shape)

    def columns(which):
        return out.at[:, pl.ds(pl.multiple_of(which * WIDTH, HEAD), WIDTH)]

    for step in range(1, BANDS):
        there = wrap(band + step, BANDS)
        remote(
            sbuf.at[there], columns(band), f_send.at[step], f_recv.at[step], (frame, there)
        ).start()
    last = pltpu.make_async_copy(sbuf.at[band], columns(band), f_send.at[0])
    last.start()
    for step in range(1, BANDS):
        await_bytes(columns(wrap(band - step, BANDS)), f_recv.at[step])
    last.wait()

    await_bytes(rmsg.at[0 : PEERS - 1], a_send.at[1])
    for which in range(2):
        for hop in range(NX):
            if hop or which:
                await_bytes(cbuf.at[0], m_send.at[which, hop])
            await_bytes(cbuf.at[0], n_send.at[which, hop])
    for half in range(2):
        for way in range(2):
            await_bytes(obuf.at[half, 0 : hops(NY)[way]], o_send.at[half, 1, way])
    for step in range(1, BANDS):
        await_bytes(sbuf.at[0], f_send.at[step])


def body(tokens, qkv_weight, out_weight, head_kind):
    bf16 = jnp.bfloat16
    dma = pltpu.SemaphoreType.DMA
    hbm = pl.BlockSpec(memory_space=pltpu.HBM)
    return pl.pallas_call(
        kernel,
        out_shape=jax.ShapeDtypeStruct(tokens.shape, tokens.dtype),
        in_specs=[hbm] * 4,
        out_specs=hbm,
        scratch_shapes=[
            pltpu.VMEM((3, NY, PAIRS, 2, DEPTH, HEAD), bf16),
            pltpu.VMEM((2, 8, 8, 16, WIDTH), bf16),
            pltpu.VMEM((2, BANDS) + tokens.shape, bf16),
            pltpu.VMEM((PEERS, 2 * SHARE, 3 * HEAD), bf16),
            pltpu.VMEM((PEERS, 2 * SHARE, 3 * HEAD), bf16),
            pltpu.VMEM((PEERS, 2 * SHARE, HEAD), bf16),
            pltpu.VMEM((PEERS, 2 * SHARE, HEAD), bf16),
            pltpu.VMEM((2, POSITIONS, HEAD), bf16),
            pltpu.VMEM((BANDS, 2, POSITIONS, HEAD), bf16),
            pltpu.VMEM((BANDS, 16, WIDTH), bf16),
            pltpu.VMEM((ROWS, 3 * HEAD), jnp.float32),
            pltpu.VMEM((POSITIONS, WIDTH), jnp.float32),
            pltpu.VMEM((ROWS, ROWS), bf16),
            pltpu.VMEM((ROWS, ROWS), bf16),
            pltpu.VMEM((ROWS, ROWS), jnp.float32),
            pltpu.SMEM((2,), jnp.int32),
            pltpu.VMEM((3, DEPTH, HEAD), bf16),
            dma((6,)),
            dma((3,)),
            dma((3,)),
            dma((2, 2)),
            dma((4,)),
            dma((2, 4, 4)),
            dma((2, 2, 2)),
            dma((2,)),
            dma((2, 2, 4)),
            dma((3, NX)),
            dma((3, NX)),
            dma((NX,)),
            dma((NX,)),
            dma((2,)),
            dma((2,)),
            dma((2, NX)),
            dma((2, NX)),
            dma((2, NX)),
            dma((2, NX)),
            dma((BANDS,)),
            dma((BANDS,)),
        ],
        compiler_params=pltpu.CompilerParams(
            collective_id=0, has_side_effects=True, vmem_limit_bytes=64 * 1024 * 1024
        ),
    )(tokens, qkv_weight.transpose(1, 0, 2), out_weight, head_kind)


def solution(mesh):
    return jax.shard_map(
        body,
        mesh=mesh,
        in_specs=(
            P(("frame", "band"), None),
            P("frame", None, "band"),
            P("frame", "band"),
            P("band"),
        ),
        out_specs=P(("frame", "band"), None),
        check_vma=False,
    )
```

```python
import jax
import jax.numpy as jnp
from jax import lax
from jax.experimental import pallas as pl
from jax.experimental.pallas import tpu as pltpu
from jax.sharding import PartitionSpec as P

MESH = pl.DeviceIdType.MESH
NX = 4
NY = 8
NZ = 8
PAIRS = NZ // 2
BANDS = 2 * NX
PEERS = NY * PAIRS
HEAD = 128
POSITIONS = 128
ROWS = 2 * POSITIONS
SHARE = POSITIONS // PEERS
DEPTH = 48
WIDTH = 384


def remote(src, dst, send_sem, recv_sem, device):
    return pltpu.make_async_remote_copy(
        src_ref=src,
        dst_ref=dst,
        send_sem=send_sem,
        recv_sem=recv_sem,
        device_id=device,
        device_id_type=MESH,
    )


def await_bytes(ref, sem):
    pltpu.make_async_copy(ref, ref, sem).wait()


def attend(queries, keys, values, bias):
    scores = lax.dot_general(
        queries, keys, (((1,), (1,)), ((), ())), preferred_element_type=jnp.float32
    ) * (HEAD**-0.5)
    if bias is not None:
        scores = scores + bias
    raised = jnp.exp(scores - jnp.max(scores, axis=-1, keepdims=True))
    probs = (raised / jnp.sum(raised, axis=-1, keepdims=True)).astype(jnp.bfloat16)
    return jnp.dot(probs, values, preferred_element_type=jnp.float32)


def wrap(value, size):
    return lax.rem(value + 8 * size, size)


def hops(size):
    return (size // 2, (size - 1) // 2)


def wander(place):
    if isinstance(place, int):
        return (place + 1) // 2 * (2 * (place % 2) - 1)
    return lax.div(place + 1, 2) * (2 * lax.rem(place, 2) - 1)


class Grid:
    def __init__(self, block, device, here, sizes, sign, sems):
        self.block = block
        self.device = device
        self.first, self.second = here
        self.n_first, self.n_second = sizes
        self.sign = sign
        self.send, self.recv1, self.recv2 = sems

    def turn(self, way):
        return self.sign if way == 0 else -self.sign

    def to_second(self, block, way, step, place):
        there = wrap(self.second + self.turn(way), self.n_second)
        remote(
            block,
            block,
            self.send.at[1, way],
            self.recv2.at[way, step, place],
            self.device(self.first, there),
        ).start()

    def begin(self, src, dst, device):
        for way in range(2):
            there = wrap(self.second + self.turn(way), self.n_second)
            remote(
                src,
                dst,
                self.send.at[1, way],
                self.recv2.at[way, 0, 0],
                device(self.first, there),
            ).start()
        for place in range(1, self.n_first):
            there = wrap(self.first + self.sign * wander(place), self.n_first)
            remote(
                src,
                dst,
                self.send.at[0, 0],
                self.recv1.at[place],
                device(there, self.second),
            ).start()

    def along_first(self, place):
        block = self.block(
            wrap(self.first - self.sign * wander(place), self.n_first), self.second
        )
        await_bytes(block, self.recv1.at[place])
        for way in range(2):
            self.to_second(block, way, 0, place)

    def along_second(self, step, place):
        for way in range(2):
            count = hops(self.n_second)[way]
            if step > count:
                continue
            block = self.block(
                wrap(self.first - self.sign * wander(place), self.n_first),
                wrap(self.second - self.turn(way) * step, self.n_second),
            )
            await_bytes(block, self.recv2.at[way, step - 1, place])
            if step < count:
                self.to_second(block, way, step, place)


def kernel(
    tokens,
    qkv,
    out_weight,
    kind_hbm,
    out,
    wbuf,
    obuf,
    tbuf,
    msg,
    fin,
    rmsg,
    rfin,
    cbuf,
    mbuf,
    sbuf,
    qkv_sum,
    total,
    by_peer,
    by_frame,
    bias,
    kind,
    cross,
    own_sem,
    z_send,
    z_recv,
    w_send,
    w_recv1,
    w_recv2,
    o_send,
    o_recv1,
    o_recv2,
    t_send,
    t_recv,
    s_send,
    s_recv,
    a_send,
    a_recv,
    m_send,
    m_recv,
    n_send,
    n_recv,
    f_send,
    f_recv,
):
    frame = lax.axis_index("frame")
    band = lax.axis_index("band")
    y, z = lax.div(frame, NZ), lax.rem(frame, NZ)
    x, core = lax.div(band, 2), lax.rem(band, 2)
    across = z + (y - z) * core
    along = y + (z - y) * core
    pair, odd = lax.div(across, 2), lax.rem(across, 2)
    other = 1 - odd
    sign = 1 - 2 * core
    sibling_band = 2 * x + 1 - core
    sibling = (frame, sibling_band)
    sibling_odd = lax.rem(y + (z - y) * core, 2)
    me = along * PAIRS + pair

    def frame_at(along_there, across_there):
        return along_there * (NZ - (NZ - 1) * core) + across_there * (1 + (NZ - 1) * core)

    beside = frame_at(along, 2 * pair + other)

    def band_at(step):
        return 2 * wrap(x + step, NX) + core

    def peer(index):
        return (frame_at(lax.div(index, PAIRS), 2 * lax.rem(index, PAIRS) + odd), band)

    barrier = pltpu.get_barrier_semaphore()

    def greet(device):
        pl.semaphore_signal(barrier, inc=1, device_id=device, device_id_type=MESH)

    greet(sibling)
    greet((beside, sibling_band))
    for step in range(1, NY):
        greet((y * NZ + wrap(z + step, NZ), band))
        greet((wrap(y + step, NY) * NZ + z, band))
    for step in (1, -1):
        greet((frame_at(wrap(along + step, NY), 2 * pair + other), band))
    for step in range(1, NX):
        greet((frame, band_at(step)))

    def head_columns(which):
        return qkv.at[:, :, pl.ds(pl.multiple_of(which * HEAD, HEAD), HEAD)]

    own = [
        pltpu.make_async_copy(head_columns(odd), wbuf.at[:, along, pair, odd], own_sem.at[0]),
        pltpu.make_async_copy(out_weight.at[0:16], obuf.at[0, y, z], own_sem.at[1]),
        pltpu.make_async_copy(out_weight.at[16:32], obuf.at[1, z, y], own_sem.at[2]),
        pltpu.make_async_copy(tokens, tbuf.at[odd, band], own_sem.at[3]),
        pltpu.make_async_copy(kind_hbm, kind, own_sem.at[4]),
        pltpu.make_async_copy(head_columns(other), cross, own_sem.at[5]),
    ]
    for copy in own:
        copy.start()
    pl.semaphore_wait(barrier, 2 + NY - 1 + NZ - 1 + 2 + NX - 1)

    for copy in own:
        copy.wait()

    grid = Grid(
        lambda first, second: wbuf.at[:, second, first],
        lambda first, second: (frame_at(second, 2 * first + odd), band),
        (pair, along),
        (PAIRS, NY),
        sign,
        (w_send, w_recv1, w_recv2),
    )

    def token_along_x(which, block):
        for step in (1, NX - 1):
            remote(
                block, block, t_send.at[which, step], t_recv.at[which, step], (frame, band_at(step))
            ).start()

    def token_passed_on(which, by):
        if which == 0:
            block = tbuf.at[odd, band_at(-by)]
        else:
            block = tbuf.at[other, 2 * wrap(x - by, NX) + which - 1]
        remote(
            block, block, t_send.at[which, 2], t_recv.at[which, 2], (frame, band_at(by))
        ).start()

    def token_to_sibling(hop):
        from_band = band_at(-hop)
        remote(
            tbuf.at[odd, from_band],
            tbuf.at[sibling_odd, from_band],
            s_send.at[hop],
            s_recv.at[hop],
            sibling,
        ).start()

    here = wbuf.at[:, along, pair, odd]
    grid.begin(here, here, grid.device)
    grid.begin(
        cross, here, lambda first, second: (frame_at(second, 2 * first + other), band)
    )
    remote(cross, here, z_send.at[0], z_recv.at[0], (beside, band)).start()
    beside_z = y * NZ + z + 1 - 2 * lax.rem(z, 2)
    beside_y = (y + 1 - 2 * lax.rem(y, 2)) * NZ + z
    remote(
        tokens, tbuf.at[lax.rem(z, 2), band], z_send.at[1], z_recv.at[1 + core], (beside_z, 2 * x)
    ).start()
    remote(
        tokens, tbuf.at[lax.rem(y, 2), band], z_send.at[2], z_recv.at[1 + core], (beside_y, 2 * x + 1)
    ).start()
    token_along_x(0, tbuf.at[odd, band])
    remote(
        tbuf.at[odd, band], tbuf.at[sibling_odd, band], s_send.at[0], s_recv.at[0], sibling
    ).start()

    tall = lax.broadcasted_iota(jnp.int32, (ROWS, ROWS), 0)
    wide = lax.broadcasted_iota(jnp.int32, (ROWS, ROWS), 1)

    def origin(row):
        return (
            lax.rem(lax.div(row, SHARE), 2) * POSITIONS
            + lax.div(row, 2 * SHARE) * SHARE
            + lax.rem(row, SHARE)
        )

    qkv_sum[...] = jnp.zeros_like(qkv_sum)
    by_peer[...] = jnp.where(wide == origin(tall), 1.0, 0.0).astype(jnp.bfloat16)
    by_frame[...] = jnp.where(tall == origin(wide), 1.0, 0.0).astype(jnp.bfloat16)
    bias[...] = jnp.where(lax.rem(tall, SHARE) == lax.rem(wide, SHARE), 0.0, -1e30)

    for which in range(2):
        await_bytes(tbuf.at[other, 2 * x + which], z_recv.at[1 + which])
        token_along_x(1 + which, tbuf.at[other, 2 * x + which])

    def out_here(half):
        return (z, y) if half == 0 else (y, z)

    def out_device(half, first, second):
        return (second * NZ + first if half == 0 else first * NZ + second, band)

    def turn(way):
        return sign if way == 0 else -sign

    def out_send2(half, way, step, chunk):
        first, second = out_here(half)
        there = wrap(second + turn(way), NY)
        remote(
            chunk,
            chunk,
            o_send.at[half, 1, way],
            o_recv2.at[half, way, step],
            out_device(half, first, there),
        ).start()

    def out_along_first():
        for half in range(2):
            first, second = out_here(half)
            block = obuf.at[half, second, first]
            for step in range(1, NY):
                remote(
                    block,
                    block,
                    o_send.at[half, 0, 0],
                    o_recv1.at[half],
                    out_device(half, wrap(first + step, NY), second),
                ).start()

    def out_along_second(step):
        for half in range(2):
            first, second = out_here(half)
            for way in range(2):
                if step > hops(NY)[way]:
                    continue
                chunk = obuf.at[half, wrap(second - turn(way) * step, NY)]
                if step:
                    await_bytes(chunk, o_recv2.at[half, way, step - 1])
                if step < hops(NY)[way]:
                    out_send2(half, way, step, chunk)

    out_along_first()
    for place in range(1, PAIRS):
        grid.along_first(place)

    def ring_step(step):
        def one(place, carry):
            grid.along_second(step, place)
            return carry

        lax.fori_loop(0, PAIRS, one, 0)

    ring_step(1)
    for hop in (1, NX - 1):
        await_bytes(tbuf.at[odd, band_at(-hop)], t_recv.at[0, hop])
    token_passed_on(0, sign)
    token_to_sibling(1)
    token_to_sibling(NX - 1)
    ring_step(2)
    for which, by in ((1, 1), (2, -1)):
        for hop in (1, NX - 1):
            await_bytes(
                tbuf.at[other, 2 * wrap(x - hop, NX) + which - 1], t_recv.at[which, hop]
            )
        token_passed_on(which, by)
    for half in range(2):
        await_bytes(obuf.at[half, out_here(half)[1], 0 : NY - 1], o_recv1.at[half])
    out_along_second(0)
    await_bytes(tbuf.at[odd, band_at(2)], t_recv.at[0, 2])
    token_to_sibling(2)
    ring_step(3)
    for hop in range(NX):
        from_band = 2 * wrap(x - hop, NX) + 1 - core
        await_bytes(tbuf.at[odd, from_band], s_recv.at[hop])
        if hop == 2:
            for which in range(2):
                await_bytes(
                    tbuf.at[other, 2 * wrap(x - hop, NX) + which], t_recv.at[1 + which, hop]
                )
    ring_step(4)
    await_bytes(wbuf.at[:, along, pair, other], z_recv.at[0])
    out_along_second(1)

    chunk = 2 * NZ * DEPTH

    def project(step, right):
        at = pl.ds(pl.multiple_of(step * chunk, HEAD), chunk)
        qkv_sum[...] += jnp.dot(
            tbuf[:, :, :, at].reshape(ROWS, chunk),
            jnp.concatenate([right(slot) for slot in range(3)], axis=1),
            preferred_element_type=jnp.float32,
        )

    @pl.when(core == 0)
    def _():
        def one(step, carry):
            project(step, lambda slot: wbuf[slot, pl.ds(2 * step, 2)].reshape(chunk, HEAD))
            return carry

        lax.fori_loop(0, NY // 2, one, 0)

    @pl.when(core == 1)
    def _():
        def one(step, carry):
            project(
                step,
                lambda slot: jnp.concatenate(
                    [
                        wbuf[slot, :, step, parity].reshape(chunk // 2, HEAD)
                        for parity in range(2)
                    ],
                    axis=0,
                ),
            )
            return carry

        lax.fori_loop(0, NY // 2, one, 0)

    rounded = qkv_sum[...].astype(jnp.bfloat16)

    msg[...] = (
        jnp.dot(by_peer[...], rounded, preferred_element_type=jnp.float32)
        .reshape(msg.shape)
        .astype(jnp.bfloat16)
    )

    def exchange(stage, source, target):
        def send(step, carry):
            there = lax.rem(me + step, PEERS)
            remote(
                source.at[there], target.at[me], a_send.at[stage], a_recv.at[stage], peer(there)
            ).start()
            return carry

        pltpu.make_async_copy(source.at[me], target.at[me], a_recv.at[stage]).start()
        lax.fori_loop(1, PEERS, send, 0)

    exchange(0, msg, fin)
    spatial = jnp.concatenate(
        [
            attend(
                rounded[at : at + POSITIONS, :HEAD],
                rounded[at : at + POSITIONS, HEAD : 2 * HEAD],
                rounded[at : at + POSITIONS, 2 * HEAD :],
                None,
            )
            for at in (0, POSITIONS)
        ],
        axis=0,
    ).astype(jnp.bfloat16)
    out_along_second(2)

    await_bytes(wbuf.at[:, 0, 0, 0], z_send.at[0])
    await_bytes(tbuf.at[0, 0], z_send.at[1])
    await_bytes(tbuf.at[0, 0], z_send.at[2])
    await_bytes(wbuf.at[:, 0, 0 : PAIRS - 1], w_send.at[0, 0])
    for way in range(2):
        await_bytes(wbuf.at[:, 0 : hops(NY)[way]], w_send.at[1, way])
        await_bytes(obuf.at[way, 0, 0 : NY - 1], o_send.at[way, 0, 0])
    for hop in range(NX):
        await_bytes(tbuf.at[0, 0], s_send.at[hop])
        if hop:
            for which in range(3):
                await_bytes(tbuf.at[0, 0], t_send.at[which, hop])
    await_bytes(fin, a_recv.at[0])
    laid = fin[...].reshape(ROWS, 3 * HEAD)
    mixed = attend(laid[:, :HEAD], laid[:, HEAD : 2 * HEAD], laid[:, 2 * HEAD :], bias[...])
    rmsg[...] = mixed.reshape(rmsg.shape).astype(jnp.bfloat16)
    exchange(1, rmsg, rfin)
    out_along_second(3)
    await_bytes(msg.at[0 : PEERS - 1], a_send.at[0])
    await_bytes(rfin, a_recv.at[1])
    back = jnp.dot(
        by_frame[...], rfin[...].reshape(ROWS, HEAD), preferred_element_type=jnp.float32
    ).astype(jnp.bfloat16)
    temporal = jnp.full((ROWS, HEAD), kind[odd], jnp.int32) == 1
    cbuf[...] = jnp.where(temporal, back, spatial).reshape(cbuf.shape)

    for step in (1, NX - 1, 2):
        remote(
            cbuf.at[odd],
            mbuf.at[band, odd],
            m_send.at[0, step],
            m_recv.at[0, step],
            (frame, band_at(step)),
        ).start()
    for step in (1, NX - 1, 2, 0):
        remote(
            cbuf.at[other],
            mbuf.at[band, odd],
            m_send.at[1, step],
            m_recv.at[1, step],
            (beside, band_at(step)),
        ).start()
    remote(
        cbuf.at[odd], mbuf.at[band, odd], n_send.at[0, 0], n_recv.at[0, 0], sibling
    ).start()
    last = pltpu.make_async_copy(cbuf.at[odd], mbuf.at[band, odd], m_recv.at[0, 0])
    last.start()
    for which, hop in ((1, 0), (0, 1), (0, 3), (1, 1), (1, 3), (0, 2), (1, 2)):
        block = mbuf.at[band_at(-hop), odd if which == 0 else other]
        await_bytes(block, m_recv.at[which, hop])
        remote(block, block, n_send.at[which, hop], n_recv.at[which, hop], sibling).start()
    out_along_second(4)
    last.wait()

    def project_out(source):
        left = jnp.concatenate([mbuf[source, 0], mbuf[source, 1]], axis=1)
        right = jnp.stack([obuf[0, source], obuf[1, :, source]], axis=1).reshape(
            2 * HEAD, WIDTH
        )
        return jnp.dot(left, right, preferred_element_type=jnp.float32)

    def own_core(hop, carry):
        total[...] += project_out(band_at(-hop))
        return carry

    def other_core(hop, carry):
        source = 2 * wrap(x - hop, NX) + 1 - core
        for which in range(2):
            await_bytes(
                mbuf.at[source, sibling_odd if which == 0 else 1 - sibling_odd],
                n_recv.at[which, hop],
            )
        total[...] += project_out(source)
        return carry

    total[...] = jnp.zeros_like(total)
    lax.fori_loop(0, NX, own_core, 0)
    lax.fori_loop(0, NX, other_core, 0)
    sbuf[...] = total[...].astype(jnp.bfloat16).reshape(sbuf.shape)

    def columns(which):
        return out.at[:, pl.ds(pl.multiple_of(which * WIDTH, HEAD), WIDTH)]

    for step in range(1, BANDS):
        there = wrap(band + step, BANDS)
        remote(
            sbuf.at[there], columns(band), f_send.at[step], f_recv.at[step], (frame, there)
        ).start()
    last = pltpu.make_async_copy(sbuf.at[band], columns(band), f_send.at[0])
    last.start()
    for step in range(1, BANDS):
        await_bytes(columns(wrap(band - step, BANDS)), f_recv.at[step])
    last.wait()

    await_bytes(rmsg.at[0 : PEERS - 1], a_send.at[1])
    for which in range(2):
        for hop in range(NX):
            if hop or which:
                await_bytes(cbuf.at[0], m_send.at[which, hop])
            await_bytes(cbuf.at[0], n_send.at[which, hop])
    for half in range(2):
        for way in range(2):
            await_bytes(obuf.at[half, 0 : hops(NY)[way]], o_send.at[half, 1, way])
    for step in range(1, BANDS):
        await_bytes(sbuf.at[0], f_send.at[step])


def body(tokens, qkv_weight, out_weight, head_kind):
    bf16 = jnp.bfloat16
    dma = pltpu.SemaphoreType.DMA
    hbm = pl.BlockSpec(memory_space=pltpu.HBM)
    return pl.pallas_call(
        kernel,
        out_shape=jax.ShapeDtypeStruct(tokens.shape, tokens.dtype),
        in_specs=[hbm] * 4,
        out_specs=hbm,
        scratch_shapes=[
            pltpu.VMEM((3, NY, PAIRS, 2, DEPTH, HEAD), bf16),
            pltpu.VMEM((2, 8, 8, 16, WIDTH), bf16),
            pltpu.VMEM((2, BANDS) + tokens.shape, bf16),
            pltpu.VMEM((PEERS, 2 * SHARE, 3 * HEAD), bf16),
            pltpu.VMEM((PEERS, 2 * SHARE, 3 * HEAD), bf16),
            pltpu.VMEM((PEERS, 2 * SHARE, HEAD), bf16),
            pltpu.VMEM((PEERS, 2 * SHARE, HEAD), bf16),
            pltpu.VMEM((2, POSITIONS, HEAD), bf16),
            pltpu.VMEM((BANDS, 2, POSITIONS, HEAD), bf16),
            pltpu.VMEM((BANDS, 16, WIDTH), bf16),
            pltpu.VMEM((ROWS, 3 * HEAD), jnp.float32),
            pltpu.VMEM((POSITIONS, WIDTH), jnp.float32),
            pltpu.VMEM((ROWS, ROWS), bf16),
            pltpu.VMEM((ROWS, ROWS), bf16),
            pltpu.VMEM((ROWS, ROWS), jnp.float32),
            pltpu.SMEM((2,), jnp.int32),
            pltpu.VMEM((3, DEPTH, HEAD), bf16),
            dma((6,)),
            dma((3,)),
            dma((3,)),
            dma((2, 2)),
            dma((4,)),
            dma((2, 4, 4)),
            dma((2, 2, 2)),
            dma((2,)),
            dma((2, 2, 4)),
            dma((3, NX)),
            dma((3, NX)),
            dma((NX,)),
            dma((NX,)),
            dma((2,)),
            dma((2,)),
            dma((2, NX)),
            dma((2, NX)),
            dma((2, NX)),
            dma((2, NX)),
            dma((BANDS,)),
            dma((BANDS,)),
        ],
        compiler_params=pltpu.CompilerParams(
            collective_id=0, has_side_effects=True, vmem_limit_bytes=64 * 1024 * 1024
        ),
    )(tokens, qkv_weight.transpose(1, 0, 2), out_weight, head_kind)


def solution(mesh):
    return jax.shard_map(
        body,
        mesh=mesh,
        in_specs=(
            P(("frame", "band"), None),
            P("frame", None, "band"),
            P("frame", "band"),
            P("band"),
        ),
        out_specs=P(("frame", "band"), None),
        check_vma=False,
    )
```

```python
import jax
import jax.numpy as jnp
from jax import lax
from jax.experimental import pallas as pl
from jax.experimental.pallas import tpu as pltpu
from jax.sharding import PartitionSpec as P

MESH = pl.DeviceIdType.MESH
NX = 4
NY = 8
NZ = 8
PAIRS = NZ // 2
BANDS = 2 * NX
PEERS = NY * PAIRS
HEAD = 128
POSITIONS = 128
ROWS = 2 * POSITIONS
SHARE = POSITIONS // PEERS
DEPTH = 48
WIDTH = 384


def remote(src, dst, send_sem, recv_sem, device):
    return pltpu.make_async_remote_copy(
        src_ref=src,
        dst_ref=dst,
        send_sem=send_sem,
        recv_sem=recv_sem,
        device_id=device,
        device_id_type=MESH,
    )


def await_bytes(ref, sem):
    pltpu.make_async_copy(ref, ref, sem).wait()


def attend(queries, keys, values, bias):
    scores = lax.dot_general(
        queries, keys, (((1,), (1,)), ((), ())), preferred_element_type=jnp.float32
    ) * (HEAD**-0.5)
    if bias is not None:
        scores = scores + bias
    raised = jnp.exp(scores - jnp.max(scores, axis=-1, keepdims=True))
    probs = (raised / jnp.sum(raised, axis=-1, keepdims=True)).astype(jnp.bfloat16)
    return jnp.dot(probs, values, preferred_element_type=jnp.float32)


def wrap(value, size):
    return lax.rem(value + 8 * size, size)


def hops(size):
    return (size // 2, (size - 1) // 2)


def wander(place):
    if isinstance(place, int):
        return (place + 1) // 2 * (2 * (place % 2) - 1)
    return lax.div(place + 1, 2) * (2 * lax.rem(place, 2) - 1)


class Grid:
    def __init__(self, block, device, here, sizes, sign, sems):
        self.block = block
        self.device = device
        self.first, self.second = here
        self.n_first, self.n_second = sizes
        self.sign = sign
        self.send, self.recv1, self.recv2 = sems

    def turn(self, way):
        return self.sign if way == 0 else -self.sign

    def to_second(self, block, way, step, place):
        there = wrap(self.second + self.turn(way), self.n_second)
        remote(
            block,
            block,
            self.send.at[1, way],
            self.recv2.at[way, step, place],
            self.device(self.first, there),
        ).start()

    def begin(self, src, dst, device):
        for way in range(2):
            there = wrap(self.second + self.turn(way), self.n_second)
            remote(
                src,
                dst,
                self.send.at[1, way],
                self.recv2.at[way, 0, 0],
                device(self.first, there),
            ).start()
        for place in range(1, self.n_first):
            there = wrap(self.first + self.sign * wander(place), self.n_first)
            remote(
                src,
                dst,
                self.send.at[0, 0],
                self.recv1.at[place],
                device(there, self.second),
            ).start()

    def along_first(self, place):
        block = self.block(
            wrap(self.first - self.sign * wander(place), self.n_first), self.second
        )
        await_bytes(block, self.recv1.at[place])
        for way in range(2):
            self.to_second(block, way, 0, place)

    def along_second(self, step, place):
        for way in range(2):
            count = hops(self.n_second)[way]
            if step > count:
                continue
            block = self.block(
                wrap(self.first - self.sign * wander(place), self.n_first),
                wrap(self.second - self.turn(way) * step, self.n_second),
            )
            await_bytes(block, self.recv2.at[way, step - 1, place])
            if step < count:
                self.to_second(block, way, step, place)


def kernel(
    tokens,
    qkv,
    out_weight,
    kind_hbm,
    out,
    wbuf,
    obuf,
    tbuf,
    msg,
    fin,
    rmsg,
    rfin,
    cbuf,
    mbuf,
    sbuf,
    qkv_sum,
    total,
    by_peer,
    by_frame,
    bias,
    kind,
    cross,
    own_sem,
    z_send,
    z_recv,
    w_send,
    w_recv1,
    w_recv2,
    o_send,
    o_recv1,
    o_recv2,
    t_send,
    t_recv,
    s_send,
    s_recv,
    a_send,
    a_recv,
    m_send,
    m_recv,
    n_send,
    n_recv,
    f_send,
    f_recv,
):
    frame = lax.axis_index("frame")
    band = lax.axis_index("band")
    y, z = lax.div(frame, NZ), lax.rem(frame, NZ)
    x, core = lax.div(band, 2), lax.rem(band, 2)
    across = z + (y - z) * core
    along = y + (z - y) * core
    pair, odd = lax.div(across, 2), lax.rem(across, 2)
    other = 1 - odd
    sign = 1 - 2 * core
    sibling_band = 2 * x + 1 - core
    sibling = (frame, sibling_band)
    sibling_odd = lax.rem(y + (z - y) * core, 2)
    me = along * PAIRS + pair

    def frame_at(along_there, across_there):
        return along_there * (NZ - (NZ - 1) * core) + across_there * (1 + (NZ - 1) * core)

    beside = frame_at(along, 2 * pair + other)

    def band_at(step):
        return 2 * wrap(x + step, NX) + core

    def peer(index):
        return (frame_at(lax.div(index, PAIRS), 2 * lax.rem(index, PAIRS) + odd), band)

    barrier = pltpu.get_barrier_semaphore()

    def greet(device):
        pl.semaphore_signal(barrier, inc=1, device_id=device, device_id_type=MESH)

    greet(sibling)
    greet((beside, sibling_band))
    for step in range(1, NY):
        greet((y * NZ + wrap(z + step, NZ), band))
        greet((wrap(y + step, NY) * NZ + z, band))
    for step in (1, -1):
        greet((frame_at(wrap(along + step, NY), 2 * pair + other), band))
    for step in range(1, NX):
        greet((frame, band_at(step)))

    def head_columns(which):
        return qkv.at[:, :, pl.ds(pl.multiple_of(which * HEAD, HEAD), HEAD)]

    own = [
        pltpu.make_async_copy(head_columns(odd), wbuf.at[:, along, pair, odd], own_sem.at[0]),
        pltpu.make_async_copy(out_weight.at[0:16], obuf.at[0, y, z], own_sem.at[1]),
        pltpu.make_async_copy(out_weight.at[16:32], obuf.at[1, z, y], own_sem.at[2]),
        pltpu.make_async_copy(tokens, tbuf.at[odd, band], own_sem.at[3]),
        pltpu.make_async_copy(kind_hbm, kind, own_sem.at[4]),
        pltpu.make_async_copy(head_columns(other), cross, own_sem.at[5]),
    ]
    for copy in own:
        copy.start()
    pl.semaphore_wait(barrier, 2 + NY - 1 + NZ - 1 + 2 + NX - 1)

    for copy in own:
        copy.wait()

    grid = Grid(
        lambda first, second: wbuf.at[:, second, first],
        lambda first, second: (frame_at(second, 2 * first + odd), band),
        (pair, along),
        (PAIRS, NY),
        sign,
        (w_send, w_recv1, w_recv2),
    )

    def token_along_x(which, block):
        for step in (1, NX - 1):
            remote(
                block, block, t_send.at[which, step], t_recv.at[which, step], (frame, band_at(step))
            ).start()

    def token_passed_on(which, by):
        if which == 0:
            block = tbuf.at[odd, band_at(-by)]
        else:
            block = tbuf.at[other, 2 * wrap(x - by, NX) + which - 1]
        remote(
            block, block, t_send.at[which, 2], t_recv.at[which, 2], (frame, band_at(by))
        ).start()

    def token_to_sibling(hop):
        from_band = band_at(-hop)
        remote(
            tbuf.at[odd, from_band],
            tbuf.at[sibling_odd, from_band],
            s_send.at[hop],
            s_recv.at[hop],
            sibling,
        ).start()

    here = wbuf.at[:, along, pair, odd]
    grid.begin(here, here, grid.device)
    grid.begin(
        cross, here, lambda first, second: (frame_at(second, 2 * first + other), band)
    )
    remote(cross, here, z_send.at[0], z_recv.at[0], (beside, band)).start()
    beside_z = y * NZ + z + 1 - 2 * lax.rem(z, 2)
    beside_y = (y + 1 - 2 * lax.rem(y, 2)) * NZ + z
    remote(
        tokens, tbuf.at[lax.rem(z, 2), band], z_send.at[1], z_recv.at[1 + core], (beside_z, 2 * x)
    ).start()
    remote(
        tokens, tbuf.at[lax.rem(y, 2), band], z_send.at[2], z_recv.at[1 + core], (beside_y, 2 * x + 1)
    ).start()
    token_along_x(0, tbuf.at[odd, band])
    remote(
        tbuf.at[odd, band], tbuf.at[sibling_odd, band], s_send.at[0], s_recv.at[0], sibling
    ).start()

    for which in range(2):
        await_bytes(tbuf.at[other, 2 * x + which], z_recv.at[1 + which])
        token_along_x(1 + which, tbuf.at[other, 2 * x + which])

    def out_here(half):
        return (z, y) if half == 0 else (y, z)

    def out_device(half, first, second):
        return (second * NZ + first if half == 0 else first * NZ + second, band)

    def turn(way):
        return sign if way == 0 else -sign

    def out_send2(half, way, step, chunk):
        first, second = out_here(half)
        there = wrap(second + turn(way), NY)
        remote(
            chunk,
            chunk,
            o_send.at[half, 1, way],
            o_recv2.at[half, way, step],
            out_device(half, first, there),
        ).start()

    def out_along_first():
        for half in range(2):
            first, second = out_here(half)
            block = obuf.at[half, second, first]
            for step in range(1, NY):
                remote(
                    block,
                    block,
                    o_send.at[half, 0, 0],
                    o_recv1.at[half],
                    out_device(half, wrap(first + step, NY), second),
                ).start()

    def out_along_second(step):
        for half in range(2):
            first, second = out_here(half)
            for way in range(2):
                if step > hops(NY)[way]:
                    continue
                chunk = obuf.at[half, wrap(second - turn(way) * step, NY)]
                if step:
                    await_bytes(chunk, o_recv2.at[half, way, step - 1])
                if step < hops(NY)[way]:
                    out_send2(half, way, step, chunk)

    for place in range(1, PAIRS):
        grid.along_first(place)

    def ring_step(step):
        def one(place, carry):
            grid.along_second(step, place)
            return carry

        lax.fori_loop(0, PAIRS, one, 0)

    ring_step(1)
    out_along_first()
    for hop in (1, NX - 1):
        await_bytes(tbuf.at[odd, band_at(-hop)], t_recv.at[0, hop])
    token_passed_on(0, sign)
    token_to_sibling(1)
    token_to_sibling(NX - 1)
    ring_step(2)
    for which, by in ((1, 1), (2, -1)):
        for hop in (1, NX - 1):
            await_bytes(
                tbuf.at[other, 2 * wrap(x - hop, NX) + which - 1], t_recv.at[which, hop]
            )
        token_passed_on(which, by)
    await_bytes(tbuf.at[odd, band_at(2)], t_recv.at[0, 2])
    token_to_sibling(2)
    ring_step(3)

    tall = lax.broadcasted_iota(jnp.int32, (ROWS, ROWS), 0)
    wide = lax.broadcasted_iota(jnp.int32, (ROWS, ROWS), 1)

    def origin(row):
        return (
            lax.rem(lax.div(row, SHARE), 2) * POSITIONS
            + lax.div(row, 2 * SHARE) * SHARE
            + lax.rem(row, SHARE)
        )

    qkv_sum[...] = jnp.zeros_like(qkv_sum)
    by_peer[...] = jnp.where(wide == origin(tall), 1.0, 0.0).astype(jnp.bfloat16)
    by_frame[...] = jnp.where(tall == origin(wide), 1.0, 0.0).astype(jnp.bfloat16)
    bias[...] = jnp.where(lax.rem(tall, SHARE) == lax.rem(wide, SHARE), 0.0, -1e30)

    for hop in range(NX):
        from_band = 2 * wrap(x - hop, NX) + 1 - core
        await_bytes(tbuf.at[odd, from_band], s_recv.at[hop])
        if hop == 2:
            for which in range(2):
                await_bytes(
                    tbuf.at[other, 2 * wrap(x - hop, NX) + which], t_recv.at[1 + which, hop]
                )
    ring_step(4)
    await_bytes(wbuf.at[:, along, pair, other], z_recv.at[0])
    for half in range(2):
        await_bytes(obuf.at[half, out_here(half)[1], 0 : NY - 1], o_recv1.at[half])
    out_along_second(0)

    chunk = 2 * NZ * DEPTH

    def project(step, right):
        at = pl.ds(pl.multiple_of(step * chunk, HEAD), chunk)
        qkv_sum[...] += jnp.dot(
            tbuf[:, :, :, at].reshape(ROWS, chunk),
            jnp.concatenate([right(slot) for slot in range(3)], axis=1),
            preferred_element_type=jnp.float32,
        )

    @pl.when(core == 0)
    def _():
        def one(step, carry):
            project(step, lambda slot: wbuf[slot, pl.ds(2 * step, 2)].reshape(chunk, HEAD))
            return carry

        lax.fori_loop(0, NY // 2, one, 0)

    @pl.when(core == 1)
    def _():
        def one(step, carry):
            project(
                step,
                lambda slot: jnp.concatenate(
                    [
                        wbuf[slot, :, step, parity].reshape(chunk // 2, HEAD)
                        for parity in range(2)
                    ],
                    axis=0,
                ),
            )
            return carry

        lax.fori_loop(0, NY // 2, one, 0)

    rounded = qkv_sum[...].astype(jnp.bfloat16)

    msg[...] = (
        jnp.dot(by_peer[...], rounded, preferred_element_type=jnp.float32)
        .reshape(msg.shape)
        .astype(jnp.bfloat16)
    )

    def exchange(stage, source, target):
        def send(step, carry):
            there = lax.rem(me + step, PEERS)
            remote(
                source.at[there], target.at[me], a_send.at[stage], a_recv.at[stage], peer(there)
            ).start()
            return carry

        pltpu.make_async_copy(source.at[me], target.at[me], a_recv.at[stage]).start()
        lax.fori_loop(1, PEERS, send, 0)

    exchange(0, msg, fin)
    spatial = jnp.concatenate(
        [
            attend(
                rounded[at : at + POSITIONS, :HEAD],
                rounded[at : at + POSITIONS, HEAD : 2 * HEAD],
                rounded[at : at + POSITIONS, 2 * HEAD :],
                None,
            )
            for at in (0, POSITIONS)
        ],
        axis=0,
    ).astype(jnp.bfloat16)
    out_along_second(1)

    await_bytes(wbuf.at[:, 0, 0, 0], z_send.at[0])
    await_bytes(tbuf.at[0, 0], z_send.at[1])
    await_bytes(tbuf.at[0, 0], z_send.at[2])
    await_bytes(wbuf.at[:, 0, 0 : PAIRS - 1], w_send.at[0, 0])
    for way in range(2):
        await_bytes(wbuf.at[:, 0 : hops(NY)[way]], w_send.at[1, way])
        await_bytes(obuf.at[way, 0, 0 : NY - 1], o_send.at[way, 0, 0])
    for hop in range(NX):
        await_bytes(tbuf.at[0, 0], s_send.at[hop])
        if hop:
            for which in range(3):
                await_bytes(tbuf.at[0, 0], t_send.at[which, hop])
    await_bytes(fin, a_recv.at[0])
    out_along_second(2)
    laid = fin[...].reshape(ROWS, 3 * HEAD)
    mixed = attend(laid[:, :HEAD], laid[:, HEAD : 2 * HEAD], laid[:, 2 * HEAD :], bias[...])
    rmsg[...] = mixed.reshape(rmsg.shape).astype(jnp.bfloat16)
    exchange(1, rmsg, rfin)
    await_bytes(msg.at[0 : PEERS - 1], a_send.at[0])
    await_bytes(rfin, a_recv.at[1])
    out_along_second(3)
    back = jnp.dot(
        by_frame[...], rfin[...].reshape(ROWS, HEAD), preferred_element_type=jnp.float32
    ).astype(jnp.bfloat16)
    temporal = jnp.full((ROWS, HEAD), kind[odd], jnp.int32) == 1
    cbuf[...] = jnp.where(temporal, back, spatial).reshape(cbuf.shape)

    for step in (1, NX - 1, 2):
        remote(
            cbuf.at[odd],
            mbuf.at[band, odd],
            m_send.at[0, step],
            m_recv.at[0, step],
            (frame, band_at(step)),
        ).start()
    for step in (1, NX - 1, 2, 0):
        remote(
            cbuf.at[other],
            mbuf.at[band, odd],
            m_send.at[1, step],
            m_recv.at[1, step],
            (beside, band_at(step)),
        ).start()
    remote(
        cbuf.at[odd], mbuf.at[band, odd], n_send.at[0, 0], n_recv.at[0, 0], sibling
    ).start()
    last = pltpu.make_async_copy(cbuf.at[odd], mbuf.at[band, odd], m_recv.at[0, 0])
    last.start()
    for which, hop in ((1, 0), (0, 1), (0, 3), (1, 1), (1, 3), (0, 2), (1, 2)):
        block = mbuf.at[band_at(-hop), odd if which == 0 else other]
        await_bytes(block, m_recv.at[which, hop])
        remote(block, block, n_send.at[which, hop], n_recv.at[which, hop], sibling).start()
    out_along_second(4)
    last.wait()

    def project_out(source):
        left = jnp.concatenate([mbuf[source, 0], mbuf[source, 1]], axis=1)
        right = jnp.stack([obuf[0, source], obuf[1, :, source]], axis=1).reshape(
            2 * HEAD, WIDTH
        )
        return jnp.dot(left, right, preferred_element_type=jnp.float32)

    def own_core(hop, carry):
        total[...] += project_out(band_at(-hop))
        return carry

    def other_core(hop, carry):
        source = 2 * wrap(x - hop, NX) + 1 - core
        for which in range(2):
            await_bytes(
                mbuf.at[source, sibling_odd if which == 0 else 1 - sibling_odd],
                n_recv.at[which, hop],
            )
        total[...] += project_out(source)
        return carry

    total[...] = jnp.zeros_like(total)
    lax.fori_loop(0, NX, own_core, 0)
    lax.fori_loop(0, NX, other_core, 0)
    sbuf[...] = total[...].astype(jnp.bfloat16).reshape(sbuf.shape)

    def columns(which):
        return out.at[:, pl.ds(pl.multiple_of(which * WIDTH, HEAD), WIDTH)]

    for step in range(1, BANDS):
        there = wrap(band + step, BANDS)
        remote(
            sbuf.at[there], columns(band), f_send.at[step], f_recv.at[step], (frame, there)
        ).start()
    last = pltpu.make_async_copy(sbuf.at[band], columns(band), f_send.at[0])
    last.start()
    for step in range(1, BANDS):
        await_bytes(columns(wrap(band - step, BANDS)), f_recv.at[step])
    last.wait()

    await_bytes(rmsg.at[0 : PEERS - 1], a_send.at[1])
    for which in range(2):
        for hop in range(NX):
            if hop or which:
                await_bytes(cbuf.at[0], m_send.at[which, hop])
            await_bytes(cbuf.at[0], n_send.at[which, hop])
    for half in range(2):
        for way in range(2):
            await_bytes(obuf.at[half, 0 : hops(NY)[way]], o_send.at[half, 1, way])
    for step in range(1, BANDS):
        await_bytes(sbuf.at[0], f_send.at[step])


def body(tokens, qkv_weight, out_weight, head_kind):
    bf16 = jnp.bfloat16
    dma = pltpu.SemaphoreType.DMA
    hbm = pl.BlockSpec(memory_space=pltpu.HBM)
    return pl.pallas_call(
        kernel,
        out_shape=jax.ShapeDtypeStruct(tokens.shape, tokens.dtype),
        in_specs=[hbm] * 4,
        out_specs=hbm,
        scratch_shapes=[
            pltpu.VMEM((3, NY, PAIRS, 2, DEPTH, HEAD), bf16),
            pltpu.VMEM((2, 8, 8, 16, WIDTH), bf16),
            pltpu.VMEM((2, BANDS) + tokens.shape, bf16),
            pltpu.VMEM((PEERS, 2 * SHARE, 3 * HEAD), bf16),
            pltpu.VMEM((PEERS, 2 * SHARE, 3 * HEAD), bf16),
            pltpu.VMEM((PEERS, 2 * SHARE, HEAD), bf16),
            pltpu.VMEM((PEERS, 2 * SHARE, HEAD), bf16),
            pltpu.VMEM((2, POSITIONS, HEAD), bf16),
            pltpu.VMEM((BANDS, 2, POSITIONS, HEAD), bf16),
            pltpu.VMEM((BANDS, 16, WIDTH), bf16),
            pltpu.VMEM((ROWS, 3 * HEAD), jnp.float32),
            pltpu.VMEM((POSITIONS, WIDTH), jnp.float32),
            pltpu.VMEM((ROWS, ROWS), bf16),
            pltpu.VMEM((ROWS, ROWS), bf16),
            pltpu.VMEM((ROWS, ROWS), jnp.float32),
            pltpu.SMEM((2,), jnp.int32),
            pltpu.VMEM((3, DEPTH, HEAD), bf16),
            dma((6,)),
            dma((3,)),
            dma((3,)),
            dma((2, 2)),
            dma((4,)),
            dma((2, 4, 4)),
            dma((2, 2, 2)),
            dma((2,)),
            dma((2, 2, 4)),
            dma((3, NX)),
            dma((3, NX)),
            dma((NX,)),
            dma((NX,)),
            dma((2,)),
            dma((2,)),
            dma((2, NX)),
            dma((2, NX)),
            dma((2, NX)),
            dma((2, NX)),
            dma((BANDS,)),
            dma((BANDS,)),
        ],
        compiler_params=pltpu.CompilerParams(
            collective_id=0, has_side_effects=True, vmem_limit_bytes=64 * 1024 * 1024
        ),
    )(tokens, qkv_weight.transpose(1, 0, 2), out_weight, head_kind)


def solution(mesh):
    return jax.shard_map(
        body,
        mesh=mesh,
        in_specs=(
            P(("frame", "band"), None),
            P("frame", None, "band"),
            P("frame", "band"),
            P("band"),
        ),
        out_specs=P(("frame", "band"), None),
        check_vma=False,
    )
```

```python
import jax
import jax.numpy as jnp
from jax import lax
from jax.experimental import pallas as pl
from jax.experimental.pallas import tpu as pltpu
from jax.sharding import PartitionSpec as P

MESH = pl.DeviceIdType.MESH
NX = 4
NY = 8
NZ = 8
PAIRS = NZ // 2
BANDS = 2 * NX
PEERS = NY * PAIRS
HEAD = 128
POSITIONS = 128
ROWS = 2 * POSITIONS
SHARE = POSITIONS // PEERS
DEPTH = 48
WIDTH = 384


def remote(src, dst, send_sem, recv_sem, device):
    return pltpu.make_async_remote_copy(
        src_ref=src,
        dst_ref=dst,
        send_sem=send_sem,
        recv_sem=recv_sem,
        device_id=device,
        device_id_type=MESH,
    )


def await_bytes(ref, sem):
    pltpu.make_async_copy(ref, ref, sem).wait()


def attend(queries, keys, values, bias):
    scores = lax.dot_general(
        queries, keys, (((1,), (1,)), ((), ())), preferred_element_type=jnp.float32
    ) * (HEAD**-0.5)
    if bias is not None:
        scores = scores + bias
    raised = jnp.exp(scores - jnp.max(scores, axis=-1, keepdims=True))
    probs = (raised / jnp.sum(raised, axis=-1, keepdims=True)).astype(jnp.bfloat16)
    return jnp.dot(probs, values, preferred_element_type=jnp.float32)


def wrap(value, size):
    return lax.rem(value + 8 * size, size)


def hops(size):
    return (size // 2, (size - 1) // 2)


def wander(place):
    if isinstance(place, int):
        return (place + 1) // 2 * (2 * (place % 2) - 1)
    return lax.div(place + 1, 2) * (2 * lax.rem(place, 2) - 1)


class Grid:
    def __init__(self, block, device, here, sizes, sign, sems):
        self.block = block
        self.device = device
        self.first, self.second = here
        self.n_first, self.n_second = sizes
        self.sign = sign
        self.send, self.recv1, self.recv2 = sems

    def turn(self, way, place):
        flip = 1 - 2 * (place // 2 if isinstance(place, int) else lax.div(place, 2))
        return (self.sign if way == 0 else -self.sign) * flip

    def to_second(self, block, way, step, place, by=1):
        there = wrap(self.second + by * self.turn(way, place), self.n_second)
        remote(
            block,
            block,
            self.send.at[1, way],
            self.recv2.at[way, step, place],
            self.device(self.first, there),
        ).start()

    def begin(self, src, dst, device):
        for way in range(2):
            there = wrap(self.second + self.turn(way, 0), self.n_second)
            remote(
                src,
                dst,
                self.send.at[1, way],
                self.recv2.at[way, 0, 0],
                device(self.first, there),
            ).start()
        for place in range(1, self.n_first):
            there = wrap(self.first + self.sign * wander(place), self.n_first)
            remote(
                src,
                dst,
                self.send.at[0, 0],
                self.recv1.at[place],
                device(there, self.second),
            ).start()

    def along_first(self, place):
        block = self.block(
            wrap(self.first - self.sign * wander(place), self.n_first), self.second
        )
        await_bytes(block, self.recv1.at[place])
        for way in range(2):
            self.to_second(block, way, 0, place)

    def along_second(self, step, place):
        for way in range(2):
            if step > hops(self.n_second)[way]:
                continue
            block = self.block(
                wrap(self.first - self.sign * wander(place), self.n_first),
                wrap(self.second - self.turn(way, place) * step, self.n_second),
            )
            await_bytes(block, self.recv2.at[way, step - 1, place])
            if step < 3:
                self.to_second(block, way, step, place)
            if step == 2 and way == 0:
                self.to_second(block, way, 3, place, 2)


def kernel(
    tokens,
    qkv,
    out_weight,
    kind_hbm,
    out,
    wbuf,
    obuf,
    tbuf,
    msg,
    fin,
    rmsg,
    rfin,
    cbuf,
    mbuf,
    sbuf,
    qkv_sum,
    total,
    by_peer,
    by_frame,
    bias,
    kind,
    cross,
    own_sem,
    z_send,
    z_recv,
    w_send,
    w_recv1,
    w_recv2,
    o_send,
    o_recv1,
    o_recv2,
    t_send,
    t_recv,
    s_send,
    s_recv,
    a_send,
    a_recv,
    m_send,
    m_recv,
    n_send,
    n_recv,
    f_send,
    f_recv,
):
    frame = lax.axis_index("frame")
    band = lax.axis_index("band")
    y, z = lax.div(frame, NZ), lax.rem(frame, NZ)
    x, core = lax.div(band, 2), lax.rem(band, 2)
    across = z + (y - z) * core
    along = y + (z - y) * core
    pair, odd = lax.div(across, 2), lax.rem(across, 2)
    other = 1 - odd
    sign = 1 - 2 * core
    sibling_band = 2 * x + 1 - core
    sibling = (frame, sibling_band)
    sibling_odd = lax.rem(y + (z - y) * core, 2)
    me = along * PAIRS + pair

    def frame_at(along_there, across_there):
        return along_there * (NZ - (NZ - 1) * core) + across_there * (1 + (NZ - 1) * core)

    beside = frame_at(along, 2 * pair + other)

    def band_at(step):
        return 2 * wrap(x + step, NX) + core

    def peer(index):
        return (frame_at(lax.div(index, PAIRS), 2 * lax.rem(index, PAIRS) + odd), band)

    barrier = pltpu.get_barrier_semaphore()

    def greet(device):
        pl.semaphore_signal(barrier, inc=1, device_id=device, device_id_type=MESH)

    greet(sibling)
    greet((beside, sibling_band))
    for step in range(1, NY):
        greet((y * NZ + wrap(z + step, NZ), band))
        greet((wrap(y + step, NY) * NZ + z, band))
    for step in (1, -1):
        greet((frame_at(wrap(along + step, NY), 2 * pair + other), band))
    for step in range(1, NX):
        greet((frame, band_at(step)))

    def head_columns(which):
        return qkv.at[:, :, pl.ds(pl.multiple_of(which * HEAD, HEAD), HEAD)]

    own = [
        pltpu.make_async_copy(head_columns(odd), wbuf.at[:, along, pair, odd], own_sem.at[0]),
        pltpu.make_async_copy(out_weight.at[0:16], obuf.at[0, y, z], own_sem.at[1]),
        pltpu.make_async_copy(out_weight.at[16:32], obuf.at[1, z, y], own_sem.at[2]),
        pltpu.make_async_copy(tokens, tbuf.at[odd, band], own_sem.at[3]),
        pltpu.make_async_copy(kind_hbm, kind, own_sem.at[4]),
        pltpu.make_async_copy(head_columns(other), cross, own_sem.at[5]),
    ]
    for copy in own:
        copy.start()
    pl.semaphore_wait(barrier, 2 + NY - 1 + NZ - 1 + 2 + NX - 1)

    for copy in own:
        copy.wait()

    grid = Grid(
        lambda first, second: wbuf.at[:, second, first],
        lambda first, second: (frame_at(second, 2 * first + odd), band),
        (pair, along),
        (PAIRS, NY),
        sign,
        (w_send, w_recv1, w_recv2),
    )

    def token_along_x(which, block):
        for step in (1, NX - 1):
            remote(
                block, block, t_send.at[which, step], t_recv.at[which, step], (frame, band_at(step))
            ).start()

    def token_passed_on(which, by):
        if which == 0:
            block = tbuf.at[odd, band_at(-by)]
        else:
            block = tbuf.at[other, 2 * wrap(x - by, NX) + which - 1]
        remote(
            block, block, t_send.at[which, 2], t_recv.at[which, 2], (frame, band_at(by))
        ).start()

    def token_to_sibling(hop):
        from_band = band_at(-hop)
        remote(
            tbuf.at[odd, from_band],
            tbuf.at[sibling_odd, from_band],
            s_send.at[hop],
            s_recv.at[hop],
            sibling,
        ).start()

    here = wbuf.at[:, along, pair, odd]
    grid.begin(here, here, grid.device)
    grid.begin(
        cross, here, lambda first, second: (frame_at(second, 2 * first + other), band)
    )
    remote(cross, here, z_send.at[0], z_recv.at[0], (beside, band)).start()
    beside_z = y * NZ + z + 1 - 2 * lax.rem(z, 2)
    beside_y = (y + 1 - 2 * lax.rem(y, 2)) * NZ + z
    remote(
        tokens, tbuf.at[lax.rem(z, 2), band], z_send.at[1], z_recv.at[1 + core], (beside_z, 2 * x)
    ).start()
    remote(
        tokens, tbuf.at[lax.rem(y, 2), band], z_send.at[2], z_recv.at[1 + core], (beside_y, 2 * x + 1)
    ).start()
    token_along_x(0, tbuf.at[odd, band])
    remote(
        tbuf.at[odd, band], tbuf.at[sibling_odd, band], s_send.at[0], s_recv.at[0], sibling
    ).start()

    tall = lax.broadcasted_iota(jnp.int32, (ROWS, ROWS), 0)
    wide = lax.broadcasted_iota(jnp.int32, (ROWS, ROWS), 1)

    def origin(row):
        return (
            lax.rem(lax.div(row, SHARE), 2) * POSITIONS
            + lax.div(row, 2 * SHARE) * SHARE
            + lax.rem(row, SHARE)
        )

    qkv_sum[...] = jnp.zeros_like(qkv_sum)
    by_peer[...] = jnp.where(wide == origin(tall), 1.0, 0.0).astype(jnp.bfloat16)
    by_frame[...] = jnp.where(tall == origin(wide), 1.0, 0.0).astype(jnp.bfloat16)
    bias[...] = jnp.where(lax.rem(tall, SHARE) == lax.rem(wide, SHARE), 0.0, -1e30)

    for which in range(2):
        await_bytes(tbuf.at[other, 2 * x + which], z_recv.at[1 + which])
        token_along_x(1 + which, tbuf.at[other, 2 * x + which])

    def out_here(half):
        return (z, y) if half == 0 else (y, z)

    def out_device(half, first, second):
        return (second * NZ + first if half == 0 else first * NZ + second, band)

    def turn(way):
        return sign if way == 0 else -sign

    def out_send2(half, way, step, chunk):
        first, second = out_here(half)
        there = wrap(second + turn(way), NY)
        remote(
            chunk,
            chunk,
            o_send.at[half, 1, way],
            o_recv2.at[half, way, step],
            out_device(half, first, there),
        ).start()

    def out_along_first():
        for half in range(2):
            first, second = out_here(half)
            block = obuf.at[half, second, first]
            for step in range(1, NY):
                remote(
                    block,
                    block,
                    o_send.at[half, 0, 0],
                    o_recv1.at[half],
                    out_device(half, wrap(first + step, NY), second),
                ).start()

    def out_along_second(step):
        for half in range(2):
            first, second = out_here(half)
            for way in range(2):
                if step > hops(NY)[way]:
                    continue
                chunk = obuf.at[half, wrap(second - turn(way) * step, NY)]
                if step:
                    await_bytes(chunk, o_recv2.at[half, way, step - 1])
                if step < hops(NY)[way]:
                    out_send2(half, way, step, chunk)

    out_along_first()
    for place in range(1, PAIRS):
        grid.along_first(place)

    def ring_step(step):
        def one(place, carry):
            grid.along_second(step, place)
            return carry

        lax.fori_loop(0, PAIRS, one, 0)

    ring_step(1)
    for hop in (1, NX - 1):
        await_bytes(tbuf.at[odd, band_at(-hop)], t_recv.at[0, hop])
    token_passed_on(0, sign)
    token_to_sibling(1)
    token_to_sibling(NX - 1)
    ring_step(2)
    for which, by in ((1, 1), (2, -1)):
        for hop in (1, NX - 1):
            await_bytes(
                tbuf.at[other, 2 * wrap(x - hop, NX) + which - 1], t_recv.at[which, hop]
            )
        token_passed_on(which, by)
    for half in range(2):
        await_bytes(obuf.at[half, out_here(half)[1], 0 : NY - 1], o_recv1.at[half])
    out_along_second(0)
    await_bytes(tbuf.at[odd, band_at(2)], t_recv.at[0, 2])
    token_to_sibling(2)
    ring_step(3)
    for hop in range(NX):
        from_band = 2 * wrap(x - hop, NX) + 1 - core
        await_bytes(tbuf.at[odd, from_band], s_recv.at[hop])
        if hop == 2:
            for which in range(2):
                await_bytes(
                    tbuf.at[other, 2 * wrap(x - hop, NX) + which], t_recv.at[1 + which, hop]
                )
    ring_step(4)
    await_bytes(wbuf.at[:, along, pair, other], z_recv.at[0])
    out_along_second(1)

    chunk = 2 * NZ * DEPTH

    def project(step, right):
        at = pl.ds(pl.multiple_of(step * chunk, HEAD), chunk)
        qkv_sum[...] += jnp.dot(
            tbuf[:, :, :, at].reshape(ROWS, chunk),
            jnp.concatenate([right(slot) for slot in range(3)], axis=1),
            preferred_element_type=jnp.float32,
        )

    @pl.when(core == 0)
    def _():
        def one(step, carry):
            project(step, lambda slot: wbuf[slot, pl.ds(2 * step, 2)].reshape(chunk, HEAD))
            return carry

        lax.fori_loop(0, NY // 2, one, 0)

    @pl.when(core == 1)
    def _():
        def one(step, carry):
            project(
                step,
                lambda slot: jnp.concatenate(
                    [
                        wbuf[slot, :, step, parity].reshape(chunk // 2, HEAD)
                        for parity in range(2)
                    ],
                    axis=0,
                ),
            )
            return carry

        lax.fori_loop(0, NY // 2, one, 0)

    rounded = qkv_sum[...].astype(jnp.bfloat16)

    msg[...] = (
        jnp.dot(by_peer[...], rounded, preferred_element_type=jnp.float32)
        .reshape(msg.shape)
        .astype(jnp.bfloat16)
    )

    def exchange(stage, source, target):
        def send(step, carry):
            there = lax.rem(me + PEERS // 2 + wander(step) + PEERS, PEERS)
            remote(
                source.at[there], target.at[me], a_send.at[stage], a_recv.at[stage], peer(there)
            ).start()
            return carry

        pltpu.make_async_copy(source.at[me], target.at[me], a_recv.at[stage]).start()
        lax.fori_loop(0, PEERS - 1, send, 0)

    exchange(0, msg, fin)
    spatial = jnp.concatenate(
        [
            attend(
                rounded[at : at + POSITIONS, :HEAD],
                rounded[at : at + POSITIONS, HEAD : 2 * HEAD],
                rounded[at : at + POSITIONS, 2 * HEAD :],
                None,
            )
            for at in (0, POSITIONS)
        ],
        axis=0,
    ).astype(jnp.bfloat16)
    out_along_second(2)

    await_bytes(wbuf.at[:, 0, 0, 0], z_send.at[0])
    await_bytes(tbuf.at[0, 0], z_send.at[1])
    await_bytes(tbuf.at[0, 0], z_send.at[2])
    await_bytes(wbuf.at[:, 0, 0 : PAIRS - 1], w_send.at[0, 0])
    for way in range(2):
        await_bytes(wbuf.at[:, 0 : hops(NY)[way]], w_send.at[1, way])
        await_bytes(obuf.at[way, 0, 0 : NY - 1], o_send.at[way, 0, 0])
    for hop in range(NX):
        await_bytes(tbuf.at[0, 0], s_send.at[hop])
        if hop:
            for which in range(3):
                await_bytes(tbuf.at[0, 0], t_send.at[which, hop])
    await_bytes(fin, a_recv.at[0])
    laid = fin[...].reshape(ROWS, 3 * HEAD)
    mixed = attend(laid[:, :HEAD], laid[:, HEAD : 2 * HEAD], laid[:, 2 * HEAD :], bias[...])
    rmsg[...] = mixed.reshape(rmsg.shape).astype(jnp.bfloat16)
    exchange(1, rmsg, rfin)
    out_along_second(3)
    await_bytes(msg.at[0 : PEERS - 1], a_send.at[0])
    await_bytes(rfin, a_recv.at[1])
    back = jnp.dot(
        by_frame[...], rfin[...].reshape(ROWS, HEAD), preferred_element_type=jnp.float32
    ).astype(jnp.bfloat16)
    temporal = jnp.full((ROWS, HEAD), kind[odd], jnp.int32) == 1
    cbuf[...] = jnp.where(temporal, back, spatial).reshape(cbuf.shape)

    for which, step in ((1, 2), (1, 1), (1, NX - 1), (0, 2), (1, 0), (0, 1), (0, NX - 1)):
        remote(
            cbuf.at[odd if which == 0 else other],
            mbuf.at[band, odd],
            m_send.at[which, step],
            m_recv.at[which, step],
            (frame if which == 0 else beside, band_at(step)),
        ).start()
    remote(
        cbuf.at[odd], mbuf.at[band, odd], n_send.at[0, 0], n_recv.at[0, 0], sibling
    ).start()
    last = pltpu.make_async_copy(cbuf.at[odd], mbuf.at[band, odd], m_recv.at[0, 0])
    last.start()
    for which, hop in ((1, 0), (0, 1), (0, 3), (1, 1), (1, 3), (0, 2), (1, 2)):
        block = mbuf.at[band_at(-hop), odd if which == 0 else other]
        await_bytes(block, m_recv.at[which, hop])
        remote(block, block, n_send.at[which, hop], n_recv.at[which, hop], sibling).start()
    out_along_second(4)
    last.wait()

    def project_out(source):
        left = jnp.concatenate([mbuf[source, 0], mbuf[source, 1]], axis=1)
        right = jnp.stack([obuf[0, source], obuf[1, :, source]], axis=1).reshape(
            2 * HEAD, WIDTH
        )
        return jnp.dot(left, right, preferred_element_type=jnp.float32)

    def own_core(hop, carry):
        total[...] += project_out(band_at(-hop))
        return carry

    def other_core(hop, carry):
        source = 2 * wrap(x - hop, NX) + 1 - core
        for which in range(2):
            await_bytes(
                mbuf.at[source, sibling_odd if which == 0 else 1 - sibling_odd],
                n_recv.at[which, hop],
            )
        total[...] += project_out(source)
        return carry

    total[...] = jnp.zeros_like(total)
    lax.fori_loop(0, NX, own_core, 0)
    lax.fori_loop(0, NX, other_core, 0)
    sbuf[...] = total[...].astype(jnp.bfloat16).reshape(sbuf.shape)

    def columns(which):
        return out.at[:, pl.ds(pl.multiple_of(which * WIDTH, HEAD), WIDTH)]

    for step in range(1, BANDS):
        there = wrap(band + step, BANDS)
        remote(
            sbuf.at[there], columns(band), f_send.at[step], f_recv.at[step], (frame, there)
        ).start()
    last = pltpu.make_async_copy(sbuf.at[band], columns(band), f_send.at[0])
    last.start()
    for step in range(1, BANDS):
        await_bytes(columns(wrap(band - step, BANDS)), f_recv.at[step])
    last.wait()

    await_bytes(rmsg.at[0 : PEERS - 1], a_send.at[1])
    for which in range(2):
        for hop in range(NX):
            if hop or which:
                await_bytes(cbuf.at[0], m_send.at[which, hop])
            await_bytes(cbuf.at[0], n_send.at[which, hop])
    for half in range(2):
        for way in range(2):
            await_bytes(obuf.at[half, 0 : hops(NY)[way]], o_send.at[half, 1, way])
    for step in range(1, BANDS):
        await_bytes(sbuf.at[0], f_send.at[step])


def body(tokens, qkv_weight, out_weight, head_kind):
    bf16 = jnp.bfloat16
    dma = pltpu.SemaphoreType.DMA
    hbm = pl.BlockSpec(memory_space=pltpu.HBM)
    return pl.pallas_call(
        kernel,
        out_shape=jax.ShapeDtypeStruct(tokens.shape, tokens.dtype),
        in_specs=[hbm] * 4,
        out_specs=hbm,
        scratch_shapes=[
            pltpu.VMEM((3, NY, PAIRS, 2, DEPTH, HEAD), bf16),
            pltpu.VMEM((2, 8, 8, 16, WIDTH), bf16),
            pltpu.VMEM((2, BANDS) + tokens.shape, bf16),
            pltpu.VMEM((PEERS, 2 * SHARE, 3 * HEAD), bf16),
            pltpu.VMEM((PEERS, 2 * SHARE, 3 * HEAD), bf16),
            pltpu.VMEM((PEERS, 2 * SHARE, HEAD), bf16),
            pltpu.VMEM((PEERS, 2 * SHARE, HEAD), bf16),
            pltpu.VMEM((2, POSITIONS, HEAD), bf16),
            pltpu.VMEM((BANDS, 2, POSITIONS, HEAD), bf16),
            pltpu.VMEM((BANDS, 16, WIDTH), bf16),
            pltpu.VMEM((ROWS, 3 * HEAD), jnp.float32),
            pltpu.VMEM((POSITIONS, WIDTH), jnp.float32),
            pltpu.VMEM((ROWS, ROWS), bf16),
            pltpu.VMEM((ROWS, ROWS), bf16),
            pltpu.VMEM((ROWS, ROWS), jnp.float32),
            pltpu.SMEM((2,), jnp.int32),
            pltpu.VMEM((3, DEPTH, HEAD), bf16),
            dma((6,)),
            dma((3,)),
            dma((3,)),
            dma((2, 2)),
            dma((4,)),
            dma((2, 4, 4)),
            dma((2, 2, 2)),
            dma((2,)),
            dma((2, 2, 4)),
            dma((3, NX)),
            dma((3, NX)),
            dma((NX,)),
            dma((NX,)),
            dma((2,)),
            dma((2,)),
            dma((2, NX)),
            dma((2, NX)),
            dma((2, NX)),
            dma((2, NX)),
            dma((BANDS,)),
            dma((BANDS,)),
        ],
        compiler_params=pltpu.CompilerParams(
            collective_id=0, has_side_effects=True, vmem_limit_bytes=64 * 1024 * 1024
        ),
    )(tokens, qkv_weight.transpose(1, 0, 2), out_weight, head_kind)


def solution(mesh):
    return jax.shard_map(
        body,
        mesh=mesh,
        in_specs=(
            P(("frame", "band"), None),
            P("frame", None, "band"),
            P("frame", "band"),
            P("band"),
        ),
        out_specs=P(("frame", "band"), None),
        check_vma=False,
    )
```

```python
import jax
import jax.numpy as jnp
from jax import lax
from jax.experimental import pallas as pl
from jax.experimental.pallas import tpu as pltpu
from jax.sharding import PartitionSpec as P

MESH = pl.DeviceIdType.MESH
NX = 4
NY = 8
NZ = 8
PAIRS = NZ // 2
BANDS = 2 * NX
PEERS = NY * PAIRS
HEAD = 128
POSITIONS = 128
ROWS = 2 * POSITIONS
SHARE = POSITIONS // PEERS
DEPTH = 48
WIDTH = 384


def remote(src, dst, send_sem, recv_sem, device):
    return pltpu.make_async_remote_copy(
        src_ref=src,
        dst_ref=dst,
        send_sem=send_sem,
        recv_sem=recv_sem,
        device_id=device,
        device_id_type=MESH,
    )


def await_bytes(ref, sem):
    pltpu.make_async_copy(ref, ref, sem).wait()


def attend(queries, keys, values, bias):
    scores = lax.dot_general(
        queries, keys, (((1,), (1,)), ((), ())), preferred_element_type=jnp.float32
    ) * (HEAD**-0.5)
    if bias is not None:
        scores = scores + bias
    raised = jnp.exp(scores - jnp.max(scores, axis=-1, keepdims=True))
    probs = (raised / jnp.sum(raised, axis=-1, keepdims=True)).astype(jnp.bfloat16)
    return jnp.dot(probs, values, preferred_element_type=jnp.float32)


def wrap(value, size):
    return lax.rem(value + 8 * size, size)


def hops(size):
    return (size // 2, (size - 1) // 2)


def wander(place):
    if isinstance(place, int):
        return (place + 1) // 2 * (2 * (place % 2) - 1)
    return lax.div(place + 1, 2) * (2 * lax.rem(place, 2) - 1)


class Grid:
    def __init__(self, block, device, here, sizes, sign, sems):
        self.block = block
        self.device = device
        self.first, self.second = here
        self.n_first, self.n_second = sizes
        self.sign = sign
        self.send, self.recv1, self.recv2 = sems

    def turn(self, way, place):
        flip = 1 - 2 * (place // 2 if isinstance(place, int) else lax.div(place, 2))
        return (self.sign if way == 0 else -self.sign) * flip

    def to_second(self, block, way, step, place, by=1):
        there = wrap(self.second + by * self.turn(way, place), self.n_second)
        remote(
            block,
            block,
            self.send.at[1, way],
            self.recv2.at[way, step, place],
            self.device(self.first, there),
        ).start()

    def begin(self, src, dst, device):
        for way in range(2):
            there = wrap(self.second + self.turn(way, 0), self.n_second)
            remote(
                src,
                dst,
                self.send.at[1, way],
                self.recv2.at[way, 0, 0],
                device(self.first, there),
            ).start()
        for place in range(1, self.n_first):
            there = wrap(self.first + self.sign * wander(place), self.n_first)
            remote(
                src,
                dst,
                self.send.at[0, 0],
                self.recv1.at[place],
                device(there, self.second),
            ).start()

    def along_first(self, place):
        block = self.block(
            wrap(self.first - self.sign * wander(place), self.n_first), self.second
        )
        await_bytes(block, self.recv1.at[place])
        for way in range(2):
            self.to_second(block, way, 0, place)

    def along_second(self, step, place):
        for way in range(2):
            if step > hops(self.n_second)[way]:
                continue
            block = self.block(
                wrap(self.first - self.sign * wander(place), self.n_first),
                wrap(self.second - self.turn(way, place) * step, self.n_second),
            )
            await_bytes(block, self.recv2.at[way, step - 1, place])
            if step < 3:
                self.to_second(block, way, step, place)
            if step == 2 and way == 0:
                self.to_second(block, way, 3, place, 2)


def kernel(
    tokens,
    qkv,
    out_weight,
    kind_hbm,
    out,
    wbuf,
    obuf,
    tbuf,
    msg,
    fin,
    rmsg,
    rfin,
    cbuf,
    mbuf,
    sbuf,
    qkv_sum,
    total,
    by_peer,
    by_frame,
    bias,
    kind,
    cross,
    own_sem,
    z_send,
    z_recv,
    w_send,
    w_recv1,
    w_recv2,
    o_send,
    o_recv1,
    o_recv2,
    t_send,
    t_recv,
    s_send,
    s_recv,
    a_send,
    a_recv,
    m_send,
    m_recv,
    n_send,
    n_recv,
    f_send,
    f_recv,
):
    frame = lax.axis_index("frame")
    band = lax.axis_index("band")
    y, z = lax.div(frame, NZ), lax.rem(frame, NZ)
    x, core = lax.div(band, 2), lax.rem(band, 2)
    across = z + (y - z) * core
    along = y + (z - y) * core
    pair, odd = lax.div(across, 2), lax.rem(across, 2)
    other = 1 - odd
    sign = 1 - 2 * core
    sibling_band = 2 * x + 1 - core
    sibling = (frame, sibling_band)
    sibling_odd = lax.rem(y + (z - y) * core, 2)
    me = along * PAIRS + pair

    def frame_at(along_there, across_there):
        return along_there * (NZ - (NZ - 1) * core) + across_there * (1 + (NZ - 1) * core)

    beside = frame_at(along, 2 * pair + other)

    def band_at(step):
        return 2 * wrap(x + step, NX) + core

    def peer(index):
        return (frame_at(lax.div(index, PAIRS), 2 * lax.rem(index, PAIRS) + odd), band)

    barrier = pltpu.get_barrier_semaphore()

    def greet(device):
        pl.semaphore_signal(barrier, inc=1, device_id=device, device_id_type=MESH)

    greet(sibling)
    greet((beside, sibling_band))
    for step in range(1, NY):
        greet((y * NZ + wrap(z + step, NZ), band))
        greet((wrap(y + step, NY) * NZ + z, band))
    for step in (1, -1):
        greet((frame_at(wrap(along + step, NY), 2 * pair + other), band))
    for step in range(1, NX):
        greet((frame, band_at(step)))

    def head_columns(which):
        return qkv.at[:, :, pl.ds(pl.multiple_of(which * HEAD, HEAD), HEAD)]

    own = [
        pltpu.make_async_copy(head_columns(odd), wbuf.at[:, along, pair, odd], own_sem.at[0]),
        pltpu.make_async_copy(out_weight.at[0:16], obuf.at[0, y, z], own_sem.at[1]),
        pltpu.make_async_copy(out_weight.at[16:32], obuf.at[1, z, y], own_sem.at[2]),
        pltpu.make_async_copy(tokens, tbuf.at[odd, band], own_sem.at[3]),
        pltpu.make_async_copy(kind_hbm, kind, own_sem.at[4]),
        pltpu.make_async_copy(head_columns(other), cross, own_sem.at[5]),
    ]
    for copy in own:
        copy.start()
    pl.semaphore_wait(barrier, 2 + NY - 1 + NZ - 1 + 2 + NX - 1)

    for copy in own:
        copy.wait()

    grid = Grid(
        lambda first, second: wbuf.at[:, second, first],
        lambda first, second: (frame_at(second, 2 * first + odd), band),
        (pair, along),
        (PAIRS, NY),
        sign,
        (w_send, w_recv1, w_recv2),
    )

    def token_along_x(which, block):
        for step in (1, NX - 1):
            remote(
                block, block, t_send.at[which, step], t_recv.at[which, step], (frame, band_at(step))
            ).start()

    def token_passed_on(which, by):
        if which == 0:
            block = tbuf.at[odd, band_at(-by)]
        else:
            block = tbuf.at[other, 2 * wrap(x - by, NX) + which - 1]
        remote(
            block, block, t_send.at[which, 2], t_recv.at[which, 2], (frame, band_at(by))
        ).start()

    def token_to_sibling(hop):
        from_band = band_at(-hop)
        remote(
            tbuf.at[odd, from_band],
            tbuf.at[sibling_odd, from_band],
            s_send.at[hop],
            s_recv.at[hop],
            sibling,
        ).start()

    here = wbuf.at[:, along, pair, odd]
    grid.begin(here, here, grid.device)
    grid.begin(
        cross, here, lambda first, second: (frame_at(second, 2 * first + other), band)
    )
    remote(cross, here, z_send.at[0], z_recv.at[0], (beside, band)).start()
    beside_z = y * NZ + z + 1 - 2 * lax.rem(z, 2)
    beside_y = (y + 1 - 2 * lax.rem(y, 2)) * NZ + z
    remote(
        tokens, tbuf.at[lax.rem(z, 2), band], z_send.at[1], z_recv.at[1 + core], (beside_z, 2 * x)
    ).start()
    remote(
        tokens, tbuf.at[lax.rem(y, 2), band], z_send.at[2], z_recv.at[1 + core], (beside_y, 2 * x + 1)
    ).start()
    token_along_x(0, tbuf.at[odd, band])
    remote(
        tbuf.at[odd, band], tbuf.at[sibling_odd, band], s_send.at[0], s_recv.at[0], sibling
    ).start()

    tall = lax.broadcasted_iota(jnp.int32, (ROWS, ROWS), 0)
    wide = lax.broadcasted_iota(jnp.int32, (ROWS, ROWS), 1)

    def origin(row):
        return (
            lax.rem(lax.div(row, SHARE), 2) * POSITIONS
            + lax.div(row, 2 * SHARE) * SHARE
            + lax.rem(row, SHARE)
        )

    qkv_sum[...] = jnp.zeros_like(qkv_sum)
    by_peer[...] = jnp.where(wide == origin(tall), 1.0, 0.0).astype(jnp.bfloat16)
    by_frame[...] = jnp.where(tall == origin(wide), 1.0, 0.0).astype(jnp.bfloat16)
    bias[...] = jnp.where(lax.rem(tall, SHARE) == lax.rem(wide, SHARE), 0.0, -1e30)

    for which in range(2):
        await_bytes(tbuf.at[other, 2 * x + which], z_recv.at[1 + which])
        token_along_x(1 + which, tbuf.at[other, 2 * x + which])

    def out_here(half):
        return (z, y) if half == 0 else (y, z)

    def out_device(half, first, second):
        return (second * NZ + first if half == 0 else first * NZ + second, band)

    def turn(way):
        return sign if way == 0 else -sign

    def out_send2(half, way, step, chunk, by=1):
        first, second = out_here(half)
        there = wrap(second + by * turn(way), NY)
        remote(
            chunk,
            chunk,
            o_send.at[half, 1, way],
            o_recv2.at[half, way, step],
            out_device(half, first, there),
        ).start()

    def out_along_first():
        for half in range(2):
            first, second = out_here(half)
            block = obuf.at[half, second, first]
            for step in range(1, NY):
                remote(
                    block,
                    block,
                    o_send.at[half, 0, 0],
                    o_recv1.at[half],
                    out_device(half, wrap(first + step, NY), second),
                ).start()

    def out_along_second(step):
        for half in range(2):
            first, second = out_here(half)
            for way in range(2):
                if step > hops(NY)[way]:
                    continue
                chunk = obuf.at[half, wrap(second - turn(way) * step, NY)]
                if step:
                    await_bytes(chunk, o_recv2.at[half, way, step - 1])
                if step < 3:
                    out_send2(half, way, step, chunk)
                if step == 2 and way == 0:
                    out_send2(half, way, 3, chunk, 2)

    out_along_first()
    for place in range(1, PAIRS):
        grid.along_first(place)

    def ring_step(step):
        def one(place, carry):
            grid.along_second(step, place)
            return carry

        lax.fori_loop(0, PAIRS, one, 0)

    ring_step(1)
    for hop in (1, NX - 1):
        await_bytes(tbuf.at[odd, band_at(-hop)], t_recv.at[0, hop])
    token_passed_on(0, sign)
    token_to_sibling(1)
    token_to_sibling(NX - 1)
    ring_step(2)
    for which, by in ((1, 1), (2, -1)):
        for hop in (1, NX - 1):
            await_bytes(
                tbuf.at[other, 2 * wrap(x - hop, NX) + which - 1], t_recv.at[which, hop]
            )
        token_passed_on(which, by)
    await_bytes(tbuf.at[odd, band_at(2)], t_recv.at[0, 2])
    token_to_sibling(2)
    ring_step(3)
    for hop in range(NX):
        from_band = 2 * wrap(x - hop, NX) + 1 - core
        await_bytes(tbuf.at[odd, from_band], s_recv.at[hop])
        if hop == 2:
            for which in range(2):
                await_bytes(
                    tbuf.at[other, 2 * wrap(x - hop, NX) + which], t_recv.at[1 + which, hop]
                )
    ring_step(4)
    await_bytes(wbuf.at[:, along, pair, other], z_recv.at[0])
    for half in range(2):
        await_bytes(obuf.at[half, out_here(half)[1], 0 : NY - 1], o_recv1.at[half])
    out_along_second(0)

    chunk = 2 * NZ * DEPTH

    def project(step, right):
        at = pl.ds(pl.multiple_of(step * chunk, HEAD), chunk)
        qkv_sum[...] += jnp.dot(
            tbuf[:, :, :, at].reshape(ROWS, chunk),
            jnp.concatenate([right(slot) for slot in range(3)], axis=1),
            preferred_element_type=jnp.float32,
        )

    @pl.when(core == 0)
    def _():
        def one(step, carry):
            project(step, lambda slot: wbuf[slot, pl.ds(2 * step, 2)].reshape(chunk, HEAD))
            return carry

        lax.fori_loop(0, NY // 2, one, 0)

    @pl.when(core == 1)
    def _():
        def one(step, carry):
            project(
                step,
                lambda slot: jnp.concatenate(
                    [
                        wbuf[slot, :, step, parity].reshape(chunk // 2, HEAD)
                        for parity in range(2)
                    ],
                    axis=0,
                ),
            )
            return carry

        lax.fori_loop(0, NY // 2, one, 0)

    rounded = qkv_sum[...].astype(jnp.bfloat16)

    msg[...] = (
        jnp.dot(by_peer[...], rounded, preferred_element_type=jnp.float32)
        .reshape(msg.shape)
        .astype(jnp.bfloat16)
    )

    def exchange(stage, source, target):
        def send(step, carry):
            there = lax.rem(me + PEERS // 2 + wander(step) + PEERS, PEERS)
            remote(
                source.at[there], target.at[me], a_send.at[stage], a_recv.at[stage], peer(there)
            ).start()
            return carry

        pltpu.make_async_copy(source.at[me], target.at[me], a_recv.at[stage]).start()
        lax.fori_loop(0, PEERS - 1, send, 0)

    exchange(0, msg, fin)
    spatial = jnp.concatenate(
        [
            attend(
                rounded[at : at + POSITIONS, :HEAD],
                rounded[at : at + POSITIONS, HEAD : 2 * HEAD],
                rounded[at : at + POSITIONS, 2 * HEAD :],
                None,
            )
            for at in (0, POSITIONS)
        ],
        axis=0,
    ).astype(jnp.bfloat16)
    out_along_second(1)

    await_bytes(wbuf.at[:, 0, 0, 0], z_send.at[0])
    await_bytes(tbuf.at[0, 0], z_send.at[1])
    await_bytes(tbuf.at[0, 0], z_send.at[2])
    await_bytes(wbuf.at[:, 0, 0 : PAIRS - 1], w_send.at[0, 0])
    for way in range(2):
        await_bytes(wbuf.at[:, 0 : hops(NY)[way]], w_send.at[1, way])
        await_bytes(obuf.at[way, 0, 0 : NY - 1], o_send.at[way, 0, 0])
    for hop in range(NX):
        await_bytes(tbuf.at[0, 0], s_send.at[hop])
        if hop:
            for which in range(3):
                await_bytes(tbuf.at[0, 0], t_send.at[which, hop])
    await_bytes(fin, a_recv.at[0])
    laid = fin[...].reshape(ROWS, 3 * HEAD)
    mixed = attend(laid[:, :HEAD], laid[:, HEAD : 2 * HEAD], laid[:, 2 * HEAD :], bias[...])
    rmsg[...] = mixed.reshape(rmsg.shape).astype(jnp.bfloat16)
    exchange(1, rmsg, rfin)
    out_along_second(2)
    await_bytes(msg.at[0 : PEERS - 1], a_send.at[0])
    await_bytes(rfin, a_recv.at[1])
    back = jnp.dot(
        by_frame[...], rfin[...].reshape(ROWS, HEAD), preferred_element_type=jnp.float32
    ).astype(jnp.bfloat16)
    temporal = jnp.full((ROWS, HEAD), kind[odd], jnp.int32) == 1
    cbuf[...] = jnp.where(temporal, back, spatial).reshape(cbuf.shape)

    for which, step in ((1, 2), (1, 1), (1, NX - 1), (0, 2), (1, 0), (0, 1), (0, NX - 1)):
        remote(
            cbuf.at[odd if which == 0 else other],
            mbuf.at[band, odd],
            m_send.at[which, step],
            m_recv.at[which, step],
            (frame if which == 0 else beside, band_at(step)),
        ).start()
    remote(
        cbuf.at[odd], mbuf.at[band, odd], n_send.at[0, 0], n_recv.at[0, 0], sibling
    ).start()
    last = pltpu.make_async_copy(cbuf.at[odd], mbuf.at[band, odd], m_recv.at[0, 0])
    last.start()
    for which, hop in ((1, 0), (0, 1), (0, 3), (1, 1), (1, 3), (0, 2), (1, 2)):
        block = mbuf.at[band_at(-hop), odd if which == 0 else other]
        await_bytes(block, m_recv.at[which, hop])
        remote(block, block, n_send.at[which, hop], n_recv.at[which, hop], sibling).start()
    out_along_second(3)
    out_along_second(4)
    last.wait()

    def project_out(source):
        left = jnp.concatenate([mbuf[source, 0], mbuf[source, 1]], axis=1)
        right = jnp.stack([obuf[0, source], obuf[1, :, source]], axis=1).reshape(
            2 * HEAD, WIDTH
        )
        return jnp.dot(left, right, preferred_element_type=jnp.float32)

    def own_core(hop, carry):
        total[...] += project_out(band_at(-hop))
        return carry

    def other_core(hop, carry):
        source = 2 * wrap(x - hop, NX) + 1 - core
        for which in range(2):
            await_bytes(
                mbuf.at[source, sibling_odd if which == 0 else 1 - sibling_odd],
                n_recv.at[which, hop],
            )
        total[...] += project_out(source)
        return carry

    total[...] = jnp.zeros_like(total)
    lax.fori_loop(0, NX, own_core, 0)
    lax.fori_loop(0, NX, other_core, 0)
    sbuf[...] = total[...].astype(jnp.bfloat16).reshape(sbuf.shape)

    def columns(which):
        return out.at[:, pl.ds(pl.multiple_of(which * WIDTH, HEAD), WIDTH)]

    for step in range(1, BANDS):
        there = wrap(band + step, BANDS)
        remote(
            sbuf.at[there], columns(band), f_send.at[step], f_recv.at[step], (frame, there)
        ).start()
    last = pltpu.make_async_copy(sbuf.at[band], columns(band), f_send.at[0])
    last.start()
    for step in range(1, BANDS):
        await_bytes(columns(wrap(band - step, BANDS)), f_recv.at[step])
    last.wait()

    await_bytes(rmsg.at[0 : PEERS - 1], a_send.at[1])
    for which in range(2):
        for hop in range(NX):
            if hop or which:
                await_bytes(cbuf.at[0], m_send.at[which, hop])
            await_bytes(cbuf.at[0], n_send.at[which, hop])
    for half in range(2):
        for way in range(2):
            await_bytes(obuf.at[half, 0 : hops(NY)[way]], o_send.at[half, 1, way])
    for step in range(1, BANDS):
        await_bytes(sbuf.at[0], f_send.at[step])


def body(tokens, qkv_weight, out_weight, head_kind):
    bf16 = jnp.bfloat16
    dma = pltpu.SemaphoreType.DMA
    hbm = pl.BlockSpec(memory_space=pltpu.HBM)
    return pl.pallas_call(
        kernel,
        out_shape=jax.ShapeDtypeStruct(tokens.shape, tokens.dtype),
        in_specs=[hbm] * 4,
        out_specs=hbm,
        scratch_shapes=[
            pltpu.VMEM((3, NY, PAIRS, 2, DEPTH, HEAD), bf16),
            pltpu.VMEM((2, 8, 8, 16, WIDTH), bf16),
            pltpu.VMEM((2, BANDS) + tokens.shape, bf16),
            pltpu.VMEM((PEERS, 2 * SHARE, 3 * HEAD), bf16),
            pltpu.VMEM((PEERS, 2 * SHARE, 3 * HEAD), bf16),
            pltpu.VMEM((PEERS, 2 * SHARE, HEAD), bf16),
            pltpu.VMEM((PEERS, 2 * SHARE, HEAD), bf16),
            pltpu.VMEM((2, POSITIONS, HEAD), bf16),
            pltpu.VMEM((BANDS, 2, POSITIONS, HEAD), bf16),
            pltpu.VMEM((BANDS, 16, WIDTH), bf16),
            pltpu.VMEM((ROWS, 3 * HEAD), jnp.float32),
            pltpu.VMEM((POSITIONS, WIDTH), jnp.float32),
            pltpu.VMEM((ROWS, ROWS), bf16),
            pltpu.VMEM((ROWS, ROWS), bf16),
            pltpu.VMEM((ROWS, ROWS), jnp.float32),
            pltpu.SMEM((2,), jnp.int32),
            pltpu.VMEM((3, DEPTH, HEAD), bf16),
            dma((6,)),
            dma((3,)),
            dma((3,)),
            dma((2, 2)),
            dma((4,)),
            dma((2, 4, 4)),
            dma((2, 2, 2)),
            dma((2,)),
            dma((2, 2, 4)),
            dma((3, NX)),
            dma((3, NX)),
            dma((NX,)),
            dma((NX,)),
            dma((2,)),
            dma((2,)),
            dma((2, NX)),
            dma((2, NX)),
            dma((2, NX)),
            dma((2, NX)),
            dma((BANDS,)),
            dma((BANDS,)),
        ],
        compiler_params=pltpu.CompilerParams(
            collective_id=0, has_side_effects=True, vmem_limit_bytes=64 * 1024 * 1024
        ),
    )(tokens, qkv_weight.transpose(1, 0, 2), out_weight, head_kind)


def solution(mesh):
    return jax.shard_map(
        body,
        mesh=mesh,
        in_specs=(
            P(("frame", "band"), None),
            P("frame", None, "band"),
            P("frame", "band"),
            P("band"),
        ),
        out_specs=P(("frame", "band"), None),
        check_vma=False,
    )
```

```python
import jax
import jax.numpy as jnp
from jax import lax
from jax.experimental import pallas as pl
from jax.experimental.pallas import tpu as pltpu
from jax.sharding import PartitionSpec as P

MESH = pl.DeviceIdType.MESH
NX = 4
NY = 8
NZ = 8
PAIRS = NZ // 2
BANDS = 2 * NX
PEERS = NY * PAIRS
HEAD = 128
POSITIONS = 128
ROWS = 2 * POSITIONS
SHARE = POSITIONS // PEERS
DEPTH = 48
WIDTH = 384


def remote(src, dst, send_sem, recv_sem, device):
    return pltpu.make_async_remote_copy(
        src_ref=src,
        dst_ref=dst,
        send_sem=send_sem,
        recv_sem=recv_sem,
        device_id=device,
        device_id_type=MESH,
    )


def await_bytes(ref, sem):
    pltpu.make_async_copy(ref, ref, sem).wait()


def attend(queries, keys, values, bias):
    scores = lax.dot_general(
        queries, keys, (((1,), (1,)), ((), ())), preferred_element_type=jnp.float32
    ) * (HEAD**-0.5)
    if bias is not None:
        scores = scores + bias
    raised = jnp.exp(scores - jnp.max(scores, axis=-1, keepdims=True))
    probs = (raised / jnp.sum(raised, axis=-1, keepdims=True)).astype(jnp.bfloat16)
    return jnp.dot(probs, values, preferred_element_type=jnp.float32)


def wrap(value, size):
    return lax.rem(value + 8 * size, size)


def hops(size):
    return (size // 2, (size - 1) // 2)


def wander(place):
    if isinstance(place, int):
        return (place + 1) // 2 * (2 * (place % 2) - 1)
    return lax.div(place + 1, 2) * (2 * lax.rem(place, 2) - 1)


class Grid:
    def __init__(self, block, device, here, sizes, sign, sems):
        self.block = block
        self.device = device
        self.first, self.second = here
        self.n_first, self.n_second = sizes
        self.sign = sign
        self.send, self.recv1, self.recv2 = sems

    def turn(self, way, place):
        flip = 1 - 2 * (place // 2 if isinstance(place, int) else lax.div(place, 2))
        return (self.sign if way == 0 else -self.sign) * flip

    def to_second(self, block, way, step, place, by=1):
        there = wrap(self.second + by * self.turn(way, place), self.n_second)
        remote(
            block,
            block,
            self.send.at[1, way],
            self.recv2.at[way, step, place],
            self.device(self.first, there),
        ).start()

    def begin(self, src, dst, device):
        for way in range(2):
            there = wrap(self.second + self.turn(way, 0), self.n_second)
            remote(
                src,
                dst,
                self.send.at[1, way],
                self.recv2.at[way, 0, 0],
                device(self.first, there),
            ).start()
        for place in range(1, self.n_first):
            there = wrap(self.first + self.sign * wander(place), self.n_first)
            remote(
                src,
                dst,
                self.send.at[0, 0],
                self.recv1.at[place],
                device(there, self.second),
            ).start()

    def along_first(self, place):
        block = self.block(
            wrap(self.first - self.sign * wander(place), self.n_first), self.second
        )
        await_bytes(block, self.recv1.at[place])
        for way in range(2):
            self.to_second(block, way, 0, place)

    def along_second(self, step, place):
        for way in range(2):
            if step > hops(self.n_second)[way]:
                continue
            block = self.block(
                wrap(self.first - self.sign * wander(place), self.n_first),
                wrap(self.second - self.turn(way, place) * step, self.n_second),
            )
            await_bytes(block, self.recv2.at[way, step - 1, place])
            if step < 3:
                self.to_second(block, way, step, place)
            if step == 2 and way == 0:
                self.to_second(block, way, 3, place, 2)


def kernel(
    tokens,
    qkv,
    out_weight,
    kind_hbm,
    out,
    wbuf,
    obuf,
    tbuf,
    msg,
    fin,
    rmsg,
    rfin,
    cbuf,
    mbuf,
    sbuf,
    qkv_sum,
    total,
    by_peer,
    by_frame,
    bias,
    kind,
    cross,
    own_sem,
    z_send,
    z_recv,
    w_send,
    w_recv1,
    w_recv2,
    o_send,
    o_recv1,
    o_recv2,
    t_send,
    t_recv,
    s_send,
    s_recv,
    a_send,
    a_recv,
    m_send,
    m_recv,
    n_send,
    n_recv,
    f_send,
    f_recv,
):
    frame = lax.axis_index("frame")
    band = lax.axis_index("band")
    y, z = lax.div(frame, NZ), lax.rem(frame, NZ)
    x, core = lax.div(band, 2), lax.rem(band, 2)
    across = z + (y - z) * core
    along = y + (z - y) * core
    pair, odd = lax.div(across, 2), lax.rem(across, 2)
    other = 1 - odd
    sign = 1 - 2 * core
    sibling_band = 2 * x + 1 - core
    sibling = (frame, sibling_band)
    sibling_odd = lax.rem(y + (z - y) * core, 2)
    me = along * PAIRS + pair

    def frame_at(along_there, across_there):
        return along_there * (NZ - (NZ - 1) * core) + across_there * (1 + (NZ - 1) * core)

    beside = frame_at(along, 2 * pair + other)

    def band_at(step):
        return 2 * wrap(x + step, NX) + core

    def peer(index):
        return (frame_at(lax.div(index, PAIRS), 2 * lax.rem(index, PAIRS) + odd), band)

    barrier = pltpu.get_barrier_semaphore()

    def greet(device):
        pl.semaphore_signal(barrier, inc=1, device_id=device, device_id_type=MESH)

    greet(sibling)
    greet((beside, sibling_band))
    for step in range(1, NY):
        greet((y * NZ + wrap(z + step, NZ), band))
        greet((wrap(y + step, NY) * NZ + z, band))
    for step in (1, -1):
        greet((frame_at(wrap(along + step, NY), 2 * pair + other), band))
    for step in range(1, NX):
        greet((frame, band_at(step)))

    def head_columns(which):
        return qkv.at[:, :, pl.ds(pl.multiple_of(which * HEAD, HEAD), HEAD)]

    own = [
        pltpu.make_async_copy(head_columns(odd), wbuf.at[:, along, pair, odd], own_sem.at[0]),
        pltpu.make_async_copy(out_weight.at[0:16], obuf.at[0, y, z], own_sem.at[1]),
        pltpu.make_async_copy(out_weight.at[16:32], obuf.at[1, z, y], own_sem.at[2]),
        pltpu.make_async_copy(tokens, tbuf.at[odd, band], own_sem.at[3]),
        pltpu.make_async_copy(kind_hbm, kind, own_sem.at[4]),
        pltpu.make_async_copy(head_columns(other), cross, own_sem.at[5]),
    ]
    for copy in own:
        copy.start()
    pl.semaphore_wait(barrier, 2 + NY - 1 + NZ - 1 + 2 + NX - 1)

    for copy in own:
        copy.wait()

    grid = Grid(
        lambda first, second: wbuf.at[:, second, first],
        lambda first, second: (frame_at(second, 2 * first + odd), band),
        (pair, along),
        (PAIRS, NY),
        sign,
        (w_send, w_recv1, w_recv2),
    )

    def token_along_x(which, block):
        for step in (1, NX - 1):
            remote(
                block, block, t_send.at[which, step], t_recv.at[which, step], (frame, band_at(step))
            ).start()

    def token_passed_on(which, by):
        if which == 0:
            block = tbuf.at[odd, band_at(-by)]
        else:
            block = tbuf.at[other, 2 * wrap(x - by, NX) + which - 1]
        remote(
            block, block, t_send.at[which, 2], t_recv.at[which, 2], (frame, band_at(by))
        ).start()

    def token_to_sibling(hop):
        from_band = band_at(-hop)
        remote(
            tbuf.at[odd, from_band],
            tbuf.at[sibling_odd, from_band],
            s_send.at[hop],
            s_recv.at[hop],
            sibling,
        ).start()

    here = wbuf.at[:, along, pair, odd]
    grid.begin(here, here, grid.device)
    grid.begin(
        cross, here, lambda first, second: (frame_at(second, 2 * first + other), band)
    )
    remote(cross, here, z_send.at[0], z_recv.at[0], (beside, band)).start()
    beside_z = y * NZ + z + 1 - 2 * lax.rem(z, 2)
    beside_y = (y + 1 - 2 * lax.rem(y, 2)) * NZ + z
    remote(
        tokens, tbuf.at[lax.rem(z, 2), band], z_send.at[1], z_recv.at[1 + core], (beside_z, 2 * x)
    ).start()
    remote(
        tokens, tbuf.at[lax.rem(y, 2), band], z_send.at[2], z_recv.at[1 + core], (beside_y, 2 * x + 1)
    ).start()
    token_along_x(0, tbuf.at[odd, band])
    remote(
        tbuf.at[odd, band], tbuf.at[sibling_odd, band], s_send.at[0], s_recv.at[0], sibling
    ).start()

    tall = lax.broadcasted_iota(jnp.int32, (ROWS, ROWS), 0)
    wide = lax.broadcasted_iota(jnp.int32, (ROWS, ROWS), 1)

    def origin(row):
        return (
            lax.rem(lax.div(row, SHARE), 2) * POSITIONS
            + lax.div(row, 2 * SHARE) * SHARE
            + lax.rem(row, SHARE)
        )

    qkv_sum[...] = jnp.zeros_like(qkv_sum)
    by_peer[...] = jnp.where(wide == origin(tall), 1.0, 0.0).astype(jnp.bfloat16)
    by_frame[...] = jnp.where(tall == origin(wide), 1.0, 0.0).astype(jnp.bfloat16)
    bias[...] = jnp.where(lax.rem(tall, SHARE) == lax.rem(wide, SHARE), 0.0, -1e30)

    def out_here(half):
        return (z, y) if half == 0 else (y, z)

    def out_device(half, first, second):
        return (second * NZ + first if half == 0 else first * NZ + second, band)

    def turn(way):
        return sign if way == 0 else -sign

    def out_send2(half, way, step, chunk, by=1):
        first, second = out_here(half)
        there = wrap(second + by * turn(way), NY)
        remote(
            chunk,
            chunk,
            o_send.at[half, 1, way],
            o_recv2.at[half, way, step],
            out_device(half, first, there),
        ).start()

    def out_along_first():
        for half in range(2):
            first, second = out_here(half)
            block = obuf.at[half, second, first]
            for step in range(1, NY):
                remote(
                    block,
                    block,
                    o_send.at[half, 0, 0],
                    o_recv1.at[half],
                    out_device(half, wrap(first + step, NY), second),
                ).start()

    def out_along_second(step):
        for half in range(2):
            first, second = out_here(half)
            for way in range(2):
                if step > hops(NY)[way]:
                    continue
                chunk = obuf.at[half, wrap(second - turn(way) * step, NY)]
                if step:
                    await_bytes(chunk, o_recv2.at[half, way, step - 1])
                if step < 3:
                    out_send2(half, way, step, chunk)
                if step == 2 and way == 0:
                    out_send2(half, way, 3, chunk, 2)

    def ring_step(step, start):
        def one(place, carry):
            grid.along_second(step, place)
            return carry

        lax.fori_loop(start, PAIRS, one, 0)

    grid.along_second(1, 0)
    for place in range(1, PAIRS):
        grid.along_first(place)
    grid.along_second(2, 0)
    for which in range(2):
        await_bytes(tbuf.at[other, 2 * x + which], z_recv.at[1 + which])
        token_along_x(1 + which, tbuf.at[other, 2 * x + which])
    ring_step(1, 1)
    for hop in (1, NX - 1):
        await_bytes(tbuf.at[odd, band_at(-hop)], t_recv.at[0, hop])
    token_passed_on(0, sign)
    token_to_sibling(1)
    token_to_sibling(NX - 1)
    ring_step(2, 1)
    for which, by in ((1, 1), (2, -1)):
        for hop in (1, NX - 1):
            await_bytes(
                tbuf.at[other, 2 * wrap(x - hop, NX) + which - 1], t_recv.at[which, hop]
            )
        token_passed_on(which, by)
    await_bytes(tbuf.at[odd, band_at(2)], t_recv.at[0, 2])
    token_to_sibling(2)
    out_along_first()
    ring_step(3, 0)
    for hop in range(NX):
        from_band = 2 * wrap(x - hop, NX) + 1 - core
        await_bytes(tbuf.at[odd, from_band], s_recv.at[hop])
        if hop == 2:
            for which in range(2):
                await_bytes(
                    tbuf.at[other, 2 * wrap(x - hop, NX) + which], t_recv.at[1 + which, hop]
                )
    ring_step(4, 0)
    await_bytes(wbuf.at[:, along, pair, other], z_recv.at[0])

    chunk = 2 * NZ * DEPTH

    def project(step, right):
        at = pl.ds(pl.multiple_of(step * chunk, HEAD), chunk)
        qkv_sum[...] += jnp.dot(
            tbuf[:, :, :, at].reshape(ROWS, chunk),
            jnp.concatenate([right(slot) for slot in range(3)], axis=1),
            preferred_element_type=jnp.float32,
        )

    @pl.when(core == 0)
    def _():
        def one(step, carry):
            project(step, lambda slot: wbuf[slot, pl.ds(2 * step, 2)].reshape(chunk, HEAD))
            return carry

        lax.fori_loop(0, NY // 2, one, 0)

    @pl.when(core == 1)
    def _():
        def one(step, carry):
            project(
                step,
                lambda slot: jnp.concatenate(
                    [
                        wbuf[slot, :, step, parity].reshape(chunk // 2, HEAD)
                        for parity in range(2)
                    ],
                    axis=0,
                ),
            )
            return carry

        lax.fori_loop(0, NY // 2, one, 0)

    rounded = qkv_sum[...].astype(jnp.bfloat16)

    msg[...] = (
        jnp.dot(by_peer[...], rounded, preferred_element_type=jnp.float32)
        .reshape(msg.shape)
        .astype(jnp.bfloat16)
    )

    def exchange(stage, source, target):
        def send(step, carry):
            there = lax.rem(me + PEERS // 2 + wander(step) + PEERS, PEERS)
            remote(
                source.at[there], target.at[me], a_send.at[stage], a_recv.at[stage], peer(there)
            ).start()
            return carry

        pltpu.make_async_copy(source.at[me], target.at[me], a_recv.at[stage]).start()
        lax.fori_loop(0, PEERS - 1, send, 0)

    exchange(0, msg, fin)
    for half in range(2):
        await_bytes(obuf.at[half, out_here(half)[1], 0 : NY - 1], o_recv1.at[half])
    out_along_second(0)
    spatial = jnp.concatenate(
        [
            attend(
                rounded[at : at + POSITIONS, :HEAD],
                rounded[at : at + POSITIONS, HEAD : 2 * HEAD],
                rounded[at : at + POSITIONS, 2 * HEAD :],
                None,
            )
            for at in (0, POSITIONS)
        ],
        axis=0,
    ).astype(jnp.bfloat16)
    await_bytes(wbuf.at[:, 0, 0, 0], z_send.at[0])
    await_bytes(tbuf.at[0, 0], z_send.at[1])
    await_bytes(tbuf.at[0, 0], z_send.at[2])
    await_bytes(wbuf.at[:, 0, 0 : PAIRS - 1], w_send.at[0, 0])
    for way in range(2):
        await_bytes(wbuf.at[:, 0 : hops(NY)[way]], w_send.at[1, way])
        await_bytes(obuf.at[way, 0, 0 : NY - 1], o_send.at[way, 0, 0])
    for hop in range(NX):
        await_bytes(tbuf.at[0, 0], s_send.at[hop])
        if hop:
            for which in range(3):
                await_bytes(tbuf.at[0, 0], t_send.at[which, hop])
    await_bytes(fin, a_recv.at[0])
    out_along_second(1)
    laid = fin[...].reshape(ROWS, 3 * HEAD)
    mixed = attend(laid[:, :HEAD], laid[:, HEAD : 2 * HEAD], laid[:, 2 * HEAD :], bias[...])
    rmsg[...] = mixed.reshape(rmsg.shape).astype(jnp.bfloat16)
    exchange(1, rmsg, rfin)
    await_bytes(msg.at[0 : PEERS - 1], a_send.at[0])
    await_bytes(rfin, a_recv.at[1])
    out_along_second(2)
    back = jnp.dot(
        by_frame[...], rfin[...].reshape(ROWS, HEAD), preferred_element_type=jnp.float32
    ).astype(jnp.bfloat16)
    temporal = jnp.full((ROWS, HEAD), kind[odd], jnp.int32) == 1
    cbuf[...] = jnp.where(temporal, back, spatial).reshape(cbuf.shape)

    for which, step in ((1, 2), (1, 1), (1, NX - 1), (0, 2), (1, 0), (0, 1), (0, NX - 1)):
        remote(
            cbuf.at[odd if which == 0 else other],
            mbuf.at[band, odd],
            m_send.at[which, step],
            m_recv.at[which, step],
            (frame if which == 0 else beside, band_at(step)),
        ).start()
    remote(
        cbuf.at[odd], mbuf.at[band, odd], n_send.at[0, 0], n_recv.at[0, 0], sibling
    ).start()
    last = pltpu.make_async_copy(cbuf.at[odd], mbuf.at[band, odd], m_recv.at[0, 0])
    last.start()
    for which, hop in ((1, 0), (0, 1), (0, 3), (1, 1), (1, 3), (0, 2), (1, 2)):
        block = mbuf.at[band_at(-hop), odd if which == 0 else other]
        await_bytes(block, m_recv.at[which, hop])
        remote(block, block, n_send.at[which, hop], n_recv.at[which, hop], sibling).start()
    out_along_second(3)
    out_along_second(4)
    last.wait()

    def project_out(source):
        left = jnp.concatenate([mbuf[source, 0], mbuf[source, 1]], axis=1)
        right = jnp.stack([obuf[0, source], obuf[1, :, source]], axis=1).reshape(
            2 * HEAD, WIDTH
        )
        return jnp.dot(left, right, preferred_element_type=jnp.float32)

    def own_core(hop, carry):
        total[...] += project_out(band_at(-hop))
        return carry

    def other_core(hop, carry):
        source = 2 * wrap(x - hop, NX) + 1 - core
        for which in range(2):
            await_bytes(
                mbuf.at[source, sibling_odd if which == 0 else 1 - sibling_odd],
                n_recv.at[which, hop],
            )
        total[...] += project_out(source)
        return carry

    total[...] = jnp.zeros_like(total)
    lax.fori_loop(0, NX, own_core, 0)
    lax.fori_loop(0, NX, other_core, 0)
    sbuf[...] = total[...].astype(jnp.bfloat16).reshape(sbuf.shape)

    def columns(which):
        return out.at[:, pl.ds(pl.multiple_of(which * WIDTH, HEAD), WIDTH)]

    for step in range(1, BANDS):
        there = wrap(band + step, BANDS)
        remote(
            sbuf.at[there], columns(band), f_send.at[step], f_recv.at[step], (frame, there)
        ).start()
    last = pltpu.make_async_copy(sbuf.at[band], columns(band), f_send.at[0])
    last.start()
    for step in range(1, BANDS):
        await_bytes(columns(wrap(band - step, BANDS)), f_recv.at[step])
    last.wait()

    await_bytes(rmsg.at[0 : PEERS - 1], a_send.at[1])
    for which in range(2):
        for hop in range(NX):
            if hop or which:
                await_bytes(cbuf.at[0], m_send.at[which, hop])
            await_bytes(cbuf.at[0], n_send.at[which, hop])
    for half in range(2):
        for way in range(2):
            await_bytes(obuf.at[half, 0 : hops(NY)[way]], o_send.at[half, 1, way])
    for step in range(1, BANDS):
        await_bytes(sbuf.at[0], f_send.at[step])


def body(tokens, qkv_weight, out_weight, head_kind):
    bf16 = jnp.bfloat16
    dma = pltpu.SemaphoreType.DMA
    hbm = pl.BlockSpec(memory_space=pltpu.HBM)
    return pl.pallas_call(
        kernel,
        out_shape=jax.ShapeDtypeStruct(tokens.shape, tokens.dtype),
        in_specs=[hbm] * 4,
        out_specs=hbm,
        scratch_shapes=[
            pltpu.VMEM((3, NY, PAIRS, 2, DEPTH, HEAD), bf16),
            pltpu.VMEM((2, 8, 8, 16, WIDTH), bf16),
            pltpu.VMEM((2, BANDS) + tokens.shape, bf16),
            pltpu.VMEM((PEERS, 2 * SHARE, 3 * HEAD), bf16),
            pltpu.VMEM((PEERS, 2 * SHARE, 3 * HEAD), bf16),
            pltpu.VMEM((PEERS, 2 * SHARE, HEAD), bf16),
            pltpu.VMEM((PEERS, 2 * SHARE, HEAD), bf16),
            pltpu.VMEM((2, POSITIONS, HEAD), bf16),
            pltpu.VMEM((BANDS, 2, POSITIONS, HEAD), bf16),
            pltpu.VMEM((BANDS, 16, WIDTH), bf16),
            pltpu.VMEM((ROWS, 3 * HEAD), jnp.float32),
            pltpu.VMEM((POSITIONS, WIDTH), jnp.float32),
            pltpu.VMEM((ROWS, ROWS), bf16),
            pltpu.VMEM((ROWS, ROWS), bf16),
            pltpu.VMEM((ROWS, ROWS), jnp.float32),
            pltpu.SMEM((2,), jnp.int32),
            pltpu.VMEM((3, DEPTH, HEAD), bf16),
            dma((6,)),
            dma((3,)),
            dma((3,)),
            dma((2, 2)),
            dma((4,)),
            dma((2, 4, 4)),
            dma((2, 2, 2)),
            dma((2,)),
            dma((2, 2, 4)),
            dma((3, NX)),
            dma((3, NX)),
            dma((NX,)),
            dma((NX,)),
            dma((2,)),
            dma((2,)),
            dma((2, NX)),
            dma((2, NX)),
            dma((2, NX)),
            dma((2, NX)),
            dma((BANDS,)),
            dma((BANDS,)),
        ],
        compiler_params=pltpu.CompilerParams(
            collective_id=0, has_side_effects=True, vmem_limit_bytes=64 * 1024 * 1024
        ),
    )(tokens, qkv_weight.transpose(1, 0, 2), out_weight, head_kind)


def solution(mesh):
    return jax.shard_map(
        body,
        mesh=mesh,
        in_specs=(
            P(("frame", "band"), None),
            P("frame", None, "band"),
            P("frame", "band"),
            P("band"),
        ),
        out_specs=P(("frame", "band"), None),
        check_vma=False,
    )
```

```python
import jax
import jax.numpy as jnp
from jax import lax
from jax.experimental import pallas as pl
from jax.experimental.pallas import tpu as pltpu
from jax.sharding import PartitionSpec as P

MESH = pl.DeviceIdType.MESH
NX = 4
NY = 8
NZ = 8
PAIRS = NZ // 2
BANDS = 2 * NX
PEERS = NY * PAIRS
HEAD = 128
POSITIONS = 128
ROWS = 2 * POSITIONS
SHARE = POSITIONS // PEERS
DEPTH = 48
WIDTH = 384


def remote(src, dst, send_sem, recv_sem, device):
    return pltpu.make_async_remote_copy(
        src_ref=src,
        dst_ref=dst,
        send_sem=send_sem,
        recv_sem=recv_sem,
        device_id=device,
        device_id_type=MESH,
    )


def await_bytes(ref, sem):
    pltpu.make_async_copy(ref, ref, sem).wait()


def attend(queries, keys, values, bias):
    scores = lax.dot_general(
        queries, keys, (((1,), (1,)), ((), ())), preferred_element_type=jnp.float32
    ) * (HEAD**-0.5)
    if bias is not None:
        scores = scores + bias
    raised = jnp.exp(scores - jnp.max(scores, axis=-1, keepdims=True))
    probs = (raised / jnp.sum(raised, axis=-1, keepdims=True)).astype(jnp.bfloat16)
    return jnp.dot(probs, values, preferred_element_type=jnp.float32)


def wrap(value, size):
    return lax.rem(value + 8 * size, size)


def hops(size):
    return (size // 2, (size - 1) // 2)


def wander(place):
    if isinstance(place, int):
        return (place + 1) // 2 * (2 * (place % 2) - 1)
    return lax.div(place + 1, 2) * (2 * lax.rem(place, 2) - 1)


class Grid:
    def __init__(self, block, device, here, sizes, sign, sems):
        self.block = block
        self.device = device
        self.first, self.second = here
        self.n_first, self.n_second = sizes
        self.sign = sign
        self.send, self.recv1, self.recv2 = sems

    def turn(self, way, place):
        flip = 1 - 2 * (place // 2 if isinstance(place, int) else lax.div(place, 2))
        return (self.sign if way == 0 else -self.sign) * flip

    def to_second(self, block, way, step, place, by=1):
        there = wrap(self.second + by * self.turn(way, place), self.n_second)
        remote(
            block,
            block,
            self.send.at[1, way],
            self.recv2.at[way, step, place],
            self.device(self.first, there),
        ).start()

    def begin(self, src, dst, device):
        for way in range(2):
            there = wrap(self.second + self.turn(way, 0), self.n_second)
            remote(
                src,
                dst,
                self.send.at[1, way],
                self.recv2.at[way, 0, 0],
                device(self.first, there),
            ).start()
        for place in range(1, self.n_first):
            there = wrap(self.first + self.sign * wander(place), self.n_first)
            remote(
                src,
                dst,
                self.send.at[0, 0],
                self.recv1.at[place],
                device(there, self.second),
            ).start()

    def along_first(self, place):
        block = self.block(
            wrap(self.first - self.sign * wander(place), self.n_first), self.second
        )
        await_bytes(block, self.recv1.at[place])
        for way in range(2):
            self.to_second(block, way, 0, place)

    def along_second(self, step, place):
        for way in range(2):
            if step > hops(self.n_second)[way]:
                continue
            block = self.block(
                wrap(self.first - self.sign * wander(place), self.n_first),
                wrap(self.second - self.turn(way, place) * step, self.n_second),
            )
            await_bytes(block, self.recv2.at[way, step - 1, place])
            if step < 3:
                self.to_second(block, way, step, place)
            if step == 2 and way == 0:
                self.to_second(block, way, 3, place, 2)


def kernel(
    tokens,
    qkv,
    out_weight,
    kind_hbm,
    out,
    wbuf,
    obuf,
    tbuf,
    msg,
    fin,
    rmsg,
    rfin,
    cbuf,
    mbuf,
    sbuf,
    qkv_sum,
    total,
    by_peer,
    by_frame,
    bias,
    kind,
    cross,
    own_sem,
    z_send,
    z_recv,
    w_send,
    w_recv1,
    w_recv2,
    o_send,
    o_recv1,
    o_recv2,
    t_send,
    t_recv,
    s_send,
    s_recv,
    a_send,
    a_recv,
    m_send,
    m_recv,
    n_send,
    n_recv,
    f_send,
    f_recv,
):
    frame = lax.axis_index("frame")
    band = lax.axis_index("band")
    y, z = lax.div(frame, NZ), lax.rem(frame, NZ)
    x, core = lax.div(band, 2), lax.rem(band, 2)
    across = z + (y - z) * core
    along = y + (z - y) * core
    pair, odd = lax.div(across, 2), lax.rem(across, 2)
    other = 1 - odd
    sign = 1 - 2 * core
    sibling_band = 2 * x + 1 - core
    sibling = (frame, sibling_band)
    sibling_odd = lax.rem(y + (z - y) * core, 2)
    me = along * PAIRS + pair

    def frame_at(along_there, across_there):
        return along_there * (NZ - (NZ - 1) * core) + across_there * (1 + (NZ - 1) * core)

    beside = frame_at(along, 2 * pair + other)

    def band_at(step):
        return 2 * wrap(x + step, NX) + core

    def peer(index):
        return (frame_at(lax.div(index, PAIRS), 2 * lax.rem(index, PAIRS) + odd), band)

    barrier = pltpu.get_barrier_semaphore()

    def greet(device):
        pl.semaphore_signal(barrier, inc=1, device_id=device, device_id_type=MESH)

    greet(sibling)
    greet((beside, sibling_band))
    for step in range(1, NY):
        greet((y * NZ + wrap(z + step, NZ), band))
        greet((wrap(y + step, NY) * NZ + z, band))
    for step in (1, -1):
        greet((frame_at(wrap(along + step, NY), 2 * pair + other), band))
    for step in range(1, NX):
        greet((frame, band_at(step)))

    def head_columns(which):
        return qkv.at[:, :, pl.ds(pl.multiple_of(which * HEAD, HEAD), HEAD)]

    own = [
        pltpu.make_async_copy(head_columns(odd), wbuf.at[:, along, pair, odd], own_sem.at[0]),
        pltpu.make_async_copy(out_weight.at[0:16], obuf.at[0, y, z], own_sem.at[1]),
        pltpu.make_async_copy(out_weight.at[16:32], obuf.at[1, z, y], own_sem.at[2]),
        pltpu.make_async_copy(tokens, tbuf.at[odd, band], own_sem.at[3]),
        pltpu.make_async_copy(kind_hbm, kind, own_sem.at[4]),
        pltpu.make_async_copy(head_columns(other), cross, own_sem.at[5]),
    ]
    for copy in own:
        copy.start()
    pl.semaphore_wait(barrier, 2 + NY - 1 + NZ - 1 + 2 + NX - 1)

    for copy in own:
        copy.wait()

    grid = Grid(
        lambda first, second: wbuf.at[:, second, first],
        lambda first, second: (frame_at(second, 2 * first + odd), band),
        (pair, along),
        (PAIRS, NY),
        sign,
        (w_send, w_recv1, w_recv2),
    )

    def token_along_x(which, block):
        for step in (1, NX - 1):
            remote(
                block, block, t_send.at[which, step], t_recv.at[which, step], (frame, band_at(step))
            ).start()

    def token_passed_on(which, by):
        if which == 0:
            block = tbuf.at[odd, band_at(-by)]
        else:
            block = tbuf.at[other, 2 * wrap(x - by, NX) + which - 1]
        remote(
            block, block, t_send.at[which, 2], t_recv.at[which, 2], (frame, band_at(by))
        ).start()

    def token_to_sibling(hop):
        from_band = band_at(-hop)
        remote(
            tbuf.at[odd, from_band],
            tbuf.at[sibling_odd, from_band],
            s_send.at[hop],
            s_recv.at[hop],
            sibling,
        ).start()

    here = wbuf.at[:, along, pair, odd]
    grid.begin(here, here, grid.device)
    grid.begin(
        cross, here, lambda first, second: (frame_at(second, 2 * first + other), band)
    )
    remote(cross, here, z_send.at[0], z_recv.at[0], (beside, band)).start()
    beside_z = y * NZ + z + 1 - 2 * lax.rem(z, 2)
    beside_y = (y + 1 - 2 * lax.rem(y, 2)) * NZ + z
    remote(
        tokens, tbuf.at[lax.rem(z, 2), band], z_send.at[1], z_recv.at[1 + core], (beside_z, 2 * x)
    ).start()
    remote(
        tokens, tbuf.at[lax.rem(y, 2), band], z_send.at[2], z_recv.at[1 + core], (beside_y, 2 * x + 1)
    ).start()
    token_along_x(0, tbuf.at[odd, band])
    remote(
        tbuf.at[odd, band], tbuf.at[sibling_odd, band], s_send.at[0], s_recv.at[0], sibling
    ).start()

    tall = lax.broadcasted_iota(jnp.int32, (ROWS, ROWS), 0)
    wide = lax.broadcasted_iota(jnp.int32, (ROWS, ROWS), 1)

    def origin(row):
        return (
            lax.rem(lax.div(row, SHARE), 2) * POSITIONS
            + lax.div(row, 2 * SHARE) * SHARE
            + lax.rem(row, SHARE)
        )

    qkv_sum[...] = jnp.zeros_like(qkv_sum)
    by_peer[...] = jnp.where(wide == origin(tall), 1.0, 0.0).astype(jnp.bfloat16)
    by_frame[...] = jnp.where(tall == origin(wide), 1.0, 0.0).astype(jnp.bfloat16)
    bias[...] = jnp.where(lax.rem(tall, SHARE) == lax.rem(wide, SHARE), 0.0, -1e30)

    def out_here(half):
        return (z, y) if half == 0 else (y, z)

    def out_device(half, first, second):
        return (second * NZ + first if half == 0 else first * NZ + second, band)

    def turn(way):
        return sign if way == 0 else -sign

    def out_send2(half, way, step, chunk, by=1):
        first, second = out_here(half)
        there = wrap(second + by * turn(way), NY)
        remote(
            chunk,
            chunk,
            o_send.at[half, 1, way],
            o_recv2.at[half, way, step],
            out_device(half, first, there),
        ).start()

    def out_along_first():
        for half in range(2):
            first, second = out_here(half)
            block = obuf.at[half, second, first]
            for step in range(1, NY):
                remote(
                    block,
                    block,
                    o_send.at[half, 0, 0],
                    o_recv1.at[half],
                    out_device(half, wrap(first + step, NY), second),
                ).start()

    def out_along_second(step):
        for half in range(2):
            first, second = out_here(half)
            for way in range(2):
                if step > hops(NY)[way]:
                    continue
                chunk = obuf.at[half, wrap(second - turn(way) * step, NY)]
                if step:
                    await_bytes(chunk, o_recv2.at[half, way, step - 1])
                if step < 3:
                    out_send2(half, way, step, chunk)
                if step == 2 and way == 0:
                    out_send2(half, way, 3, chunk, 2)

    def ring_step(step, start):
        def one(place, carry):
            grid.along_second(step, place)
            return carry

        lax.fori_loop(start, PAIRS, one, 0)

    out_along_first()
    grid.along_second(1, 0)
    for place in range(1, PAIRS):
        grid.along_first(place)
    grid.along_second(2, 0)
    for which in range(2):
        await_bytes(tbuf.at[other, 2 * x + which], z_recv.at[1 + which])
        token_along_x(1 + which, tbuf.at[other, 2 * x + which])
    ring_step(1, 1)
    for hop in (1, NX - 1):
        await_bytes(tbuf.at[odd, band_at(-hop)], t_recv.at[0, hop])
    token_passed_on(0, sign)
    token_to_sibling(1)
    token_to_sibling(NX - 1)
    ring_step(2, 1)
    for which, by in ((1, 1), (2, -1)):
        for hop in (1, NX - 1):
            await_bytes(
                tbuf.at[other, 2 * wrap(x - hop, NX) + which - 1], t_recv.at[which, hop]
            )
        token_passed_on(which, by)
    await_bytes(tbuf.at[odd, band_at(2)], t_recv.at[0, 2])
    token_to_sibling(2)
    ring_step(3, 0)
    for hop in range(NX):
        from_band = 2 * wrap(x - hop, NX) + 1 - core
        await_bytes(tbuf.at[odd, from_band], s_recv.at[hop])
        if hop == 2:
            for which in range(2):
                await_bytes(
                    tbuf.at[other, 2 * wrap(x - hop, NX) + which], t_recv.at[1 + which, hop]
                )
    ring_step(4, 0)
    for half in range(2):
        await_bytes(obuf.at[half, out_here(half)[1], 0 : NY - 1], o_recv1.at[half])
    out_along_second(0)
    await_bytes(wbuf.at[:, along, pair, other], z_recv.at[0])

    chunk = 2 * NZ * DEPTH

    def project(step, right):
        at = pl.ds(pl.multiple_of(step * chunk, HEAD), chunk)
        qkv_sum[...] += jnp.dot(
            tbuf[:, :, :, at].reshape(ROWS, chunk),
            jnp.concatenate([right(slot) for slot in range(3)], axis=1),
            preferred_element_type=jnp.float32,
        )

    @pl.when(core == 0)
    def _():
        def one(step, carry):
            project(step, lambda slot: wbuf[slot, pl.ds(2 * step, 2)].reshape(chunk, HEAD))
            return carry

        lax.fori_loop(0, NY // 2, one, 0)

    @pl.when(core == 1)
    def _():
        def one(step, carry):
            project(
                step,
                lambda slot: jnp.concatenate(
                    [
                        wbuf[slot, :, step, parity].reshape(chunk // 2, HEAD)
                        for parity in range(2)
                    ],
                    axis=0,
                ),
            )
            return carry

        lax.fori_loop(0, NY // 2, one, 0)

    rounded = qkv_sum[...].astype(jnp.bfloat16)

    msg[...] = (
        jnp.dot(by_peer[...], rounded, preferred_element_type=jnp.float32)
        .reshape(msg.shape)
        .astype(jnp.bfloat16)
    )

    def exchange(stage, source, target):
        def send(step, carry):
            there = lax.rem(me + PEERS // 2 + wander(step) + PEERS, PEERS)
            remote(
                source.at[there], target.at[me], a_send.at[stage], a_recv.at[stage], peer(there)
            ).start()
            return carry

        pltpu.make_async_copy(source.at[me], target.at[me], a_recv.at[stage]).start()
        lax.fori_loop(0, PEERS - 1, send, 0)

    exchange(0, msg, fin)
    spatial = jnp.concatenate(
        [
            attend(
                rounded[at : at + POSITIONS, :HEAD],
                rounded[at : at + POSITIONS, HEAD : 2 * HEAD],
                rounded[at : at + POSITIONS, 2 * HEAD :],
                None,
            )
            for at in (0, POSITIONS)
        ],
        axis=0,
    ).astype(jnp.bfloat16)
    out_along_second(1)

    await_bytes(wbuf.at[:, 0, 0, 0], z_send.at[0])
    await_bytes(tbuf.at[0, 0], z_send.at[1])
    await_bytes(tbuf.at[0, 0], z_send.at[2])
    await_bytes(wbuf.at[:, 0, 0 : PAIRS - 1], w_send.at[0, 0])
    for way in range(2):
        await_bytes(wbuf.at[:, 0 : hops(NY)[way]], w_send.at[1, way])
        await_bytes(obuf.at[way, 0, 0 : NY - 1], o_send.at[way, 0, 0])
    for hop in range(NX):
        await_bytes(tbuf.at[0, 0], s_send.at[hop])
        if hop:
            for which in range(3):
                await_bytes(tbuf.at[0, 0], t_send.at[which, hop])
    await_bytes(fin, a_recv.at[0])
    laid = fin[...].reshape(ROWS, 3 * HEAD)
    mixed = attend(laid[:, :HEAD], laid[:, HEAD : 2 * HEAD], laid[:, 2 * HEAD :], bias[...])
    rmsg[...] = mixed.reshape(rmsg.shape).astype(jnp.bfloat16)
    exchange(1, rmsg, rfin)
    out_along_second(2)
    await_bytes(msg.at[0 : PEERS - 1], a_send.at[0])
    await_bytes(rfin, a_recv.at[1])
    back = jnp.dot(
        by_frame[...], rfin[...].reshape(ROWS, HEAD), preferred_element_type=jnp.float32
    ).astype(jnp.bfloat16)
    temporal = jnp.full((ROWS, HEAD), kind[odd], jnp.int32) == 1
    cbuf[...] = jnp.where(temporal, back, spatial).reshape(cbuf.shape)

    for which, step in ((1, 2), (1, 1), (1, NX - 1), (0, 2), (1, 0), (0, 1), (0, NX - 1)):
        remote(
            cbuf.at[odd if which == 0 else other],
            mbuf.at[band, odd],
            m_send.at[which, step],
            m_recv.at[which, step],
            (frame if which == 0 else beside, band_at(step)),
        ).start()
    remote(
        cbuf.at[odd], mbuf.at[band, odd], n_send.at[0, 0], n_recv.at[0, 0], sibling
    ).start()
    last = pltpu.make_async_copy(cbuf.at[odd], mbuf.at[band, odd], m_recv.at[0, 0])
    last.start()
    for which, hop in ((1, 0), (0, 1), (0, 3), (1, 1), (1, 3), (0, 2), (1, 2)):
        block = mbuf.at[band_at(-hop), odd if which == 0 else other]
        await_bytes(block, m_recv.at[which, hop])
        remote(block, block, n_send.at[which, hop], n_recv.at[which, hop], sibling).start()
    out_along_second(3)
    out_along_second(4)
    last.wait()

    def project_out(source):
        left = jnp.concatenate([mbuf[source, 0], mbuf[source, 1]], axis=1)
        right = jnp.stack([obuf[0, source], obuf[1, :, source]], axis=1).reshape(
            2 * HEAD, WIDTH
        )
        return jnp.dot(left, right, preferred_element_type=jnp.float32)

    def own_core(hop, carry):
        total[...] += project_out(band_at(-hop))
        return carry

    def other_core(hop, carry):
        source = 2 * wrap(x - hop, NX) + 1 - core
        for which in range(2):
            await_bytes(
                mbuf.at[source, sibling_odd if which == 0 else 1 - sibling_odd],
                n_recv.at[which, hop],
            )
        total[...] += project_out(source)
        return carry

    total[...] = jnp.zeros_like(total)
    lax.fori_loop(0, NX, own_core, 0)
    lax.fori_loop(0, NX, other_core, 0)
    sbuf[...] = total[...].astype(jnp.bfloat16).reshape(sbuf.shape)

    def columns(which):
        return out.at[:, pl.ds(pl.multiple_of(which * WIDTH, HEAD), WIDTH)]

    for step in range(1, BANDS):
        there = wrap(band + step, BANDS)
        remote(
            sbuf.at[there], columns(band), f_send.at[step], f_recv.at[step], (frame, there)
        ).start()
    last = pltpu.make_async_copy(sbuf.at[band], columns(band), f_send.at[0])
    last.start()
    for step in range(1, BANDS):
        await_bytes(columns(wrap(band - step, BANDS)), f_recv.at[step])
    last.wait()

    await_bytes(rmsg.at[0 : PEERS - 1], a_send.at[1])
    for which in range(2):
        for hop in range(NX):
            if hop or which:
                await_bytes(cbuf.at[0], m_send.at[which, hop])
            await_bytes(cbuf.at[0], n_send.at[which, hop])
    for half in range(2):
        for way in range(2):
            await_bytes(obuf.at[half, 0 : hops(NY)[way]], o_send.at[half, 1, way])
    for step in range(1, BANDS):
        await_bytes(sbuf.at[0], f_send.at[step])


def body(tokens, qkv_weight, out_weight, head_kind):
    bf16 = jnp.bfloat16
    dma = pltpu.SemaphoreType.DMA
    hbm = pl.BlockSpec(memory_space=pltpu.HBM)
    return pl.pallas_call(
        kernel,
        out_shape=jax.ShapeDtypeStruct(tokens.shape, tokens.dtype),
        in_specs=[hbm] * 4,
        out_specs=hbm,
        scratch_shapes=[
            pltpu.VMEM((3, NY, PAIRS, 2, DEPTH, HEAD), bf16),
            pltpu.VMEM((2, 8, 8, 16, WIDTH), bf16),
            pltpu.VMEM((2, BANDS) + tokens.shape, bf16),
            pltpu.VMEM((PEERS, 2 * SHARE, 3 * HEAD), bf16),
            pltpu.VMEM((PEERS, 2 * SHARE, 3 * HEAD), bf16),
            pltpu.VMEM((PEERS, 2 * SHARE, HEAD), bf16),
            pltpu.VMEM((PEERS, 2 * SHARE, HEAD), bf16),
            pltpu.VMEM((2, POSITIONS, HEAD), bf16),
            pltpu.VMEM((BANDS, 2, POSITIONS, HEAD), bf16),
            pltpu.VMEM((BANDS, 16, WIDTH), bf16),
            pltpu.VMEM((ROWS, 3 * HEAD), jnp.float32),
            pltpu.VMEM((POSITIONS, WIDTH), jnp.float32),
            pltpu.VMEM((ROWS, ROWS), bf16),
            pltpu.VMEM((ROWS, ROWS), bf16),
            pltpu.VMEM((ROWS, ROWS), jnp.float32),
            pltpu.SMEM((2,), jnp.int32),
            pltpu.VMEM((3, DEPTH, HEAD), bf16),
            dma((6,)),
            dma((3,)),
            dma((3,)),
            dma((2, 2)),
            dma((4,)),
            dma((2, 4, 4)),
            dma((2, 2, 2)),
            dma((2,)),
            dma((2, 2, 4)),
            dma((3, NX)),
            dma((3, NX)),
            dma((NX,)),
            dma((NX,)),
            dma((2,)),
            dma((2,)),
            dma((2, NX)),
            dma((2, NX)),
            dma((2, NX)),
            dma((2, NX)),
            dma((BANDS,)),
            dma((BANDS,)),
        ],
        compiler_params=pltpu.CompilerParams(
            collective_id=0, has_side_effects=True, vmem_limit_bytes=64 * 1024 * 1024
        ),
    )(tokens, qkv_weight.transpose(1, 0, 2), out_weight, head_kind)


def solution(mesh):
    return jax.shard_map(
        body,
        mesh=mesh,
        in_specs=(
            P(("frame", "band"), None),
            P("frame", None, "band"),
            P("frame", "band"),
            P("band"),
        ),
        out_specs=P(("frame", "band"), None),
        check_vma=False,
    )
```

```python
import jax
import jax.numpy as jnp
from jax import lax
from jax.experimental import pallas as pl
from jax.experimental.pallas import tpu as pltpu
from jax.sharding import PartitionSpec as P

MESH = pl.DeviceIdType.MESH
NX = 4
NY = 8
NZ = 8
PAIRS = NZ // 2
BANDS = 2 * NX
PEERS = NY * PAIRS
HEAD = 128
POSITIONS = 128
ROWS = 2 * POSITIONS
SHARE = POSITIONS // PEERS
DEPTH = 48
WIDTH = 384


def remote(src, dst, send_sem, recv_sem, device):
    return pltpu.make_async_remote_copy(
        src_ref=src,
        dst_ref=dst,
        send_sem=send_sem,
        recv_sem=recv_sem,
        device_id=device,
        device_id_type=MESH,
    )


def await_bytes(ref, sem):
    pltpu.make_async_copy(ref, ref, sem).wait()


def attend(queries, keys, values, bias):
    scores = lax.dot_general(
        queries, keys, (((1,), (1,)), ((), ())), preferred_element_type=jnp.float32
    ) * (HEAD**-0.5)
    if bias is not None:
        scores = scores + bias
    raised = jnp.exp(scores - jnp.max(scores, axis=-1, keepdims=True))
    probs = (raised / jnp.sum(raised, axis=-1, keepdims=True)).astype(jnp.bfloat16)
    return jnp.dot(probs, values, preferred_element_type=jnp.float32)


def wrap(value, size):
    return lax.rem(value + 8 * size, size)


def hops(size):
    return (size // 2, (size - 1) // 2)


def wander(place):
    if isinstance(place, int):
        return (place + 1) // 2 * (2 * (place % 2) - 1)
    return lax.div(place + 1, 2) * (2 * lax.rem(place, 2) - 1)


class Grid:
    def __init__(self, block, device, here, sizes, sign, sems):
        self.block = block
        self.device = device
        self.first, self.second = here
        self.n_first, self.n_second = sizes
        self.sign = sign
        self.send, self.recv1, self.recv2 = sems

    def turn(self, way, place):
        flip = 1 - 2 * (place // 2 if isinstance(place, int) else lax.div(place, 2))
        return (self.sign if way == 0 else -self.sign) * flip

    def to_second(self, block, way, step, place, by=1):
        there = wrap(self.second + by * self.turn(way, place), self.n_second)
        remote(
            block,
            block,
            self.send.at[1, way],
            self.recv2.at[way, step, place],
            self.device(self.first, there),
        ).start()

    def begin(self, src, dst, device):
        for way in range(2):
            there = wrap(self.second + self.turn(way, 0), self.n_second)
            remote(
                src,
                dst,
                self.send.at[1, way],
                self.recv2.at[way, 0, 0],
                device(self.first, there),
            ).start()
        for place in range(1, self.n_first):
            there = wrap(self.first + self.sign * wander(place), self.n_first)
            remote(
                src,
                dst,
                self.send.at[0, 0],
                self.recv1.at[place],
                device(there, self.second),
            ).start()

    def along_first(self, place):
        block = self.block(
            wrap(self.first - self.sign * wander(place), self.n_first), self.second
        )
        await_bytes(block, self.recv1.at[place])
        for way in range(2):
            self.to_second(block, way, 0, place)

    def along_second(self, step, place):
        for way in range(2):
            if step > hops(self.n_second)[way]:
                continue
            block = self.block(
                wrap(self.first - self.sign * wander(place), self.n_first),
                wrap(self.second - self.turn(way, place) * step, self.n_second),
            )
            await_bytes(block, self.recv2.at[way, step - 1, place])
            if step < 3:
                self.to_second(block, way, step, place)
            if step == 2 and way == 0:
                self.to_second(block, way, 3, place, 2)


def kernel(
    tokens,
    qkv,
    out_weight,
    kind_hbm,
    out,
    wbuf,
    obuf,
    tbuf,
    msg,
    fin,
    rmsg,
    rfin,
    cbuf,
    mbuf,
    sbuf,
    qkv_sum,
    total,
    by_peer,
    by_frame,
    bias,
    kind,
    cross,
    own_sem,
    z_send,
    z_recv,
    w_send,
    w_recv1,
    w_recv2,
    o_send,
    o_recv1,
    o_recv2,
    t_send,
    t_recv,
    s_send,
    s_recv,
    a_send,
    a_recv,
    m_send,
    m_recv,
    n_send,
    n_recv,
    f_send,
    f_recv,
):
    frame = lax.axis_index("frame")
    band = lax.axis_index("band")
    y, z = lax.div(frame, NZ), lax.rem(frame, NZ)
    x, core = lax.div(band, 2), lax.rem(band, 2)
    across = z + (y - z) * core
    along = y + (z - y) * core
    pair, odd = lax.div(across, 2), lax.rem(across, 2)
    other = 1 - odd
    sign = 1 - 2 * core
    sibling_band = 2 * x + 1 - core
    sibling = (frame, sibling_band)
    sibling_odd = lax.rem(y + (z - y) * core, 2)
    me = along * PAIRS + pair

    def frame_at(along_there, across_there):
        return along_there * (NZ - (NZ - 1) * core) + across_there * (1 + (NZ - 1) * core)

    beside = frame_at(along, 2 * pair + other)

    def band_at(step):
        return 2 * wrap(x + step, NX) + core

    def peer(index):
        return (frame_at(lax.div(index, PAIRS), 2 * lax.rem(index, PAIRS) + odd), band)

    barrier = pltpu.get_barrier_semaphore()

    def greet(device):
        pl.semaphore_signal(barrier, inc=1, device_id=device, device_id_type=MESH)

    greet(sibling)
    greet((beside, sibling_band))
    for step in range(1, NY):
        greet((y * NZ + wrap(z + step, NZ), band))
        greet((wrap(y + step, NY) * NZ + z, band))
    for step in (1, -1):
        greet((frame_at(wrap(along + step, NY), 2 * pair + other), band))
    for step in range(1, NX):
        greet((frame, band_at(step)))

    def head_columns(which):
        return qkv.at[:, :, pl.ds(pl.multiple_of(which * HEAD, HEAD), HEAD)]

    own = [
        pltpu.make_async_copy(head_columns(odd), wbuf.at[:, along, pair, odd], own_sem.at[0]),
        pltpu.make_async_copy(out_weight.at[0:16], obuf.at[0, y, z], own_sem.at[1]),
        pltpu.make_async_copy(out_weight.at[16:32], obuf.at[1, z, y], own_sem.at[2]),
        pltpu.make_async_copy(tokens, tbuf.at[odd, band], own_sem.at[3]),
        pltpu.make_async_copy(kind_hbm, kind, own_sem.at[4]),
        pltpu.make_async_copy(head_columns(other), cross, own_sem.at[5]),
    ]
    for copy in own:
        copy.start()
    pl.semaphore_wait(barrier, 2 + NY - 1 + NZ - 1 + 2 + NX - 1)

    for copy in own:
        copy.wait()

    grid = Grid(
        lambda first, second: wbuf.at[:, second, first],
        lambda first, second: (frame_at(second, 2 * first + odd), band),
        (pair, along),
        (PAIRS, NY),
        sign,
        (w_send, w_recv1, w_recv2),
    )

    def token_along_x(which, block):
        for step in (1, NX - 1):
            remote(
                block, block, t_send.at[which, step], t_recv.at[which, step], (frame, band_at(step))
            ).start()

    def token_passed_on(which, by):
        if which == 0:
            block = tbuf.at[odd, band_at(-by)]
        else:
            block = tbuf.at[other, 2 * wrap(x - by, NX) + which - 1]
        remote(
            block, block, t_send.at[which, 2], t_recv.at[which, 2], (frame, band_at(by))
        ).start()

    def token_to_sibling(hop):
        from_band = band_at(-hop)
        remote(
            tbuf.at[odd, from_band],
            tbuf.at[sibling_odd, from_band],
            s_send.at[hop],
            s_recv.at[hop],
            sibling,
        ).start()

    here = wbuf.at[:, along, pair, odd]
    grid.begin(here, here, grid.device)
    grid.begin(
        cross, here, lambda first, second: (frame_at(second, 2 * first + other), band)
    )
    remote(cross, here, z_send.at[0], z_recv.at[0], (beside, band)).start()
    beside_z = y * NZ + z + 1 - 2 * lax.rem(z, 2)
    beside_y = (y + 1 - 2 * lax.rem(y, 2)) * NZ + z
    remote(
        tokens, tbuf.at[lax.rem(z, 2), band], z_send.at[1], z_recv.at[1 + core], (beside_z, 2 * x)
    ).start()
    remote(
        tokens, tbuf.at[lax.rem(y, 2), band], z_send.at[2], z_recv.at[1 + core], (beside_y, 2 * x + 1)
    ).start()
    token_along_x(0, tbuf.at[odd, band])
    remote(
        tbuf.at[odd, band], tbuf.at[sibling_odd, band], s_send.at[0], s_recv.at[0], sibling
    ).start()

    tall = lax.broadcasted_iota(jnp.int32, (ROWS, ROWS), 0)
    wide = lax.broadcasted_iota(jnp.int32, (ROWS, ROWS), 1)

    def origin(row):
        return (
            lax.rem(lax.div(row, SHARE), 2) * POSITIONS
            + lax.div(row, 2 * SHARE) * SHARE
            + lax.rem(row, SHARE)
        )

    qkv_sum[...] = jnp.zeros_like(qkv_sum)
    by_peer[...] = jnp.where(wide == origin(tall), 1.0, 0.0).astype(jnp.bfloat16)
    by_frame[...] = jnp.where(tall == origin(wide), 1.0, 0.0).astype(jnp.bfloat16)
    bias[...] = jnp.where(lax.rem(tall, SHARE) == lax.rem(wide, SHARE), 0.0, -1e30)

    grid.along_second(1, 0)
    for which in range(2):
        await_bytes(tbuf.at[other, 2 * x + which], z_recv.at[1 + which])
        token_along_x(1 + which, tbuf.at[other, 2 * x + which])

    def out_here(half):
        return (z, y) if half == 0 else (y, z)

    def out_device(half, first, second):
        return (second * NZ + first if half == 0 else first * NZ + second, band)

    def turn(way):
        return sign if way == 0 else -sign

    def out_send2(half, way, step, chunk, by=1):
        first, second = out_here(half)
        there = wrap(second + by * turn(way), NY)
        remote(
            chunk,
            chunk,
            o_send.at[half, 1, way],
            o_recv2.at[half, way, step],
            out_device(half, first, there),
        ).start()

    def out_along_first():
        for half in range(2):
            first, second = out_here(half)
            block = obuf.at[half, second, first]
            for step in range(1, NY):
                remote(
                    block,
                    block,
                    o_send.at[half, 0, 0],
                    o_recv1.at[half],
                    out_device(half, wrap(first + step, NY), second),
                ).start()

    def out_along_second(step):
        for half in range(2):
            first, second = out_here(half)
            for way in range(2):
                if step > hops(NY)[way]:
                    continue
                chunk = obuf.at[half, wrap(second - turn(way) * step, NY)]
                if step:
                    await_bytes(chunk, o_recv2.at[half, way, step - 1])
                if step < 3:
                    out_send2(half, way, step, chunk)
                if step == 2 and way == 0:
                    out_send2(half, way, 3, chunk, 2)

    out_along_first()
    for place in range(1, PAIRS):
        grid.along_first(place)

    def ring_step(step, start):
        def one(place, carry):
            grid.along_second(step, place)
            return carry

        lax.fori_loop(start, PAIRS, one, 0)

    grid.along_second(2, 0)
    ring_step(1, 1)
    for hop in (1, NX - 1):
        await_bytes(tbuf.at[odd, band_at(-hop)], t_recv.at[0, hop])
    token_passed_on(0, sign)
    token_to_sibling(1)
    token_to_sibling(NX - 1)
    ring_step(2, 1)
    for which, by in ((1, 1), (2, -1)):
        for hop in (1, NX - 1):
            await_bytes(
                tbuf.at[other, 2 * wrap(x - hop, NX) + which - 1], t_recv.at[which, hop]
            )
        token_passed_on(which, by)
    await_bytes(tbuf.at[odd, band_at(2)], t_recv.at[0, 2])
    token_to_sibling(2)
    ring_step(3, 0)
    for hop in range(NX):
        from_band = 2 * wrap(x - hop, NX) + 1 - core
        await_bytes(tbuf.at[odd, from_band], s_recv.at[hop])
        if hop == 2:
            for which in range(2):
                await_bytes(
                    tbuf.at[other, 2 * wrap(x - hop, NX) + which], t_recv.at[1 + which, hop]
                )
    ring_step(4, 0)
    await_bytes(wbuf.at[:, along, pair, other], z_recv.at[0])
    for half in range(2):
        await_bytes(obuf.at[half, out_here(half)[1], 0 : NY - 1], o_recv1.at[half])
    out_along_second(0)

    chunk = 2 * NZ * DEPTH

    def project(step, right):
        at = pl.ds(pl.multiple_of(step * chunk, HEAD), chunk)
        qkv_sum[...] += jnp.dot(
            tbuf[:, :, :, at].reshape(ROWS, chunk),
            jnp.concatenate([right(slot) for slot in range(3)], axis=1),
            preferred_element_type=jnp.float32,
        )

    @pl.when(core == 0)
    def _():
        def one(step, carry):
            project(step, lambda slot: wbuf[slot, pl.ds(2 * step, 2)].reshape(chunk, HEAD))
            return carry

        lax.fori_loop(0, NY // 2, one, 0)

    @pl.when(core == 1)
    def _():
        def one(step, carry):
            project(
                step,
                lambda slot: jnp.concatenate(
                    [
                        wbuf[slot, :, step, parity].reshape(chunk // 2, HEAD)
                        for parity in range(2)
                    ],
                    axis=0,
                ),
            )
            return carry

        lax.fori_loop(0, NY // 2, one, 0)

    rounded = qkv_sum[...].astype(jnp.bfloat16)

    msg[...] = (
        jnp.dot(by_peer[...], rounded, preferred_element_type=jnp.float32)
        .reshape(msg.shape)
        .astype(jnp.bfloat16)
    )

    def exchange(stage, source, target):
        def send(step, carry):
            there = lax.rem(me + PEERS // 2 + wander(step) + PEERS, PEERS)
            remote(
                source.at[there], target.at[me], a_send.at[stage], a_recv.at[stage], peer(there)
            ).start()
            return carry

        pltpu.make_async_copy(source.at[me], target.at[me], a_recv.at[stage]).start()
        lax.fori_loop(0, PEERS - 1, send, 0)

    exchange(0, msg, fin)
    spatial = jnp.concatenate(
        [
            attend(
                rounded[at : at + POSITIONS, :HEAD],
                rounded[at : at + POSITIONS, HEAD : 2 * HEAD],
                rounded[at : at + POSITIONS, 2 * HEAD :],
                None,
            )
            for at in (0, POSITIONS)
        ],
        axis=0,
    ).astype(jnp.bfloat16)
    out_along_second(1)

    await_bytes(wbuf.at[:, 0, 0, 0], z_send.at[0])
    await_bytes(tbuf.at[0, 0], z_send.at[1])
    await_bytes(tbuf.at[0, 0], z_send.at[2])
    await_bytes(wbuf.at[:, 0, 0 : PAIRS - 1], w_send.at[0, 0])
    for way in range(2):
        await_bytes(wbuf.at[:, 0 : hops(NY)[way]], w_send.at[1, way])
        await_bytes(obuf.at[way, 0, 0 : NY - 1], o_send.at[way, 0, 0])
    for hop in range(NX):
        await_bytes(tbuf.at[0, 0], s_send.at[hop])
        if hop:
            for which in range(3):
                await_bytes(tbuf.at[0, 0], t_send.at[which, hop])
    await_bytes(fin, a_recv.at[0])
    laid = fin[...].reshape(ROWS, 3 * HEAD)
    mixed = attend(laid[:, :HEAD], laid[:, HEAD : 2 * HEAD], laid[:, 2 * HEAD :], bias[...])
    rmsg[...] = mixed.reshape(rmsg.shape).astype(jnp.bfloat16)
    exchange(1, rmsg, rfin)
    out_along_second(2)
    await_bytes(msg.at[0 : PEERS - 1], a_send.at[0])
    await_bytes(rfin, a_recv.at[1])
    back = jnp.dot(
        by_frame[...], rfin[...].reshape(ROWS, HEAD), preferred_element_type=jnp.float32
    ).astype(jnp.bfloat16)
    temporal = jnp.full((ROWS, HEAD), kind[odd], jnp.int32) == 1
    cbuf[...] = jnp.where(temporal, back, spatial).reshape(cbuf.shape)

    for which, step in ((1, 2), (1, 1), (1, NX - 1), (0, 2), (1, 0), (0, 1), (0, NX - 1)):
        remote(
            cbuf.at[odd if which == 0 else other],
            mbuf.at[band, odd],
            m_send.at[which, step],
            m_recv.at[which, step],
            (frame if which == 0 else beside, band_at(step)),
        ).start()
    remote(
        cbuf.at[odd], mbuf.at[band, odd], n_send.at[0, 0], n_recv.at[0, 0], sibling
    ).start()
    last = pltpu.make_async_copy(cbuf.at[odd], mbuf.at[band, odd], m_recv.at[0, 0])
    last.start()
    for which, hop in ((1, 0), (0, 1), (0, 3), (1, 1), (1, 3), (0, 2), (1, 2)):
        block = mbuf.at[band_at(-hop), odd if which == 0 else other]
        await_bytes(block, m_recv.at[which, hop])
        remote(block, block, n_send.at[which, hop], n_recv.at[which, hop], sibling).start()
    out_along_second(3)
    out_along_second(4)
    last.wait()

    def project_out(source):
        left = jnp.concatenate([mbuf[source, 0], mbuf[source, 1]], axis=1)
        right = jnp.stack([obuf[0, source], obuf[1, :, source]], axis=1).reshape(
            2 * HEAD, WIDTH
        )
        return jnp.dot(left, right, preferred_element_type=jnp.float32)

    def own_core(hop, carry):
        total[...] += project_out(band_at(-hop))
        return carry

    def other_core(hop, carry):
        source = 2 * wrap(x - hop, NX) + 1 - core
        for which in range(2):
            await_bytes(
                mbuf.at[source, sibling_odd if which == 0 else 1 - sibling_odd],
                n_recv.at[which, hop],
            )
        total[...] += project_out(source)
        return carry

    total[...] = jnp.zeros_like(total)
    lax.fori_loop(0, NX, own_core, 0)
    lax.fori_loop(0, NX, other_core, 0)
    sbuf[...] = total[...].astype(jnp.bfloat16).reshape(sbuf.shape)

    def columns(which):
        return out.at[:, pl.ds(pl.multiple_of(which * WIDTH, HEAD), WIDTH)]

    for step in range(1, BANDS):
        there = wrap(band + step, BANDS)
        remote(
            sbuf.at[there], columns(band), f_send.at[step], f_recv.at[step], (frame, there)
        ).start()
    last = pltpu.make_async_copy(sbuf.at[band], columns(band), f_send.at[0])
    last.start()
    for step in range(1, BANDS):
        await_bytes(columns(wrap(band - step, BANDS)), f_recv.at[step])
    last.wait()

    await_bytes(rmsg.at[0 : PEERS - 1], a_send.at[1])
    for which in range(2):
        for hop in range(NX):
            if hop or which:
                await_bytes(cbuf.at[0], m_send.at[which, hop])
            await_bytes(cbuf.at[0], n_send.at[which, hop])
    for half in range(2):
        for way in range(2):
            await_bytes(obuf.at[half, 0 : hops(NY)[way]], o_send.at[half, 1, way])
    for step in range(1, BANDS):
        await_bytes(sbuf.at[0], f_send.at[step])


def body(tokens, qkv_weight, out_weight, head_kind):
    bf16 = jnp.bfloat16
    dma = pltpu.SemaphoreType.DMA
    hbm = pl.BlockSpec(memory_space=pltpu.HBM)
    return pl.pallas_call(
        kernel,
        out_shape=jax.ShapeDtypeStruct(tokens.shape, tokens.dtype),
        in_specs=[hbm] * 4,
        out_specs=hbm,
        scratch_shapes=[
            pltpu.VMEM((3, NY, PAIRS, 2, DEPTH, HEAD), bf16),
            pltpu.VMEM((2, 8, 8, 16, WIDTH), bf16),
            pltpu.VMEM((2, BANDS) + tokens.shape, bf16),
            pltpu.VMEM((PEERS, 2 * SHARE, 3 * HEAD), bf16),
            pltpu.VMEM((PEERS, 2 * SHARE, 3 * HEAD), bf16),
            pltpu.VMEM((PEERS, 2 * SHARE, HEAD), bf16),
            pltpu.VMEM((PEERS, 2 * SHARE, HEAD), bf16),
            pltpu.VMEM((2, POSITIONS, HEAD), bf16),
            pltpu.VMEM((BANDS, 2, POSITIONS, HEAD), bf16),
            pltpu.VMEM((BANDS, 16, WIDTH), bf16),
            pltpu.VMEM((ROWS, 3 * HEAD), jnp.float32),
            pltpu.VMEM((POSITIONS, WIDTH), jnp.float32),
            pltpu.VMEM((ROWS, ROWS), bf16),
            pltpu.VMEM((ROWS, ROWS), bf16),
            pltpu.VMEM((ROWS, ROWS), jnp.float32),
            pltpu.SMEM((2,), jnp.int32),
            pltpu.VMEM((3, DEPTH, HEAD), bf16),
            dma((6,)),
            dma((3,)),
            dma((3,)),
            dma((2, 2)),
            dma((4,)),
            dma((2, 4, 4)),
            dma((2, 2, 2)),
            dma((2,)),
            dma((2, 2, 4)),
            dma((3, NX)),
            dma((3, NX)),
            dma((NX,)),
            dma((NX,)),
            dma((2,)),
            dma((2,)),
            dma((2, NX)),
            dma((2, NX)),
            dma((2, NX)),
            dma((2, NX)),
            dma((BANDS,)),
            dma((BANDS,)),
        ],
        compiler_params=pltpu.CompilerParams(
            collective_id=0, has_side_effects=True, vmem_limit_bytes=64 * 1024 * 1024
        ),
    )(tokens, qkv_weight.transpose(1, 0, 2), out_weight, head_kind)


def solution(mesh):
    return jax.shard_map(
        body,
        mesh=mesh,
        in_specs=(
            P(("frame", "band"), None),
            P("frame", None, "band"),
            P("frame", "band"),
            P("band"),
        ),
        out_specs=P(("frame", "band"), None),
        check_vma=False,
    )
```

```python
import jax
import jax.numpy as jnp
from jax import lax
from jax.experimental import pallas as pl
from jax.experimental.pallas import tpu as pltpu
from jax.sharding import PartitionSpec as P

MESH = pl.DeviceIdType.MESH
NX = 4
NY = 8
NZ = 8
PAIRS = NZ // 2
BANDS = 2 * NX
PEERS = NY * PAIRS
HEAD = 128
POSITIONS = 128
ROWS = 2 * POSITIONS
SHARE = POSITIONS // PEERS
DEPTH = 48
WIDTH = 384


def remote(src, dst, send_sem, recv_sem, device):
    return pltpu.make_async_remote_copy(
        src_ref=src,
        dst_ref=dst,
        send_sem=send_sem,
        recv_sem=recv_sem,
        device_id=device,
        device_id_type=MESH,
    )


def await_bytes(ref, sem):
    pltpu.make_async_copy(ref, ref, sem).wait()


def attend(queries, keys, values, bias):
    scores = lax.dot_general(
        queries, keys, (((1,), (1,)), ((), ())), preferred_element_type=jnp.float32
    ) * (HEAD**-0.5)
    if bias is not None:
        scores = scores + bias
    raised = jnp.exp(scores - jnp.max(scores, axis=-1, keepdims=True))
    probs = (raised / jnp.sum(raised, axis=-1, keepdims=True)).astype(jnp.bfloat16)
    return jnp.dot(probs, values, preferred_element_type=jnp.float32)


def wrap(value, size):
    return lax.rem(value + 8 * size, size)


def hops(size):
    return (size // 2, (size - 1) // 2)


def wander(place):
    if isinstance(place, int):
        return (place + 1) // 2 * (2 * (place % 2) - 1)
    return lax.div(place + 1, 2) * (2 * lax.rem(place, 2) - 1)


class Grid:
    def __init__(self, block, device, here, sizes, sign, sems):
        self.block = block
        self.device = device
        self.first, self.second = here
        self.n_first, self.n_second = sizes
        self.sign = sign
        self.send, self.recv1, self.recv2 = sems

    def turn(self, way, place):
        flip = 1 - 2 * (place // 2 if isinstance(place, int) else lax.div(place, 2))
        return (self.sign if way == 0 else -self.sign) * flip

    def to_second(self, block, way, step, place, by=1):
        there = wrap(self.second + by * self.turn(way, place), self.n_second)
        remote(
            block,
            block,
            self.send.at[1, way],
            self.recv2.at[way, step, place],
            self.device(self.first, there),
        ).start()

    def begin(self, src, dst, device):
        for way in range(2):
            there = wrap(self.second + self.turn(way, 0), self.n_second)
            remote(
                src,
                dst,
                self.send.at[1, way],
                self.recv2.at[way, 0, 0],
                device(self.first, there),
            ).start()
        for place in range(1, self.n_first):
            there = wrap(self.first + self.sign * wander(place), self.n_first)
            remote(
                src,
                dst,
                self.send.at[0, 0],
                self.recv1.at[place],
                device(there, self.second),
            ).start()

    def along_first(self, place):
        block = self.block(
            wrap(self.first - self.sign * wander(place), self.n_first), self.second
        )
        await_bytes(block, self.recv1.at[place])
        for way in range(2):
            self.to_second(block, way, 0, place)

    def along_second(self, step, place):
        for way in range(2):
            if step > hops(self.n_second)[way]:
                continue
            block = self.block(
                wrap(self.first - self.sign * wander(place), self.n_first),
                wrap(self.second - self.turn(way, place) * step, self.n_second),
            )
            await_bytes(block, self.recv2.at[way, step - 1, place])
            if step < 3:
                self.to_second(block, way, step, place)
            if step == 2 and way == 0:
                self.to_second(block, way, 3, place, 2)


def kernel(
    tokens,
    qkv,
    out_weight,
    kind_hbm,
    out,
    wbuf,
    obuf,
    tbuf,
    msg,
    fin,
    rmsg,
    rfin,
    cbuf,
    mbuf,
    sbuf,
    qkv_sum,
    total,
    by_peer,
    by_frame,
    bias,
    kind,
    cross,
    own_sem,
    z_send,
    z_recv,
    w_send,
    w_recv1,
    w_recv2,
    o_send,
    o_recv1,
    o_recv2,
    t_send,
    t_recv,
    s_send,
    s_recv,
    a_send,
    a_recv,
    m_send,
    m_recv,
    n_send,
    n_recv,
    f_send,
    f_recv,
):
    frame = lax.axis_index("frame")
    band = lax.axis_index("band")
    y, z = lax.div(frame, NZ), lax.rem(frame, NZ)
    x, core = lax.div(band, 2), lax.rem(band, 2)
    across = z + (y - z) * core
    along = y + (z - y) * core
    pair, odd = lax.div(across, 2), lax.rem(across, 2)
    other = 1 - odd
    sign = 1 - 2 * core
    sibling_band = 2 * x + 1 - core
    sibling = (frame, sibling_band)
    sibling_odd = lax.rem(y + (z - y) * core, 2)
    me = along * PAIRS + pair

    def frame_at(along_there, across_there):
        return along_there * (NZ - (NZ - 1) * core) + across_there * (1 + (NZ - 1) * core)

    beside = frame_at(along, 2 * pair + other)

    def band_at(step):
        return 2 * wrap(x + step, NX) + core

    def peer(index):
        return (frame_at(lax.div(index, PAIRS), 2 * lax.rem(index, PAIRS) + odd), band)

    def head_columns(which):
        return qkv.at[:, :, pl.ds(pl.multiple_of(which * HEAD, HEAD), HEAD)]

    own = [
        pltpu.make_async_copy(head_columns(odd), wbuf.at[:, along, pair, odd], own_sem.at[0]),
        pltpu.make_async_copy(out_weight.at[0:16], obuf.at[0, y, z], own_sem.at[1]),
        pltpu.make_async_copy(out_weight.at[16:32], obuf.at[1, z, y], own_sem.at[2]),
        pltpu.make_async_copy(tokens, tbuf.at[odd, band], own_sem.at[3]),
        pltpu.make_async_copy(kind_hbm, kind, own_sem.at[4]),
        pltpu.make_async_copy(head_columns(other), cross, own_sem.at[5]),
    ]
    for copy in own:
        copy.start()

    barrier = pltpu.get_barrier_semaphore()

    def greet(device):
        pl.semaphore_signal(barrier, inc=1, device_id=device, device_id_type=MESH)

    greet(sibling)
    greet((beside, sibling_band))
    for step in range(1, NY):
        greet((y * NZ + wrap(z + step, NZ), band))
        greet((wrap(y + step, NY) * NZ + z, band))
    for step in (1, -1):
        greet((frame_at(wrap(along + step, NY), 2 * pair + other), band))
    for step in range(1, NX):
        greet((frame, band_at(step)))

    pl.semaphore_wait(barrier, 2 + NY - 1 + NZ - 1 + 2 + NX - 1)

    own[0].wait()
    own[5].wait()

    grid = Grid(
        lambda first, second: wbuf.at[:, second, first],
        lambda first, second: (frame_at(second, 2 * first + odd), band),
        (pair, along),
        (PAIRS, NY),
        sign,
        (w_send, w_recv1, w_recv2),
    )

    def token_along_x(which, block):
        for step in (1, NX - 1):
            remote(
                block, block, t_send.at[which, step], t_recv.at[which, step], (frame, band_at(step))
            ).start()

    def token_passed_on(which, by):
        if which == 0:
            block = tbuf.at[odd, band_at(-by)]
        else:
            block = tbuf.at[other, 2 * wrap(x - by, NX) + which - 1]
        remote(
            block, block, t_send.at[which, 2], t_recv.at[which, 2], (frame, band_at(by))
        ).start()

    def token_to_sibling(hop):
        from_band = band_at(-hop)
        remote(
            tbuf.at[odd, from_band],
            tbuf.at[sibling_odd, from_band],
            s_send.at[hop],
            s_recv.at[hop],
            sibling,
        ).start()

    here = wbuf.at[:, along, pair, odd]
    grid.begin(here, here, grid.device)
    grid.begin(
        cross, here, lambda first, second: (frame_at(second, 2 * first + other), band)
    )
    remote(cross, here, z_send.at[0], z_recv.at[0], (beside, band)).start()
    beside_z = y * NZ + z + 1 - 2 * lax.rem(z, 2)
    beside_y = (y + 1 - 2 * lax.rem(y, 2)) * NZ + z
    remote(
        tokens, tbuf.at[lax.rem(z, 2), band], z_send.at[1], z_recv.at[1 + core], (beside_z, 2 * x)
    ).start()
    remote(
        tokens, tbuf.at[lax.rem(y, 2), band], z_send.at[2], z_recv.at[1 + core], (beside_y, 2 * x + 1)
    ).start()
    for copy in own[1:5]:
        copy.wait()
    token_along_x(0, tbuf.at[odd, band])
    remote(
        tbuf.at[odd, band], tbuf.at[sibling_odd, band], s_send.at[0], s_recv.at[0], sibling
    ).start()

    tall = lax.broadcasted_iota(jnp.int32, (ROWS, ROWS), 0)
    wide = lax.broadcasted_iota(jnp.int32, (ROWS, ROWS), 1)

    def origin(row):
        return (
            lax.rem(lax.div(row, SHARE), 2) * POSITIONS
            + lax.div(row, 2 * SHARE) * SHARE
            + lax.rem(row, SHARE)
        )

    qkv_sum[...] = jnp.zeros_like(qkv_sum)
    by_peer[...] = jnp.where(wide == origin(tall), 1.0, 0.0).astype(jnp.bfloat16)
    by_frame[...] = jnp.where(tall == origin(wide), 1.0, 0.0).astype(jnp.bfloat16)
    bias[...] = jnp.where(lax.rem(tall, SHARE) == lax.rem(wide, SHARE), 0.0, -1e30)

    for which in range(2):
        await_bytes(tbuf.at[other, 2 * x + which], z_recv.at[1 + which])
        token_along_x(1 + which, tbuf.at[other, 2 * x + which])

    def out_here(half):
        return (z, y) if half == 0 else (y, z)

    def out_device(half, first, second):
        return (second * NZ + first if half == 0 else first * NZ + second, band)

    def turn(way):
        return sign if way == 0 else -sign

    def out_send2(half, way, step, chunk, by=1):
        first, second = out_here(half)
        there = wrap(second + by * turn(way), NY)
        remote(
            chunk,
            chunk,
            o_send.at[half, 1, way],
            o_recv2.at[half, way, step],
            out_device(half, first, there),
        ).start()

    def out_to_first(half, block, by, sem):
        first, second = out_here(half)
        remote(
            block,
            block,
            o_send.at[half, 0, 0],
            o_recv1.at[half, sem],
            out_device(half, wrap(first + by, NY), second),
        ).start()

    def out_along_first():
        for half in range(2):
            first, second = out_here(half)
            block = obuf.at[half, second, first]
            out_to_first(half, block, 2 * sign, 0)
            out_to_first(half, block, -2 * sign, 1)
            out_to_first(half, block, sign, 2)
            out_to_first(half, block, -sign, 2)

    def out_beyond():
        for half in range(2):
            first, second = out_here(half)
            block = obuf.at[half, second, wrap(first - 2 * sign, NY)]
            await_bytes(block, o_recv1.at[half, 0])
            out_to_first(half, block, 2 * sign, 2)
            out_to_first(half, block, sign, 2)
            block = obuf.at[half, second, wrap(first + 2 * sign, NY)]
            await_bytes(block, o_recv1.at[half, 1])
            out_to_first(half, block, -sign, 2)

    def out_along_second(step):
        for half in range(2):
            first, second = out_here(half)
            for way in range(2):
                if step > hops(NY)[way]:
                    continue
                chunk = obuf.at[half, wrap(second - turn(way) * step, NY)]
                if step:
                    await_bytes(chunk, o_recv2.at[half, way, step - 1])
                if step < 3:
                    out_send2(half, way, step, chunk)
                if step == 2 and way == 0:
                    out_send2(half, way, 3, chunk, 2)

    out_along_first()
    for place in range(1, PAIRS):
        grid.along_first(place)

    def ring_step(step):
        def one(place, carry):
            grid.along_second(step, place)
            return carry

        lax.fori_loop(0, PAIRS, one, 0)

    ring_step(1)
    out_beyond()
    for hop in (1, NX - 1):
        await_bytes(tbuf.at[odd, band_at(-hop)], t_recv.at[0, hop])
    token_passed_on(0, sign)
    token_to_sibling(1)
    token_to_sibling(NX - 1)
    ring_step(2)
    for which, by in ((1, 1), (2, -1)):
        for hop in (1, NX - 1):
            await_bytes(
                tbuf.at[other, 2 * wrap(x - hop, NX) + which - 1], t_recv.at[which, hop]
            )
        token_passed_on(which, by)
    await_bytes(tbuf.at[odd, band_at(2)], t_recv.at[0, 2])
    token_to_sibling(2)
    ring_step(3)
    for hop in range(NX):
        from_band = 2 * wrap(x - hop, NX) + 1 - core
        await_bytes(tbuf.at[odd, from_band], s_recv.at[hop])
        if hop == 2:
            for which in range(2):
                await_bytes(
                    tbuf.at[other, 2 * wrap(x - hop, NX) + which], t_recv.at[1 + which, hop]
                )
    ring_step(4)
    await_bytes(wbuf.at[:, along, pair, other], z_recv.at[0])
    for half in range(2):
        await_bytes(obuf.at[half, out_here(half)[1], 0 : NY - 3], o_recv1.at[half, 2])
    out_along_second(0)

    chunk = 2 * NZ * DEPTH

    def project(step, right):
        at = pl.ds(pl.multiple_of(step * chunk, HEAD), chunk)
        qkv_sum[...] += jnp.dot(
            tbuf[:, :, :, at].reshape(ROWS, chunk),
            jnp.concatenate([right(slot) for slot in range(3)], axis=1),
            preferred_element_type=jnp.float32,
        )

    @pl.when(core == 0)
    def _():
        def one(step, carry):
            project(step, lambda slot: wbuf[slot, pl.ds(2 * step, 2)].reshape(chunk, HEAD))
            return carry

        lax.fori_loop(0, NY // 2, one, 0)

    @pl.when(core == 1)
    def _():
        def one(step, carry):
            project(
                step,
                lambda slot: jnp.concatenate(
                    [
                        wbuf[slot, :, step, parity].reshape(chunk // 2, HEAD)
                        for parity in range(2)
                    ],
                    axis=0,
                ),
            )
            return carry

        lax.fori_loop(0, NY // 2, one, 0)

    rounded = qkv_sum[...].astype(jnp.bfloat16)

    msg[...] = (
        jnp.dot(by_peer[...], rounded, preferred_element_type=jnp.float32)
        .reshape(msg.shape)
        .astype(jnp.bfloat16)
    )

    def exchange(stage, source, target):
        def send(step, carry):
            there = lax.rem(me + PEERS // 2 + wander(step) + PEERS, PEERS)
            remote(
                source.at[there], target.at[me], a_send.at[stage], a_recv.at[stage], peer(there)
            ).start()
            return carry

        pltpu.make_async_copy(source.at[me], target.at[me], a_recv.at[stage]).start()
        lax.fori_loop(0, PEERS - 1, send, 0)

    exchange(0, msg, fin)
    spatial = jnp.concatenate(
        [
            attend(
                rounded[at : at + POSITIONS, :HEAD],
                rounded[at : at + POSITIONS, HEAD : 2 * HEAD],
                rounded[at : at + POSITIONS, 2 * HEAD :],
                None,
            )
            for at in (0, POSITIONS)
        ],
        axis=0,
    ).astype(jnp.bfloat16)
    out_along_second(1)

    await_bytes(wbuf.at[:, 0, 0, 0], z_send.at[0])
    await_bytes(tbuf.at[0, 0], z_send.at[1])
    await_bytes(tbuf.at[0, 0], z_send.at[2])
    await_bytes(wbuf.at[:, 0, 0 : PAIRS - 1], w_send.at[0, 0])
    for way in range(2):
        await_bytes(wbuf.at[:, 0 : hops(NY)[way]], w_send.at[1, way])
        await_bytes(obuf.at[way, 0, 0 : NY - 1], o_send.at[way, 0, 0])
    for hop in range(NX):
        await_bytes(tbuf.at[0, 0], s_send.at[hop])
        if hop:
            for which in range(3):
                await_bytes(tbuf.at[0, 0], t_send.at[which, hop])
    await_bytes(fin, a_recv.at[0])
    laid = fin[...].reshape(ROWS, 3 * HEAD)
    mixed = attend(laid[:, :HEAD], laid[:, HEAD : 2 * HEAD], laid[:, 2 * HEAD :], bias[...])
    rmsg[...] = mixed.reshape(rmsg.shape).astype(jnp.bfloat16)
    exchange(1, rmsg, rfin)
    out_along_second(2)
    await_bytes(msg.at[0 : PEERS - 1], a_send.at[0])
    await_bytes(rfin, a_recv.at[1])
    back = jnp.dot(
        by_frame[...], rfin[...].reshape(ROWS, HEAD), preferred_element_type=jnp.float32
    ).astype(jnp.bfloat16)
    temporal = jnp.full((ROWS, HEAD), kind[odd], jnp.int32) == 1
    cbuf[...] = jnp.where(temporal, back, spatial).reshape(cbuf.shape)

    for which, step in ((1, 2), (1, 1), (1, NX - 1), (0, 2), (1, 0), (0, 1), (0, NX - 1)):
        remote(
            cbuf.at[odd if which == 0 else other],
            mbuf.at[band, odd],
            m_send.at[which, step],
            m_recv.at[which, step],
            (frame if which == 0 else beside, band_at(step)),
        ).start()
    remote(
        cbuf.at[odd], mbuf.at[band, odd], n_send.at[0, 0], n_recv.at[0, 0], sibling
    ).start()
    last = pltpu.make_async_copy(cbuf.at[odd], mbuf.at[band, odd], m_recv.at[0, 0])
    last.start()
    for which, hop in ((1, 0), (0, 1), (0, 3), (1, 1), (1, 3), (0, 2), (1, 2)):
        block = mbuf.at[band_at(-hop), odd if which == 0 else other]
        await_bytes(block, m_recv.at[which, hop])
        remote(block, block, n_send.at[which, hop], n_recv.at[which, hop], sibling).start()
    out_along_second(3)
    out_along_second(4)
    last.wait()

    def project_out(source):
        left = jnp.concatenate([mbuf[source, 0], mbuf[source, 1]], axis=1)
        right = jnp.stack([obuf[0, source], obuf[1, :, source]], axis=1).reshape(
            2 * HEAD, WIDTH
        )
        return jnp.dot(left, right, preferred_element_type=jnp.float32)

    def own_core(hop, carry):
        total[...] += project_out(band_at(-hop))
        return carry

    def other_core(hop, carry):
        source = 2 * wrap(x - hop, NX) + 1 - core
        for which in range(2):
            await_bytes(
                mbuf.at[source, sibling_odd if which == 0 else 1 - sibling_odd],
                n_recv.at[which, hop],
            )
        total[...] += project_out(source)
        return carry

    total[...] = jnp.zeros_like(total)
    lax.fori_loop(0, NX, own_core, 0)
    lax.fori_loop(0, NX, other_core, 0)
    sbuf[...] = total[...].astype(jnp.bfloat16).reshape(sbuf.shape)

    def columns(which):
        return out.at[:, pl.ds(pl.multiple_of(which * WIDTH, HEAD), WIDTH)]

    for step in range(1, BANDS):
        there = wrap(band + step, BANDS)
        remote(
            sbuf.at[there], columns(band), f_send.at[step], f_recv.at[step], (frame, there)
        ).start()
    last = pltpu.make_async_copy(sbuf.at[band], columns(band), f_send.at[0])
    last.start()
    for step in range(1, BANDS):
        await_bytes(columns(wrap(band - step, BANDS)), f_recv.at[step])
    last.wait()

    await_bytes(rmsg.at[0 : PEERS - 1], a_send.at[1])
    for which in range(2):
        for hop in range(NX):
            if hop or which:
                await_bytes(cbuf.at[0], m_send.at[which, hop])
            await_bytes(cbuf.at[0], n_send.at[which, hop])
    for half in range(2):
        for way in range(2):
            await_bytes(obuf.at[half, 0 : hops(NY)[way]], o_send.at[half, 1, way])
    for step in range(1, BANDS):
        await_bytes(sbuf.at[0], f_send.at[step])


def body(tokens, qkv_weight, out_weight, head_kind):
    bf16 = jnp.bfloat16
    dma = pltpu.SemaphoreType.DMA
    hbm = pl.BlockSpec(memory_space=pltpu.HBM)
    return pl.pallas_call(
        kernel,
        out_shape=jax.ShapeDtypeStruct(tokens.shape, tokens.dtype),
        in_specs=[hbm] * 4,
        out_specs=hbm,
        scratch_shapes=[
            pltpu.VMEM((3, NY, PAIRS, 2, DEPTH, HEAD), bf16),
            pltpu.VMEM((2, 8, 8, 16, WIDTH), bf16),
            pltpu.VMEM((2, BANDS) + tokens.shape, bf16),
            pltpu.VMEM((PEERS, 2 * SHARE, 3 * HEAD), bf16),
            pltpu.VMEM((PEERS, 2 * SHARE, 3 * HEAD), bf16),
            pltpu.VMEM((PEERS, 2 * SHARE, HEAD), bf16),
            pltpu.VMEM((PEERS, 2 * SHARE, HEAD), bf16),
            pltpu.VMEM((2, POSITIONS, HEAD), bf16),
            pltpu.VMEM((BANDS, 2, POSITIONS, HEAD), bf16),
            pltpu.VMEM((BANDS, 16, WIDTH), bf16),
            pltpu.VMEM((ROWS, 3 * HEAD), jnp.float32),
            pltpu.VMEM((POSITIONS, WIDTH), jnp.float32),
            pltpu.VMEM((ROWS, ROWS), bf16),
            pltpu.VMEM((ROWS, ROWS), bf16),
            pltpu.VMEM((ROWS, ROWS), jnp.float32),
            pltpu.SMEM((2,), jnp.int32),
            pltpu.VMEM((3, DEPTH, HEAD), bf16),
            dma((6,)),
            dma((3,)),
            dma((3,)),
            dma((2, 2)),
            dma((4,)),
            dma((2, 4, 4)),
            dma((2, 2, 2)),
            dma((2, 3)),
            dma((2, 2, 4)),
            dma((3, NX)),
            dma((3, NX)),
            dma((NX,)),
            dma((NX,)),
            dma((2,)),
            dma((2,)),
            dma((2, NX)),
            dma((2, NX)),
            dma((2, NX)),
            dma((2, NX)),
            dma((BANDS,)),
            dma((BANDS,)),
        ],
        compiler_params=pltpu.CompilerParams(
            collective_id=0, has_side_effects=True, vmem_limit_bytes=64 * 1024 * 1024
        ),
    )(tokens, qkv_weight.transpose(1, 0, 2), out_weight, head_kind)


def solution(mesh):
    return jax.shard_map(
        body,
        mesh=mesh,
        in_specs=(
            P(("frame", "band"), None),
            P("frame", None, "band"),
            P("frame", "band"),
            P("band"),
        ),
        out_specs=P(("frame", "band"), None),
        check_vma=False,
    )
```

```python
import jax
import jax.numpy as jnp
from jax import lax
from jax.experimental import pallas as pl
from jax.experimental.pallas import tpu as pltpu
from jax.sharding import PartitionSpec as P

MESH = pl.DeviceIdType.MESH
NX = 4
NY = 8
NZ = 8
PAIRS = NZ // 2
BANDS = 2 * NX
PEERS = NY * PAIRS
HEAD = 128
POSITIONS = 128
ROWS = 2 * POSITIONS
SHARE = POSITIONS // PEERS
DEPTH = 48
WIDTH = 384


def remote(src, dst, send_sem, recv_sem, device):
    return pltpu.make_async_remote_copy(
        src_ref=src,
        dst_ref=dst,
        send_sem=send_sem,
        recv_sem=recv_sem,
        device_id=device,
        device_id_type=MESH,
    )


def await_bytes(ref, sem):
    pltpu.make_async_copy(ref, ref, sem).wait()


def attend(queries, keys, values, bias):
    scores = lax.dot_general(
        queries, keys, (((1,), (1,)), ((), ())), preferred_element_type=jnp.float32
    ) * (HEAD**-0.5)
    if bias is not None:
        scores = scores + bias
    raised = jnp.exp(scores - jnp.max(scores, axis=-1, keepdims=True))
    probs = (raised / jnp.sum(raised, axis=-1, keepdims=True)).astype(jnp.bfloat16)
    return jnp.dot(probs, values, preferred_element_type=jnp.float32)


def wrap(value, size):
    return lax.rem(value + 8 * size, size)


def hops(size):
    return (size // 2, (size - 1) // 2)


def wander(place):
    if isinstance(place, int):
        return (place + 1) // 2 * (2 * (place % 2) - 1)
    return lax.div(place + 1, 2) * (2 * lax.rem(place, 2) - 1)


class Grid:
    def __init__(self, block, device, here, sizes, sign, sems):
        self.block = block
        self.device = device
        self.first, self.second = here
        self.n_first, self.n_second = sizes
        self.sign = sign
        self.send, self.recv1, self.recv2 = sems

    def turn(self, way, place):
        flip = 1 - 2 * (place // 2 if isinstance(place, int) else lax.div(place, 2))
        return (self.sign if way == 0 else -self.sign) * flip

    def to_second(self, block, way, step, place, by=1):
        there = wrap(self.second + by * self.turn(way, place), self.n_second)
        remote(
            block,
            block,
            self.send.at[1, way],
            self.recv2.at[way, step, place],
            self.device(self.first, there),
        ).start()

    def begin(self, src, dst, device):
        for way in range(2):
            there = wrap(self.second + self.turn(way, 0), self.n_second)
            remote(
                src,
                dst,
                self.send.at[1, way],
                self.recv2.at[way, 0, 0],
                device(self.first, there),
            ).start()
        for place in range(1, self.n_first):
            there = wrap(self.first + self.sign * wander(place), self.n_first)
            remote(
                src,
                dst,
                self.send.at[0, 0],
                self.recv1.at[place],
                device(there, self.second),
            ).start()

    def along_first(self, place):
        block = self.block(
            wrap(self.first - self.sign * wander(place), self.n_first), self.second
        )
        await_bytes(block, self.recv1.at[place])
        for way in range(2):
            self.to_second(block, way, 0, place)

    def along_second(self, step, place):
        for way in range(2):
            if step > hops(self.n_second)[way]:
                continue
            block = self.block(
                wrap(self.first - self.sign * wander(place), self.n_first),
                wrap(self.second - self.turn(way, place) * step, self.n_second),
            )
            await_bytes(block, self.recv2.at[way, step - 1, place])
            if step < 3:
                self.to_second(block, way, step, place)
            if step == 2 and way == 0:
                self.to_second(block, way, 3, place, 2)


def kernel(
    tokens,
    qkv,
    out_weight,
    kind_hbm,
    out,
    wbuf,
    obuf,
    tbuf,
    msg,
    fin,
    rmsg,
    rfin,
    cbuf,
    mbuf,
    sbuf,
    qkv_sum,
    total,
    by_peer,
    by_frame,
    bias,
    kind,
    cross,
    own_sem,
    z_send,
    z_recv,
    w_send,
    w_recv1,
    w_recv2,
    o_send,
    o_recv1,
    o_recv2,
    t_send,
    t_recv,
    s_send,
    s_recv,
    a_send,
    a_recv,
    m_send,
    m_recv,
    n_send,
    n_recv,
    f_send,
    f_recv,
):
    frame = lax.axis_index("frame")
    band = lax.axis_index("band")
    y, z = lax.div(frame, NZ), lax.rem(frame, NZ)
    x, core = lax.div(band, 2), lax.rem(band, 2)
    across = z + (y - z) * core
    along = y + (z - y) * core
    pair, odd = lax.div(across, 2), lax.rem(across, 2)
    other = 1 - odd
    sign = 1 - 2 * core
    sibling_band = 2 * x + 1 - core
    sibling = (frame, sibling_band)
    sibling_odd = lax.rem(y + (z - y) * core, 2)
    me = along * PAIRS + pair

    def frame_at(along_there, across_there):
        return along_there * (NZ - (NZ - 1) * core) + across_there * (1 + (NZ - 1) * core)

    beside = frame_at(along, 2 * pair + other)

    def band_at(step):
        return 2 * wrap(x + step, NX) + core

    def peer(index):
        return (frame_at(lax.div(index, PAIRS), 2 * lax.rem(index, PAIRS) + odd), band)

    def head_columns(which):
        return qkv.at[:, :, pl.ds(pl.multiple_of(which * HEAD, HEAD), HEAD)]

    own = [
        pltpu.make_async_copy(head_columns(odd), wbuf.at[:, along, pair, odd], own_sem.at[0]),
        pltpu.make_async_copy(out_weight.at[0:16], obuf.at[0, y, z], own_sem.at[1]),
        pltpu.make_async_copy(out_weight.at[16:32], obuf.at[1, z, y], own_sem.at[2]),
        pltpu.make_async_copy(tokens, tbuf.at[odd, band], own_sem.at[3]),
        pltpu.make_async_copy(kind_hbm, kind, own_sem.at[4]),
        pltpu.make_async_copy(head_columns(other), cross, own_sem.at[5]),
    ]
    for copy in own:
        copy.start()

    barrier = pltpu.get_barrier_semaphore()

    def greet(device):
        pl.semaphore_signal(barrier, inc=1, device_id=device, device_id_type=MESH)

    greet(sibling)
    greet((beside, sibling_band))
    for step in range(1, NY):
        greet((y * NZ + wrap(z + step, NZ), band))
        greet((wrap(y + step, NY) * NZ + z, band))
    for step in (1, -1):
        greet((frame_at(wrap(along + step, NY), 2 * pair + other), band))
    for step in range(1, NX):
        greet((frame, band_at(step)))

    pl.semaphore_wait(barrier, 2 + NY - 1 + NZ - 1 + 2 + NX - 1)

    own[0].wait()
    own[5].wait()

    grid = Grid(
        lambda first, second: wbuf.at[:, second, first],
        lambda first, second: (frame_at(second, 2 * first + odd), band),
        (pair, along),
        (PAIRS, NY),
        sign,
        (w_send, w_recv1, w_recv2),
    )

    def token_along_x(which, block):
        for step in (1, NX - 1):
            remote(
                block, block, t_send.at[which, step], t_recv.at[which, step], (frame, band_at(step))
            ).start()

    def token_passed_on(which, by):
        if which == 0:
            block = tbuf.at[odd, band_at(-by)]
        else:
            block = tbuf.at[other, 2 * wrap(x - by, NX) + which - 1]
        remote(
            block, block, t_send.at[which, 2], t_recv.at[which, 2], (frame, band_at(by))
        ).start()

    def token_to_sibling(hop):
        from_band = band_at(-hop)
        remote(
            tbuf.at[odd, from_band],
            tbuf.at[sibling_odd, from_band],
            s_send.at[hop],
            s_recv.at[hop],
            sibling,
        ).start()

    here = wbuf.at[:, along, pair, odd]
    grid.begin(here, here, grid.device)
    beside_z = y * NZ + z + 1 - 2 * lax.rem(z, 2)
    beside_y = (y + 1 - 2 * lax.rem(y, 2)) * NZ + z
    remote(
        tokens, tbuf.at[lax.rem(z, 2), band], z_send.at[1], z_recv.at[1 + core], (beside_z, 2 * x)
    ).start()
    remote(
        tokens, tbuf.at[lax.rem(y, 2), band], z_send.at[2], z_recv.at[1 + core], (beside_y, 2 * x + 1)
    ).start()
    grid.begin(
        cross, here, lambda first, second: (frame_at(second, 2 * first + other), band)
    )
    remote(cross, here, z_send.at[0], z_recv.at[0], (beside, band)).start()
    for copy in own[1:5]:
        copy.wait()
    token_along_x(0, tbuf.at[odd, band])
    remote(
        tbuf.at[odd, band], tbuf.at[sibling_odd, band], s_send.at[0], s_recv.at[0], sibling
    ).start()

    tall = lax.broadcasted_iota(jnp.int32, (ROWS, ROWS), 0)
    wide = lax.broadcasted_iota(jnp.int32, (ROWS, ROWS), 1)

    def origin(row):
        return (
            lax.rem(lax.div(row, SHARE), 2) * POSITIONS
            + lax.div(row, 2 * SHARE) * SHARE
            + lax.rem(row, SHARE)
        )

    qkv_sum[...] = jnp.zeros_like(qkv_sum)
    by_peer[...] = jnp.where(wide == origin(tall), 1.0, 0.0).astype(jnp.bfloat16)
    by_frame[...] = jnp.where(tall == origin(wide), 1.0, 0.0).astype(jnp.bfloat16)
    bias[...] = jnp.where(lax.rem(tall, SHARE) == lax.rem(wide, SHARE), 0.0, -1e30)

    for which in range(2):
        await_bytes(tbuf.at[other, 2 * x + which], z_recv.at[1 + which])
        token_along_x(1 + which, tbuf.at[other, 2 * x + which])

    def out_here(half):
        return (z, y) if half == 0 else (y, z)

    def out_device(half, first, second):
        return (second * NZ + first if half == 0 else first * NZ + second, band)

    def turn(way):
        return sign if way == 0 else -sign

    def out_send2(half, way, step, chunk, by=1):
        first, second = out_here(half)
        there = wrap(second + by * turn(way), NY)
        remote(
            chunk,
            chunk,
            o_send.at[half, 1, way],
            o_recv2.at[half, way, step],
            out_device(half, first, there),
        ).start()

    def out_to_first(half, block, by, sem):
        first, second = out_here(half)
        remote(
            block,
            block,
            o_send.at[half, 0, 0],
            o_recv1.at[half, sem],
            out_device(half, wrap(first + by, NY), second),
        ).start()

    def out_along_first():
        for half in range(2):
            first, second = out_here(half)
            block = obuf.at[half, second, first]
            out_to_first(half, block, 2 * sign, 0)
            out_to_first(half, block, -2 * sign, 1)
            out_to_first(half, block, sign, 2)
            out_to_first(half, block, -sign, 2)

    def out_beyond():
        for half in range(2):
            first, second = out_here(half)
            block = obuf.at[half, second, wrap(first - 2 * sign, NY)]
            await_bytes(block, o_recv1.at[half, 0])
            out_to_first(half, block, 2 * sign, 2)
            out_to_first(half, block, sign, 2)
            block = obuf.at[half, second, wrap(first + 2 * sign, NY)]
            await_bytes(block, o_recv1.at[half, 1])
            out_to_first(half, block, -sign, 2)

    def out_along_second(step):
        for half in range(2):
            first, second = out_here(half)
            for way in range(2):
                if step > hops(NY)[way]:
                    continue
                chunk = obuf.at[half, wrap(second - turn(way) * step, NY)]
                if step:
                    await_bytes(chunk, o_recv2.at[half, way, step - 1])
                if step < 3:
                    out_send2(half, way, step, chunk)
                if step == 2 and way == 0:
                    out_send2(half, way, 3, chunk, 2)

    out_along_first()
    for place in range(1, PAIRS):
        grid.along_first(place)

    def ring_step(step):
        def one(place, carry):
            grid.along_second(step, place)
            return carry

        lax.fori_loop(0, PAIRS, one, 0)

    ring_step(1)
    out_beyond()
    for hop in (1, NX - 1):
        await_bytes(tbuf.at[odd, band_at(-hop)], t_recv.at[0, hop])
    token_passed_on(0, sign)
    token_to_sibling(1)
    token_to_sibling(NX - 1)
    ring_step(2)
    for which, by in ((1, 1), (2, -1)):
        for hop in (1, NX - 1):
            await_bytes(
                tbuf.at[other, 2 * wrap(x - hop, NX) + which - 1], t_recv.at[which, hop]
            )
        token_passed_on(which, by)
    await_bytes(tbuf.at[odd, band_at(2)], t_recv.at[0, 2])
    token_to_sibling(2)
    ring_step(3)
    for hop in range(NX):
        from_band = 2 * wrap(x - hop, NX) + 1 - core
        await_bytes(tbuf.at[odd, from_band], s_recv.at[hop])
        if hop == 2:
            for which in range(2):
                await_bytes(
                    tbuf.at[other, 2 * wrap(x - hop, NX) + which], t_recv.at[1 + which, hop]
                )
    ring_step(4)
    await_bytes(wbuf.at[:, along, pair, other], z_recv.at[0])
    for half in range(2):
        await_bytes(obuf.at[half, out_here(half)[1], 0 : NY - 3], o_recv1.at[half, 2])
    out_along_second(0)

    chunk = 2 * NZ * DEPTH

    def project(step, right):
        at = pl.ds(pl.multiple_of(step * chunk, HEAD), chunk)
        qkv_sum[...] += jnp.dot(
            tbuf[:, :, :, at].reshape(ROWS, chunk),
            jnp.concatenate([right(slot) for slot in range(3)], axis=1),
            preferred_element_type=jnp.float32,
        )

    @pl.when(core == 0)
    def _():
        def one(step, carry):
            project(step, lambda slot: wbuf[slot, pl.ds(2 * step, 2)].reshape(chunk, HEAD))
            return carry

        lax.fori_loop(0, NY // 2, one, 0)

    @pl.when(core == 1)
    def _():
        def one(step, carry):
            project(
                step,
                lambda slot: jnp.concatenate(
                    [
                        wbuf[slot, :, step, parity].reshape(chunk // 2, HEAD)
                        for parity in range(2)
                    ],
                    axis=0,
                ),
            )
            return carry

        lax.fori_loop(0, NY // 2, one, 0)

    rounded = qkv_sum[...].astype(jnp.bfloat16)

    msg[...] = (
        jnp.dot(by_peer[...], rounded, preferred_element_type=jnp.float32)
        .reshape(msg.shape)
        .astype(jnp.bfloat16)
    )

    def exchange(stage, source, target):
        def send(step, carry):
            there = lax.rem(me + PEERS // 2 + wander(step) + PEERS, PEERS)
            remote(
                source.at[there], target.at[me], a_send.at[stage], a_recv.at[stage], peer(there)
            ).start()
            return carry

        pltpu.make_async_copy(source.at[me], target.at[me], a_recv.at[stage]).start()
        lax.fori_loop(0, PEERS - 1, send, 0)

    exchange(0, msg, fin)
    spatial = jnp.concatenate(
        [
            attend(
                rounded[at : at + POSITIONS, :HEAD],
                rounded[at : at + POSITIONS, HEAD : 2 * HEAD],
                rounded[at : at + POSITIONS, 2 * HEAD :],
                None,
            )
            for at in (0, POSITIONS)
        ],
        axis=0,
    ).astype(jnp.bfloat16)
    out_along_second(1)

    await_bytes(wbuf.at[:, 0, 0, 0], z_send.at[0])
    await_bytes(tbuf.at[0, 0], z_send.at[1])
    await_bytes(tbuf.at[0, 0], z_send.at[2])
    await_bytes(wbuf.at[:, 0, 0 : PAIRS - 1], w_send.at[0, 0])
    for way in range(2):
        await_bytes(wbuf.at[:, 0 : hops(NY)[way]], w_send.at[1, way])
        await_bytes(obuf.at[way, 0, 0 : NY - 1], o_send.at[way, 0, 0])
    for hop in range(NX):
        await_bytes(tbuf.at[0, 0], s_send.at[hop])
        if hop:
            for which in range(3):
                await_bytes(tbuf.at[0, 0], t_send.at[which, hop])
    await_bytes(fin, a_recv.at[0])
    laid = fin[...].reshape(ROWS, 3 * HEAD)
    mixed = attend(laid[:, :HEAD], laid[:, HEAD : 2 * HEAD], laid[:, 2 * HEAD :], bias[...])
    rmsg[...] = mixed.reshape(rmsg.shape).astype(jnp.bfloat16)
    exchange(1, rmsg, rfin)
    out_along_second(2)
    await_bytes(msg.at[0 : PEERS - 1], a_send.at[0])
    await_bytes(rfin, a_recv.at[1])
    back = jnp.dot(
        by_frame[...], rfin[...].reshape(ROWS, HEAD), preferred_element_type=jnp.float32
    ).astype(jnp.bfloat16)
    temporal = jnp.full((ROWS, HEAD), kind[odd], jnp.int32) == 1
    cbuf[...] = jnp.where(temporal, back, spatial).reshape(cbuf.shape)

    for which, step in ((1, 2), (1, 1), (1, NX - 1), (0, 2), (1, 0), (0, 1), (0, NX - 1)):
        remote(
            cbuf.at[odd if which == 0 else other],
            mbuf.at[band, odd],
            m_send.at[which, step],
            m_recv.at[which, step],
            (frame if which == 0 else beside, band_at(step)),
        ).start()
    remote(
        cbuf.at[odd], mbuf.at[band, odd], n_send.at[0, 0], n_recv.at[0, 0], sibling
    ).start()
    last = pltpu.make_async_copy(cbuf.at[odd], mbuf.at[band, odd], m_recv.at[0, 0])
    last.start()
    for which, hop in ((1, 0), (0, 1), (0, 3), (1, 1), (1, 3), (0, 2), (1, 2)):
        block = mbuf.at[band_at(-hop), odd if which == 0 else other]
        await_bytes(block, m_recv.at[which, hop])
        remote(block, block, n_send.at[which, hop], n_recv.at[which, hop], sibling).start()
    out_along_second(3)
    out_along_second(4)
    last.wait()

    def project_out(source):
        left = jnp.concatenate([mbuf[source, 0], mbuf[source, 1]], axis=1)
        right = jnp.stack([obuf[0, source], obuf[1, :, source]], axis=1).reshape(
            2 * HEAD, WIDTH
        )
        return jnp.dot(left, right, preferred_element_type=jnp.float32)

    def own_core(hop, carry):
        total[...] += project_out(band_at(-hop))
        return carry

    def other_core(hop, carry):
        source = 2 * wrap(x - hop, NX) + 1 - core
        for which in range(2):
            await_bytes(
                mbuf.at[source, sibling_odd if which == 0 else 1 - sibling_odd],
                n_recv.at[which, hop],
            )
        total[...] += project_out(source)
        return carry

    total[...] = jnp.zeros_like(total)
    lax.fori_loop(0, NX, own_core, 0)
    lax.fori_loop(0, NX, other_core, 0)
    sbuf[...] = total[...].astype(jnp.bfloat16).reshape(sbuf.shape)

    def columns(which):
        return out.at[:, pl.ds(pl.multiple_of(which * WIDTH, HEAD), WIDTH)]

    for step in range(1, BANDS):
        there = wrap(band + step, BANDS)
        remote(
            sbuf.at[there], columns(band), f_send.at[step], f_recv.at[step], (frame, there)
        ).start()
    last = pltpu.make_async_copy(sbuf.at[band], columns(band), f_send.at[0])
    last.start()
    for step in range(1, BANDS):
        await_bytes(columns(wrap(band - step, BANDS)), f_recv.at[step])
    last.wait()

    await_bytes(rmsg.at[0 : PEERS - 1], a_send.at[1])
    for which in range(2):
        for hop in range(NX):
            if hop or which:
                await_bytes(cbuf.at[0], m_send.at[which, hop])
            await_bytes(cbuf.at[0], n_send.at[which, hop])
    for half in range(2):
        for way in range(2):
            await_bytes(obuf.at[half, 0 : hops(NY)[way]], o_send.at[half, 1, way])
    for step in range(1, BANDS):
        await_bytes(sbuf.at[0], f_send.at[step])


def body(tokens, qkv_weight, out_weight, head_kind):
    bf16 = jnp.bfloat16
    dma = pltpu.SemaphoreType.DMA
    hbm = pl.BlockSpec(memory_space=pltpu.HBM)
    return pl.pallas_call(
        kernel,
        out_shape=jax.ShapeDtypeStruct(tokens.shape, tokens.dtype),
        in_specs=[hbm] * 4,
        out_specs=hbm,
        scratch_shapes=[
            pltpu.VMEM((3, NY, PAIRS, 2, DEPTH, HEAD), bf16),
            pltpu.VMEM((2, 8, 8, 16, WIDTH), bf16),
            pltpu.VMEM((2, BANDS) + tokens.shape, bf16),
            pltpu.VMEM((PEERS, 2 * SHARE, 3 * HEAD), bf16),
            pltpu.VMEM((PEERS, 2 * SHARE, 3 * HEAD), bf16),
            pltpu.VMEM((PEERS, 2 * SHARE, HEAD), bf16),
            pltpu.VMEM((PEERS, 2 * SHARE, HEAD), bf16),
            pltpu.VMEM((2, POSITIONS, HEAD), bf16),
            pltpu.VMEM((BANDS, 2, POSITIONS, HEAD), bf16),
            pltpu.VMEM((BANDS, 16, WIDTH), bf16),
            pltpu.VMEM((ROWS, 3 * HEAD), jnp.float32),
            pltpu.VMEM((POSITIONS, WIDTH), jnp.float32),
            pltpu.VMEM((ROWS, ROWS), bf16),
            pltpu.VMEM((ROWS, ROWS), bf16),
            pltpu.VMEM((ROWS, ROWS), jnp.float32),
            pltpu.SMEM((2,), jnp.int32),
            pltpu.VMEM((3, DEPTH, HEAD), bf16),
            dma((6,)),
            dma((3,)),
            dma((3,)),
            dma((2, 2)),
            dma((4,)),
            dma((2, 4, 4)),
            dma((2, 2, 2)),
            dma((2, 3)),
            dma((2, 2, 4)),
            dma((3, NX)),
            dma((3, NX)),
            dma((NX,)),
            dma((NX,)),
            dma((2,)),
            dma((2,)),
            dma((2, NX)),
            dma((2, NX)),
            dma((2, NX)),
            dma((2, NX)),
            dma((BANDS,)),
            dma((BANDS,)),
        ],
        compiler_params=pltpu.CompilerParams(
            collective_id=0, has_side_effects=True, vmem_limit_bytes=64 * 1024 * 1024
        ),
    )(tokens, qkv_weight.transpose(1, 0, 2), out_weight, head_kind)


def solution(mesh):
    return jax.shard_map(
        body,
        mesh=mesh,
        in_specs=(
            P(("frame", "band"), None),
            P("frame", None, "band"),
            P("frame", "band"),
            P("band"),
        ),
        out_specs=P(("frame", "band"), None),
        check_vma=False,
    )
```

```python
import jax
import jax.numpy as jnp
from jax import lax
from jax.experimental import pallas as pl
from jax.experimental.pallas import tpu as pltpu
from jax.sharding import PartitionSpec as P

MESH = pl.DeviceIdType.MESH
NX = 4
NY = 8
NZ = 8
PAIRS = NZ // 2
BANDS = 2 * NX
PEERS = NY * PAIRS
HEAD = 128
POSITIONS = 128
ROWS = 2 * POSITIONS
SHARE = POSITIONS // PEERS
DEPTH = 48
WIDTH = 384


def remote(src, dst, send_sem, recv_sem, device):
    return pltpu.make_async_remote_copy(
        src_ref=src,
        dst_ref=dst,
        send_sem=send_sem,
        recv_sem=recv_sem,
        device_id=device,
        device_id_type=MESH,
    )


def await_bytes(ref, sem):
    pltpu.make_async_copy(ref, ref, sem).wait()


def attend(queries, keys, values, bias):
    scores = lax.dot_general(
        queries, keys, (((1,), (1,)), ((), ())), preferred_element_type=jnp.float32
    ) * (HEAD**-0.5)
    if bias is not None:
        scores = scores + bias
    raised = jnp.exp(scores - jnp.max(scores, axis=-1, keepdims=True))
    probs = (raised / jnp.sum(raised, axis=-1, keepdims=True)).astype(jnp.bfloat16)
    return jnp.dot(probs, values, preferred_element_type=jnp.float32)


def wrap(value, size):
    return lax.rem(value + 8 * size, size)


def hops(size):
    return (size // 2, (size - 1) // 2)


def wander(place):
    if isinstance(place, int):
        return (place + 1) // 2 * (2 * (place % 2) - 1)
    return lax.div(place + 1, 2) * (2 * lax.rem(place, 2) - 1)


class Grid:
    def __init__(self, block, device, here, sizes, sign, sems):
        self.block = block
        self.device = device
        self.first, self.second = here
        self.n_first, self.n_second = sizes
        self.sign = sign
        self.send, self.recv1, self.recv2 = sems

    def turn(self, way, place):
        flip = 1 - 2 * (place // 2 if isinstance(place, int) else lax.div(place, 2))
        return (self.sign if way == 0 else -self.sign) * flip

    def to_second(self, block, way, step, place, by=1):
        there = wrap(self.second + by * self.turn(way, place), self.n_second)
        remote(
            block,
            block,
            self.send.at[1, way],
            self.recv2.at[way, step, place],
            self.device(self.first, there),
        ).start()

    def begin(self, src, dst, device):
        for way in range(2):
            there = wrap(self.second + self.turn(way, 0), self.n_second)
            remote(
                src,
                dst,
                self.send.at[1, way],
                self.recv2.at[way, 0, 0],
                device(self.first, there),
            ).start()
        for place in range(1, self.n_first):
            there = wrap(self.first + self.sign * wander(place), self.n_first)
            remote(
                src,
                dst,
                self.send.at[0, 0],
                self.recv1.at[place],
                device(there, self.second),
            ).start()

    def along_first(self, place):
        block = self.block(
            wrap(self.first - self.sign * wander(place), self.n_first), self.second
        )
        await_bytes(block, self.recv1.at[place])
        for way in range(2):
            self.to_second(block, way, 0, place)

    def along_second(self, step, place):
        for way in range(2):
            if step > hops(self.n_second)[way]:
                continue
            block = self.block(
                wrap(self.first - self.sign * wander(place), self.n_first),
                wrap(self.second - self.turn(way, place) * step, self.n_second),
            )
            await_bytes(block, self.recv2.at[way, step - 1, place])
            if step < 3:
                self.to_second(block, way, step, place)
            if step == 2 and way == 0:
                self.to_second(block, way, 3, place, 2)


def kernel(
    tokens,
    qkv,
    out_weight,
    kind_hbm,
    out,
    wbuf,
    obuf,
    tbuf,
    msg,
    fin,
    rmsg,
    rfin,
    cbuf,
    mbuf,
    sbuf,
    qkv_sum,
    total,
    by_peer,
    by_frame,
    bias,
    kind,
    cross,
    own_sem,
    z_send,
    z_recv,
    w_send,
    w_recv1,
    w_recv2,
    o_send,
    o_recv1,
    o_recv2,
    t_send,
    t_recv,
    s_send,
    s_recv,
    a_send,
    a_recv,
    m_send,
    m_recv,
    n_send,
    n_recv,
    f_send,
    f_recv,
):
    frame = lax.axis_index("frame")
    band = lax.axis_index("band")
    y, z = lax.div(frame, NZ), lax.rem(frame, NZ)
    x, core = lax.div(band, 2), lax.rem(band, 2)
    across = z + (y - z) * core
    along = y + (z - y) * core
    pair, odd = lax.div(across, 2), lax.rem(across, 2)
    other = 1 - odd
    sign = 1 - 2 * core
    sibling_band = 2 * x + 1 - core
    sibling = (frame, sibling_band)
    sibling_odd = lax.rem(y + (z - y) * core, 2)
    me = along * PAIRS + pair

    def frame_at(along_there, across_there):
        return along_there * (NZ - (NZ - 1) * core) + across_there * (1 + (NZ - 1) * core)

    beside = frame_at(along, 2 * pair + other)

    def band_at(step):
        return 2 * wrap(x + step, NX) + core

    def peer(index):
        return (frame_at(lax.div(index, PAIRS), 2 * lax.rem(index, PAIRS) + odd), band)

    def head_columns(which):
        return qkv.at[:, :, pl.ds(pl.multiple_of(which * HEAD, HEAD), HEAD)]

    own = [
        pltpu.make_async_copy(head_columns(odd), wbuf.at[:, along, pair, odd], own_sem.at[0]),
        pltpu.make_async_copy(out_weight.at[0:16], obuf.at[0, y, z], own_sem.at[1]),
        pltpu.make_async_copy(out_weight.at[16:32], obuf.at[1, z, y], own_sem.at[2]),
        pltpu.make_async_copy(tokens, tbuf.at[odd, band], own_sem.at[3]),
        pltpu.make_async_copy(kind_hbm, kind, own_sem.at[4]),
        pltpu.make_async_copy(head_columns(other), cross, own_sem.at[5]),
    ]
    for copy in own:
        copy.start()

    barrier = pltpu.get_barrier_semaphore()

    def greet(device):
        pl.semaphore_signal(barrier, inc=1, device_id=device, device_id_type=MESH)

    greet(sibling)
    greet((beside, sibling_band))
    for step in range(1, NY):
        greet((y * NZ + wrap(z + step, NZ), band))
        greet((wrap(y + step, NY) * NZ + z, band))
    for step in (1, -1):
        greet((frame_at(wrap(along + step, NY), 2 * pair + other), band))
    for step in range(1, NX):
        greet((frame, band_at(step)))

    pl.semaphore_wait(barrier, 2 + NY - 1 + NZ - 1 + 2 + NX - 1)

    own[0].wait()
    own[5].wait()

    grid = Grid(
        lambda first, second: wbuf.at[:, second, first],
        lambda first, second: (frame_at(second, 2 * first + odd), band),
        (pair, along),
        (PAIRS, NY),
        sign,
        (w_send, w_recv1, w_recv2),
    )

    def token_along_x(which, block):
        for step in (1, NX - 1):
            remote(
                block, block, t_send.at[which, step], t_recv.at[which, step], (frame, band_at(step))
            ).start()

    def token_passed_on(which, by):
        if which == 0:
            block = tbuf.at[odd, band_at(-by)]
        else:
            block = tbuf.at[other, 2 * wrap(x - by, NX) + which - 1]
        remote(
            block, block, t_send.at[which, 2], t_recv.at[which, 2], (frame, band_at(by))
        ).start()

    def token_to_sibling(hop):
        from_band = band_at(-hop)
        remote(
            tbuf.at[odd, from_band],
            tbuf.at[sibling_odd, from_band],
            s_send.at[hop],
            s_recv.at[hop],
            sibling,
        ).start()

    here = wbuf.at[:, along, pair, odd]
    grid.begin(here, here, grid.device)
    beside_z = y * NZ + z + 1 - 2 * lax.rem(z, 2)
    beside_y = (y + 1 - 2 * lax.rem(y, 2)) * NZ + z
    remote(
        tokens, tbuf.at[lax.rem(z, 2), band], z_send.at[1], z_recv.at[1 + core], (beside_z, 2 * x)
    ).start()
    remote(
        tokens, tbuf.at[lax.rem(y, 2), band], z_send.at[2], z_recv.at[1 + core], (beside_y, 2 * x + 1)
    ).start()
    grid.begin(
        cross, here, lambda first, second: (frame_at(second, 2 * first + other), band)
    )
    remote(cross, here, z_send.at[0], z_recv.at[0], (beside, band)).start()
    for copy in own[1:5]:
        copy.wait()
    token_along_x(0, tbuf.at[odd, band])
    remote(
        tbuf.at[odd, band], tbuf.at[sibling_odd, band], s_send.at[0], s_recv.at[0], sibling
    ).start()

    tall = lax.broadcasted_iota(jnp.int32, (ROWS, ROWS), 0)
    wide = lax.broadcasted_iota(jnp.int32, (ROWS, ROWS), 1)

    def origin(row):
        return (
            lax.rem(lax.div(row, SHARE), 2) * POSITIONS
            + lax.div(row, 2 * SHARE) * SHARE
            + lax.rem(row, SHARE)
        )

    by_peer[...] = jnp.where(wide == origin(tall), 1.0, 0.0).astype(jnp.bfloat16)
    by_frame[...] = jnp.where(tall == origin(wide), 1.0, 0.0).astype(jnp.bfloat16)
    bias[...] = jnp.where(lax.rem(tall, SHARE) == lax.rem(wide, SHARE), 0.0, -1e30)

    for which in range(2):
        await_bytes(tbuf.at[other, 2 * x + which], z_recv.at[1 + which])
        token_along_x(1 + which, tbuf.at[other, 2 * x + which])

    def out_here(half):
        return (z, y) if half == 0 else (y, z)

    def out_device(half, first, second):
        return (second * NZ + first if half == 0 else first * NZ + second, band)

    def turn(way):
        return sign if way == 0 else -sign

    def out_send2(half, way, step, chunk, by=1):
        first, second = out_here(half)
        there = wrap(second + by * turn(way), NY)
        remote(
            chunk,
            chunk,
            o_send.at[half, 1, way],
            o_recv2.at[half, way, step],
            out_device(half, first, there),
        ).start()

    def out_to_first(half, block, by, sem):
        first, second = out_here(half)
        remote(
            block,
            block,
            o_send.at[half, 0, 0],
            o_recv1.at[half, sem],
            out_device(half, wrap(first + by, NY), second),
        ).start()

    def out_along_first():
        for half in range(2):
            first, second = out_here(half)
            block = obuf.at[half, second, first]
            out_to_first(half, block, 2 * sign, 0)
            out_to_first(half, block, -2 * sign, 1)
            out_to_first(half, block, sign, 2)
            out_to_first(half, block, -sign, 2)

    def out_beyond():
        for half in range(2):
            first, second = out_here(half)
            block = obuf.at[half, second, wrap(first - 2 * sign, NY)]
            await_bytes(block, o_recv1.at[half, 0])
            out_to_first(half, block, 2 * sign, 2)
            out_to_first(half, block, sign, 2)
            block = obuf.at[half, second, wrap(first + 2 * sign, NY)]
            await_bytes(block, o_recv1.at[half, 1])
            out_to_first(half, block, -sign, 2)

    def out_along_second(step):
        for half in range(2):
            first, second = out_here(half)
            for way in range(2):
                if step > hops(NY)[way]:
                    continue
                chunk = obuf.at[half, wrap(second - turn(way) * step, NY)]
                if step:
                    await_bytes(chunk, o_recv2.at[half, way, step - 1])
                if step < 3:
                    out_send2(half, way, step, chunk)
                if step == 2 and way == 0:
                    out_send2(half, way, 3, chunk, 2)

    out_along_first()
    for place in range(1, PAIRS):
        grid.along_first(place)

    def ring_step(step):
        def one(place, carry):
            grid.along_second(step, place)
            return carry

        lax.fori_loop(0, PAIRS, one, 0)

    ring_step(1)
    for hop in (1, NX - 1):
        await_bytes(tbuf.at[odd, band_at(-hop)], t_recv.at[0, hop])
    token_passed_on(0, sign)
    token_to_sibling(1)
    token_to_sibling(NX - 1)
    ring_step(2)
    out_beyond()
    for which, by in ((1, 1), (2, -1)):
        for hop in (1, NX - 1):
            await_bytes(
                tbuf.at[other, 2 * wrap(x - hop, NX) + which - 1], t_recv.at[which, hop]
            )
        token_passed_on(which, by)
    await_bytes(tbuf.at[odd, band_at(2)], t_recv.at[0, 2])
    token_to_sibling(2)
    ring_step(3)
    for hop in range(NX):
        from_band = 2 * wrap(x - hop, NX) + 1 - core
        await_bytes(tbuf.at[odd, from_band], s_recv.at[hop])
        if hop == 2:
            for which in range(2):
                await_bytes(
                    tbuf.at[other, 2 * wrap(x - hop, NX) + which], t_recv.at[1 + which, hop]
                )
    ring_step(4)
    await_bytes(wbuf.at[:, along, pair, other], z_recv.at[0])
    for half in range(2):
        await_bytes(obuf.at[half, out_here(half)[1], 0 : NY - 3], o_recv1.at[half, 2])
    out_along_second(0)

    def project(right):
        qkv_sum[...] = jnp.dot(
            tbuf[...].reshape(ROWS, -1),
            jnp.concatenate([right(slot) for slot in range(3)], axis=1),
            preferred_element_type=jnp.float32,
        )

    @pl.when(core == 0)
    def _():
        project(lambda slot: wbuf[slot].reshape(-1, HEAD))

    @pl.when(core == 1)
    def _():
        project(
            lambda slot: jnp.concatenate(
                [
                    wbuf[slot, :, there, parity].reshape(-1, HEAD)
                    for there in range(PAIRS)
                    for parity in range(2)
                ],
                axis=0,
            )
        )

    rounded = qkv_sum[...].astype(jnp.bfloat16)

    msg[...] = (
        jnp.dot(by_peer[...], rounded, preferred_element_type=jnp.float32)
        .reshape(msg.shape)
        .astype(jnp.bfloat16)
    )

    def exchange(stage, source, target):
        def send(step, carry):
            there = lax.rem(me + PEERS // 2 + wander(step) + PEERS, PEERS)
            remote(
                source.at[there], target.at[me], a_send.at[stage], a_recv.at[stage], peer(there)
            ).start()
            return carry

        pltpu.make_async_copy(source.at[me], target.at[me], a_recv.at[stage]).start()
        lax.fori_loop(0, PEERS - 1, send, 0)

    exchange(0, msg, fin)
    spatial = jnp.concatenate(
        [
            attend(
                rounded[at : at + POSITIONS, :HEAD],
                rounded[at : at + POSITIONS, HEAD : 2 * HEAD],
                rounded[at : at + POSITIONS, 2 * HEAD :],
                None,
            )
            for at in (0, POSITIONS)
        ],
        axis=0,
    ).astype(jnp.bfloat16)
    out_along_second(1)

    await_bytes(wbuf.at[:, 0, 0, 0], z_send.at[0])
    await_bytes(tbuf.at[0, 0], z_send.at[1])
    await_bytes(tbuf.at[0, 0], z_send.at[2])
    await_bytes(wbuf.at[:, 0, 0 : PAIRS - 1], w_send.at[0, 0])
    for way in range(2):
        await_bytes(wbuf.at[:, 0 : hops(NY)[way]], w_send.at[1, way])
        await_bytes(obuf.at[way, 0, 0 : NY - 1], o_send.at[way, 0, 0])
    for hop in range(NX):
        await_bytes(tbuf.at[0, 0], s_send.at[hop])
        if hop:
            for which in range(3):
                await_bytes(tbuf.at[0, 0], t_send.at[which, hop])
    await_bytes(fin, a_recv.at[0])
    laid = fin[...].reshape(ROWS, 3 * HEAD)
    mixed = attend(laid[:, :HEAD], laid[:, HEAD : 2 * HEAD], laid[:, 2 * HEAD :], bias[...])
    rmsg[...] = mixed.reshape(rmsg.shape).astype(jnp.bfloat16)
    exchange(1, rmsg, rfin)
    out_along_second(2)
    await_bytes(msg.at[0 : PEERS - 1], a_send.at[0])
    await_bytes(rfin, a_recv.at[1])
    back = jnp.dot(
        by_frame[...], rfin[...].reshape(ROWS, HEAD), preferred_element_type=jnp.float32
    ).astype(jnp.bfloat16)
    temporal = jnp.full((ROWS, HEAD), kind[odd], jnp.int32) == 1
    cbuf[...] = jnp.where(temporal, back, spatial).reshape(cbuf.shape)

    for which, step in ((1, 2), (1, 1), (1, NX - 1), (0, 2), (1, 0), (0, 1), (0, NX - 1)):
        remote(
            cbuf.at[odd if which == 0 else other],
            mbuf.at[band, odd],
            m_send.at[which, step],
            m_recv.at[which, step],
            (frame if which == 0 else beside, band_at(step)),
        ).start()
    remote(
        cbuf.at[odd], mbuf.at[band, odd], n_send.at[0, 0], n_recv.at[0, 0], sibling
    ).start()
    last = pltpu.make_async_copy(cbuf.at[odd], mbuf.at[band, odd], m_recv.at[0, 0])
    last.start()
    for which, hop in ((1, 0), (0, 1), (0, 3), (1, 1), (1, 3), (0, 2), (1, 2)):
        block = mbuf.at[band_at(-hop), odd if which == 0 else other]
        await_bytes(block, m_recv.at[which, hop])
        remote(block, block, n_send.at[which, hop], n_recv.at[which, hop], sibling).start()
    out_along_second(3)
    out_along_second(4)
    last.wait()

    def project_out(source):
        left = jnp.concatenate([mbuf[source, 0], mbuf[source, 1]], axis=1)
        right = jnp.stack([obuf[0, source], obuf[1, :, source]], axis=1).reshape(
            2 * HEAD, WIDTH
        )
        return jnp.dot(left, right, preferred_element_type=jnp.float32)

    def own_core(hop, carry):
        total[...] += project_out(band_at(-hop))
        return carry

    def other_core(hop, carry):
        source = 2 * wrap(x - hop, NX) + 1 - core
        for which in range(2):
            await_bytes(
                mbuf.at[source, sibling_odd if which == 0 else 1 - sibling_odd],
                n_recv.at[which, hop],
            )
        total[...] += project_out(source)
        return carry

    total[...] = jnp.zeros_like(total)
    lax.fori_loop(0, NX, own_core, 0)
    lax.fori_loop(0, NX, other_core, 0)
    sbuf[...] = total[...].astype(jnp.bfloat16).reshape(sbuf.shape)

    def columns(which):
        return out.at[:, pl.ds(pl.multiple_of(which * WIDTH, HEAD), WIDTH)]

    for step in range(1, BANDS):
        there = wrap(band + step, BANDS)
        remote(
            sbuf.at[there], columns(band), f_send.at[step], f_recv.at[step], (frame, there)
        ).start()
    last = pltpu.make_async_copy(sbuf.at[band], columns(band), f_send.at[0])
    last.start()
    for step in range(1, BANDS):
        await_bytes(columns(wrap(band - step, BANDS)), f_recv.at[step])
    last.wait()

    await_bytes(rmsg.at[0 : PEERS - 1], a_send.at[1])
    for which in range(2):
        for hop in range(NX):
            if hop or which:
                await_bytes(cbuf.at[0], m_send.at[which, hop])
            await_bytes(cbuf.at[0], n_send.at[which, hop])
    for half in range(2):
        for way in range(2):
            await_bytes(obuf.at[half, 0 : hops(NY)[way]], o_send.at[half, 1, way])
    for step in range(1, BANDS):
        await_bytes(sbuf.at[0], f_send.at[step])


def body(tokens, qkv_weight, out_weight, head_kind):
    bf16 = jnp.bfloat16
    dma = pltpu.SemaphoreType.DMA
    hbm = pl.BlockSpec(memory_space=pltpu.HBM)
    return pl.pallas_call(
        kernel,
        out_shape=jax.ShapeDtypeStruct(tokens.shape, tokens.dtype),
        in_specs=[hbm] * 4,
        out_specs=hbm,
        scratch_shapes=[
            pltpu.VMEM((3, NY, PAIRS, 2, DEPTH, HEAD), bf16),
            pltpu.VMEM((2, 8, 8, 16, WIDTH), bf16),
            pltpu.VMEM((2, BANDS) + tokens.shape, bf16),
            pltpu.VMEM((PEERS, 2 * SHARE, 3 * HEAD), bf16),
            pltpu.VMEM((PEERS, 2 * SHARE, 3 * HEAD), bf16),
            pltpu.VMEM((PEERS, 2 * SHARE, HEAD), bf16),
            pltpu.VMEM((PEERS, 2 * SHARE, HEAD), bf16),
            pltpu.VMEM((2, POSITIONS, HEAD), bf16),
            pltpu.VMEM((BANDS, 2, POSITIONS, HEAD), bf16),
            pltpu.VMEM((BANDS, 16, WIDTH), bf16),
            pltpu.VMEM((ROWS, 3 * HEAD), jnp.float32),
            pltpu.VMEM((POSITIONS, WIDTH), jnp.float32),
            pltpu.VMEM((ROWS, ROWS), bf16),
            pltpu.VMEM((ROWS, ROWS), bf16),
            pltpu.VMEM((ROWS, ROWS), jnp.float32),
            pltpu.SMEM((2,), jnp.int32),
            pltpu.VMEM((3, DEPTH, HEAD), bf16),
            dma((6,)),
            dma((3,)),
            dma((3,)),
            dma((2, 2)),
            dma((4,)),
            dma((2, 4, 4)),
            dma((2, 2, 2)),
            dma((2, 3)),
            dma((2, 2, 4)),
            dma((3, NX)),
            dma((3, NX)),
            dma((NX,)),
            dma((NX,)),
            dma((2,)),
            dma((2,)),
            dma((2, NX)),
            dma((2, NX)),
            dma((2, NX)),
            dma((2, NX)),
            dma((BANDS,)),
            dma((BANDS,)),
        ],
        compiler_params=pltpu.CompilerParams(
            collective_id=0, has_side_effects=True, vmem_limit_bytes=64 * 1024 * 1024
        ),
    )(tokens, qkv_weight.transpose(1, 0, 2), out_weight, head_kind)


def solution(mesh):
    return jax.shard_map(
        body,
        mesh=mesh,
        in_specs=(
            P(("frame", "band"), None),
            P("frame", None, "band"),
            P("frame", "band"),
            P("band"),
        ),
        out_specs=P(("frame", "band"), None),
        check_vma=False,
    )
```

```python
import jax
import jax.numpy as jnp
from jax import lax
from jax.experimental import pallas as pl
from jax.experimental.pallas import tpu as pltpu
from jax.sharding import PartitionSpec as P

MESH = pl.DeviceIdType.MESH
NX = 4
NY = 8
NZ = 8
PAIRS = NZ // 2
BANDS = 2 * NX
PEERS = NY * PAIRS
HEAD = 128
POSITIONS = 128
ROWS = 2 * POSITIONS
SHARE = POSITIONS // PEERS
DEPTH = 48
WIDTH = 384


def remote(src, dst, send_sem, recv_sem, device):
    return pltpu.make_async_remote_copy(
        src_ref=src,
        dst_ref=dst,
        send_sem=send_sem,
        recv_sem=recv_sem,
        device_id=device,
        device_id_type=MESH,
    )


def await_bytes(ref, sem):
    pltpu.make_async_copy(ref, ref, sem).wait()


def attend(queries, keys, values, bias):
    scores = lax.dot_general(
        queries, keys, (((1,), (1,)), ((), ())), preferred_element_type=jnp.float32
    ) * (HEAD**-0.5)
    if bias is not None:
        scores = scores + bias
    raised = jnp.exp(scores - jnp.max(scores, axis=-1, keepdims=True))
    probs = (raised / jnp.sum(raised, axis=-1, keepdims=True)).astype(jnp.bfloat16)
    return jnp.dot(probs, values, preferred_element_type=jnp.float32)


def wrap(value, size):
    return lax.rem(value + 8 * size, size)


def hops(size):
    return (size // 2, (size - 1) // 2)


def wander(place):
    if isinstance(place, int):
        return (place + 1) // 2 * (2 * (place % 2) - 1)
    return lax.div(place + 1, 2) * (2 * lax.rem(place, 2) - 1)


class Grid:
    def __init__(self, block, device, here, sizes, sign, sems):
        self.block = block
        self.device = device
        self.first, self.second = here
        self.n_first, self.n_second = sizes
        self.sign = sign
        self.send, self.recv1, self.recv2 = sems

    def turn(self, way, place):
        flip = 1 - 2 * (place // 2 if isinstance(place, int) else lax.div(place, 2))
        return (self.sign if way == 0 else -self.sign) * flip

    def to_second(self, block, way, step, place, by=1):
        there = wrap(self.second + by * self.turn(way, place), self.n_second)
        remote(
            block,
            block,
            self.send.at[1, way],
            self.recv2.at[way, step, place],
            self.device(self.first, there),
        ).start()

    def begin(self, src, dst, device):
        for way in range(2):
            there = wrap(self.second + self.turn(way, 0), self.n_second)
            remote(
                src,
                dst,
                self.send.at[1, way],
                self.recv2.at[way, 0, 0],
                device(self.first, there),
            ).start()
        for place in range(1, self.n_first):
            there = wrap(self.first + self.sign * wander(place), self.n_first)
            remote(
                src,
                dst,
                self.send.at[0, 0],
                self.recv1.at[place],
                device(there, self.second),
            ).start()

    def along_first(self, place):
        block = self.block(
            wrap(self.first - self.sign * wander(place), self.n_first), self.second
        )
        await_bytes(block, self.recv1.at[place])
        for way in range(2):
            self.to_second(block, way, 0, place)
            if place == self.n_first - 1:
                self.to_second(block, way, 1, place, 2)

    def along_second(self, step, place, pass_on=True):
        for way in range(2):
            if step > hops(self.n_second)[way]:
                continue
            block = self.block(
                wrap(self.first - self.sign * wander(place), self.n_first),
                wrap(self.second - self.turn(way, place) * step, self.n_second),
            )
            await_bytes(block, self.recv2.at[way, step - 1, place])
            if step < 3 and pass_on:
                self.to_second(block, way, step, place)
            if step == 2 and way == 0:
                self.to_second(block, way, 3, place, 2)


def kernel(
    tokens,
    qkv,
    out_weight,
    kind_hbm,
    out,
    wbuf,
    obuf,
    tbuf,
    msg,
    fin,
    rmsg,
    rfin,
    cbuf,
    mbuf,
    sbuf,
    qkv_sum,
    total,
    by_peer,
    by_frame,
    bias,
    kind,
    cross,
    own_sem,
    z_send,
    z_recv,
    w_send,
    w_recv1,
    w_recv2,
    o_send,
    o_recv1,
    o_recv2,
    t_send,
    t_recv,
    s_send,
    s_recv,
    a_send,
    a_recv,
    m_send,
    m_recv,
    n_send,
    n_recv,
    f_send,
    f_recv,
):
    frame = lax.axis_index("frame")
    band = lax.axis_index("band")
    y, z = lax.div(frame, NZ), lax.rem(frame, NZ)
    x, core = lax.div(band, 2), lax.rem(band, 2)
    across = z + (y - z) * core
    along = y + (z - y) * core
    pair, odd = lax.div(across, 2), lax.rem(across, 2)
    other = 1 - odd
    sign = 1 - 2 * core
    sibling_band = 2 * x + 1 - core
    sibling = (frame, sibling_band)
    sibling_odd = lax.rem(y + (z - y) * core, 2)
    me = along * PAIRS + pair

    def frame_at(along_there, across_there):
        return along_there * (NZ - (NZ - 1) * core) + across_there * (1 + (NZ - 1) * core)

    beside = frame_at(along, 2 * pair + other)

    def band_at(step):
        return 2 * wrap(x + step, NX) + core

    def peer(index):
        return (frame_at(lax.div(index, PAIRS), 2 * lax.rem(index, PAIRS) + odd), band)

    def head_columns(which):
        return qkv.at[:, :, pl.ds(pl.multiple_of(which * HEAD, HEAD), HEAD)]

    own = [
        pltpu.make_async_copy(head_columns(odd), wbuf.at[:, along, pair, odd], own_sem.at[0]),
        pltpu.make_async_copy(out_weight.at[0:16], obuf.at[0, y, z], own_sem.at[1]),
        pltpu.make_async_copy(out_weight.at[16:32], obuf.at[1, z, y], own_sem.at[2]),
        pltpu.make_async_copy(tokens, tbuf.at[odd, band], own_sem.at[3]),
        pltpu.make_async_copy(kind_hbm, kind, own_sem.at[4]),
        pltpu.make_async_copy(head_columns(other), cross, own_sem.at[5]),
    ]
    for copy in own:
        copy.start()

    barrier = pltpu.get_barrier_semaphore()

    def greet(device):
        pl.semaphore_signal(barrier, inc=1, device_id=device, device_id_type=MESH)

    greet(sibling)
    greet((beside, sibling_band))
    for step in range(1, NY):
        greet((y * NZ + wrap(z + step, NZ), band))
        greet((wrap(y + step, NY) * NZ + z, band))
    for step in (1, -1):
        greet((frame_at(wrap(along + step, NY), 2 * pair + other), band))
    for step in range(1, NX):
        greet((frame, band_at(step)))

    pl.semaphore_wait(barrier, 2 + NY - 1 + NZ - 1 + 2 + NX - 1)

    own[0].wait()
    own[5].wait()

    grid = Grid(
        lambda first, second: wbuf.at[:, second, first],
        lambda first, second: (frame_at(second, 2 * first + odd), band),
        (pair, along),
        (PAIRS, NY),
        sign,
        (w_send, w_recv1, w_recv2),
    )

    def token_along_x(which, block):
        for step in (1, NX - 1):
            remote(
                block, block, t_send.at[which, step], t_recv.at[which, step], (frame, band_at(step))
            ).start()

    def token_passed_on(which, by):
        if which == 0:
            block = tbuf.at[odd, band_at(-by)]
        else:
            block = tbuf.at[other, 2 * wrap(x - by, NX) + which - 1]
        remote(
            block, block, t_send.at[which, 2], t_recv.at[which, 2], (frame, band_at(by))
        ).start()

    def token_to_sibling(hop):
        from_band = band_at(-hop)
        remote(
            tbuf.at[odd, from_band],
            tbuf.at[sibling_odd, from_band],
            s_send.at[hop],
            s_recv.at[hop],
            sibling,
        ).start()

    here = wbuf.at[:, along, pair, odd]
    grid.begin(here, here, grid.device)
    beside_z = y * NZ + z + 1 - 2 * lax.rem(z, 2)
    beside_y = (y + 1 - 2 * lax.rem(y, 2)) * NZ + z
    remote(
        tokens, tbuf.at[lax.rem(z, 2), band], z_send.at[1], z_recv.at[1 + core], (beside_z, 2 * x)
    ).start()
    remote(
        tokens, tbuf.at[lax.rem(y, 2), band], z_send.at[2], z_recv.at[1 + core], (beside_y, 2 * x + 1)
    ).start()
    grid.begin(
        cross, here, lambda first, second: (frame_at(second, 2 * first + other), band)
    )
    remote(cross, here, z_send.at[0], z_recv.at[0], (beside, band)).start()
    for copy in own[1:5]:
        copy.wait()
    token_along_x(0, tbuf.at[odd, band])
    remote(
        tbuf.at[odd, band], tbuf.at[sibling_odd, band], s_send.at[0], s_recv.at[0], sibling
    ).start()

    tall = lax.broadcasted_iota(jnp.int32, (ROWS, ROWS), 0)
    wide = lax.broadcasted_iota(jnp.int32, (ROWS, ROWS), 1)

    def origin(row):
        return (
            lax.rem(lax.div(row, SHARE), 2) * POSITIONS
            + lax.div(row, 2 * SHARE) * SHARE
            + lax.rem(row, SHARE)
        )

    qkv_sum[...] = jnp.zeros_like(qkv_sum)
    by_peer[...] = jnp.where(wide == origin(tall), 1.0, 0.0).astype(jnp.bfloat16)
    by_frame[...] = jnp.where(tall == origin(wide), 1.0, 0.0).astype(jnp.bfloat16)
    bias[...] = jnp.where(lax.rem(tall, SHARE) == lax.rem(wide, SHARE), 0.0, -1e30)

    for which in range(2):
        await_bytes(tbuf.at[other, 2 * x + which], z_recv.at[1 + which])
        token_along_x(1 + which, tbuf.at[other, 2 * x + which])

    def out_here(half):
        return (z, y) if half == 0 else (y, z)

    def out_device(half, first, second):
        return (second * NZ + first if half == 0 else first * NZ + second, band)

    def turn(way):
        return sign if way == 0 else -sign

    def out_send2(half, way, step, chunk, by=1):
        first, second = out_here(half)
        there = wrap(second + by * turn(way), NY)
        remote(
            chunk,
            chunk,
            o_send.at[half, 1, way],
            o_recv2.at[half, way, step],
            out_device(half, first, there),
        ).start()

    def out_to_first(half, block, by, sem):
        first, second = out_here(half)
        remote(
            block,
            block,
            o_send.at[half, 0, 0],
            o_recv1.at[half, sem],
            out_device(half, wrap(first + by, NY), second),
        ).start()

    def out_along_first():
        for half in range(2):
            first, second = out_here(half)
            block = obuf.at[half, second, first]
            out_to_first(half, block, 2 * sign, 0)
            out_to_first(half, block, -2 * sign, 1)
            out_to_first(half, block, sign, 2)
            out_to_first(half, block, -sign, 2)

    def out_beyond():
        for half in range(2):
            first, second = out_here(half)
            block = obuf.at[half, second, wrap(first - 2 * sign, NY)]
            await_bytes(block, o_recv1.at[half, 0])
            out_to_first(half, block, 2 * sign, 2)
            out_to_first(half, block, sign, 2)
            block = obuf.at[half, second, wrap(first + 2 * sign, NY)]
            await_bytes(block, o_recv1.at[half, 1])
            out_to_first(half, block, -sign, 2)

    def out_along_second(step):
        for half in range(2):
            first, second = out_here(half)
            for way in range(2):
                if step > hops(NY)[way]:
                    continue
                chunk = obuf.at[half, wrap(second - turn(way) * step, NY)]
                if step:
                    await_bytes(chunk, o_recv2.at[half, way, step - 1])
                if step < 3:
                    out_send2(half, way, step, chunk)
                if step == 2 and way == 0:
                    out_send2(half, way, 3, chunk, 2)

    out_along_first()
    for place in range(1, PAIRS):
        grid.along_first(place)

    def ring_step(step, count=PAIRS):
        def one(place, carry):
            grid.along_second(step, place)
            return carry

        lax.fori_loop(0, count, one, 0)

    ring_step(1, PAIRS - 1)
    grid.along_second(1, PAIRS - 1, False)
    out_beyond()
    for hop in (1, NX - 1):
        await_bytes(tbuf.at[odd, band_at(-hop)], t_recv.at[0, hop])
    token_passed_on(0, sign)
    token_to_sibling(1)
    token_to_sibling(NX - 1)
    ring_step(2)
    for which, by in ((1, 1), (2, -1)):
        for hop in (1, NX - 1):
            await_bytes(
                tbuf.at[other, 2 * wrap(x - hop, NX) + which - 1], t_recv.at[which, hop]
            )
        token_passed_on(which, by)
    await_bytes(tbuf.at[odd, band_at(2)], t_recv.at[0, 2])
    token_to_sibling(2)
    ring_step(3)
    for hop in range(NX):
        from_band = 2 * wrap(x - hop, NX) + 1 - core
        await_bytes(tbuf.at[odd, from_band], s_recv.at[hop])
        if hop == 2:
            for which in range(2):
                await_bytes(
                    tbuf.at[other, 2 * wrap(x - hop, NX) + which], t_recv.at[1 + which, hop]
                )
    ring_step(4)
    await_bytes(wbuf.at[:, along, pair, other], z_recv.at[0])
    for half in range(2):
        await_bytes(obuf.at[half, out_here(half)[1], 0 : NY - 3], o_recv1.at[half, 2])
    out_along_second(0)

    chunk = 2 * NZ * DEPTH

    def project(step, right):
        at = pl.ds(pl.multiple_of(step * chunk, HEAD), chunk)
        qkv_sum[...] += jnp.dot(
            tbuf[:, :, :, at].reshape(ROWS, chunk),
            jnp.concatenate([right(slot) for slot in range(3)], axis=1),
            preferred_element_type=jnp.float32,
        )

    @pl.when(core == 0)
    def _():
        def one(step, carry):
            project(step, lambda slot: wbuf[slot, pl.ds(2 * step, 2)].reshape(chunk, HEAD))
            return carry

        lax.fori_loop(0, NY // 2, one, 0)

    @pl.when(core == 1)
    def _():
        def one(step, carry):
            project(
                step,
                lambda slot: jnp.concatenate(
                    [
                        wbuf[slot, :, step, parity].reshape(chunk // 2, HEAD)
                        for parity in range(2)
                    ],
                    axis=0,
                ),
            )
            return carry

        lax.fori_loop(0, NY // 2, one, 0)

    rounded = qkv_sum[...].astype(jnp.bfloat16)

    msg[...] = (
        jnp.dot(by_peer[...], rounded, preferred_element_type=jnp.float32)
        .reshape(msg.shape)
        .astype(jnp.bfloat16)
    )

    def exchange(stage, source, target):
        def send(step, carry):
            there = lax.rem(me + PEERS // 2 + wander(step) + PEERS, PEERS)
            remote(
                source.at[there], target.at[me], a_send.at[stage], a_recv.at[stage], peer(there)
            ).start()
            return carry

        pltpu.make_async_copy(source.at[me], target.at[me], a_recv.at[stage]).start()
        lax.fori_loop(0, PEERS - 1, send, 0)

    exchange(0, msg, fin)
    spatial = jnp.concatenate(
        [
            attend(
                rounded[at : at + POSITIONS, :HEAD],
                rounded[at : at + POSITIONS, HEAD : 2 * HEAD],
                rounded[at : at + POSITIONS, 2 * HEAD :],
                None,
            )
            for at in (0, POSITIONS)
        ],
        axis=0,
    ).astype(jnp.bfloat16)
    out_along_second(1)

    await_bytes(wbuf.at[:, 0, 0, 0], z_send.at[0])
    await_bytes(tbuf.at[0, 0], z_send.at[1])
    await_bytes(tbuf.at[0, 0], z_send.at[2])
    await_bytes(wbuf.at[:, 0, 0 : PAIRS - 1], w_send.at[0, 0])
    for way in range(2):
        await_bytes(wbuf.at[:, 0 : hops(NY)[way]], w_send.at[1, way])
        await_bytes(obuf.at[way, 0, 0 : NY - 1], o_send.at[way, 0, 0])
    for hop in range(NX):
        await_bytes(tbuf.at[0, 0], s_send.at[hop])
        if hop:
            for which in range(3):
                await_bytes(tbuf.at[0, 0], t_send.at[which, hop])
    await_bytes(fin, a_recv.at[0])
    laid = fin[...].reshape(ROWS, 3 * HEAD)
    mixed = attend(laid[:, :HEAD], laid[:, HEAD : 2 * HEAD], laid[:, 2 * HEAD :], bias[...])
    rmsg[...] = mixed.reshape(rmsg.shape).astype(jnp.bfloat16)
    exchange(1, rmsg, rfin)
    out_along_second(2)
    await_bytes(msg.at[0 : PEERS - 1], a_send.at[0])
    await_bytes(rfin, a_recv.at[1])
    back = jnp.dot(
        by_frame[...], rfin[...].reshape(ROWS, HEAD), preferred_element_type=jnp.float32
    ).astype(jnp.bfloat16)
    temporal = jnp.full((ROWS, HEAD), kind[odd], jnp.int32) == 1
    cbuf[...] = jnp.where(temporal, back, spatial).reshape(cbuf.shape)

    for which, step in ((1, 2), (1, 1), (1, NX - 1), (0, 2), (1, 0), (0, 1), (0, NX - 1)):
        remote(
            cbuf.at[odd if which == 0 else other],
            mbuf.at[band, odd],
            m_send.at[which, step],
            m_recv.at[which, step],
            (frame if which == 0 else beside, band_at(step)),
        ).start()
    remote(
        cbuf.at[odd], mbuf.at[band, odd], n_send.at[0, 0], n_recv.at[0, 0], sibling
    ).start()
    last = pltpu.make_async_copy(cbuf.at[odd], mbuf.at[band, odd], m_recv.at[0, 0])
    last.start()
    for which, hop in ((1, 0), (0, 1), (0, 3), (1, 1), (1, 3), (0, 2), (1, 2)):
        block = mbuf.at[band_at(-hop), odd if which == 0 else other]
        await_bytes(block, m_recv.at[which, hop])
        remote(block, block, n_send.at[which, hop], n_recv.at[which, hop], sibling).start()
    out_along_second(3)
    out_along_second(4)
    last.wait()

    def project_out(source):
        left = jnp.concatenate([mbuf[source, 0], mbuf[source, 1]], axis=1)
        right = jnp.stack([obuf[0, source], obuf[1, :, source]], axis=1).reshape(
            2 * HEAD, WIDTH
        )
        return jnp.dot(left, right, preferred_element_type=jnp.float32)

    def own_core(hop, carry):
        total[...] += project_out(band_at(-hop))
        return carry

    def other_core(hop, carry):
        source = 2 * wrap(x - hop, NX) + 1 - core
        for which in range(2):
            await_bytes(
                mbuf.at[source, sibling_odd if which == 0 else 1 - sibling_odd],
                n_recv.at[which, hop],
            )
        total[...] += project_out(source)
        return carry

    total[...] = jnp.zeros_like(total)
    lax.fori_loop(0, NX, own_core, 0)
    lax.fori_loop(0, NX, other_core, 0)
    sbuf[...] = total[...].astype(jnp.bfloat16).reshape(sbuf.shape)

    def columns(which):
        return out.at[:, pl.ds(pl.multiple_of(which * WIDTH, HEAD), WIDTH)]

    for step in range(1, BANDS):
        there = wrap(band + step, BANDS)
        remote(
            sbuf.at[there], columns(band), f_send.at[step], f_recv.at[step], (frame, there)
        ).start()
    last = pltpu.make_async_copy(sbuf.at[band], columns(band), f_send.at[0])
    last.start()
    for step in range(1, BANDS):
        await_bytes(columns(wrap(band - step, BANDS)), f_recv.at[step])
    last.wait()

    await_bytes(rmsg.at[0 : PEERS - 1], a_send.at[1])
    for which in range(2):
        for hop in range(NX):
            if hop or which:
                await_bytes(cbuf.at[0], m_send.at[which, hop])
            await_bytes(cbuf.at[0], n_send.at[which, hop])
    for half in range(2):
        for way in range(2):
            await_bytes(obuf.at[half, 0 : hops(NY)[way]], o_send.at[half, 1, way])
    for step in range(1, BANDS):
        await_bytes(sbuf.at[0], f_send.at[step])


def body(tokens, qkv_weight, out_weight, head_kind):
    bf16 = jnp.bfloat16
    dma = pltpu.SemaphoreType.DMA
    hbm = pl.BlockSpec(memory_space=pltpu.HBM)
    return pl.pallas_call(
        kernel,
        out_shape=jax.ShapeDtypeStruct(tokens.shape, tokens.dtype),
        in_specs=[hbm] * 4,
        out_specs=hbm,
        scratch_shapes=[
            pltpu.VMEM((3, NY, PAIRS, 2, DEPTH, HEAD), bf16),
            pltpu.VMEM((2, 8, 8, 16, WIDTH), bf16),
            pltpu.VMEM((2, BANDS) + tokens.shape, bf16),
            pltpu.VMEM((PEERS, 2 * SHARE, 3 * HEAD), bf16),
            pltpu.VMEM((PEERS, 2 * SHARE, 3 * HEAD), bf16),
            pltpu.VMEM((PEERS, 2 * SHARE, HEAD), bf16),
            pltpu.VMEM((PEERS, 2 * SHARE, HEAD), bf16),
            pltpu.VMEM((2, POSITIONS, HEAD), bf16),
            pltpu.VMEM((BANDS, 2, POSITIONS, HEAD), bf16),
            pltpu.VMEM((BANDS, 16, WIDTH), bf16),
            pltpu.VMEM((ROWS, 3 * HEAD), jnp.float32),
            pltpu.VMEM((POSITIONS, WIDTH), jnp.float32),
            pltpu.VMEM((ROWS, ROWS), bf16),
            pltpu.VMEM((ROWS, ROWS), bf16),
            pltpu.VMEM((ROWS, ROWS), jnp.float32),
            pltpu.SMEM((2,), jnp.int32),
            pltpu.VMEM((3, DEPTH, HEAD), bf16),
            dma((6,)),
            dma((3,)),
            dma((3,)),
            dma((2, 2)),
            dma((4,)),
            dma((2, 4, 4)),
            dma((2, 2, 2)),
            dma((2, 3)),
            dma((2, 2, 4)),
            dma((3, NX)),
            dma((3, NX)),
            dma((NX,)),
            dma((NX,)),
            dma((2,)),
            dma((2,)),
            dma((2, NX)),
            dma((2, NX)),
            dma((2, NX)),
            dma((2, NX)),
            dma((BANDS,)),
            dma((BANDS,)),
        ],
        compiler_params=pltpu.CompilerParams(
            collective_id=0, has_side_effects=True, vmem_limit_bytes=64 * 1024 * 1024
        ),
    )(tokens, qkv_weight.transpose(1, 0, 2), out_weight, head_kind)


def solution(mesh):
    return jax.shard_map(
        body,
        mesh=mesh,
        in_specs=(
            P(("frame", "band"), None),
            P("frame", None, "band"),
            P("frame", "band"),
            P("band"),
        ),
        out_specs=P(("frame", "band"), None),
        check_vma=False,
    )
```

```python
import jax
import jax.numpy as jnp
from jax import lax
from jax.experimental import pallas as pl
from jax.experimental.pallas import tpu as pltpu
from jax.sharding import PartitionSpec as P

MESH = pl.DeviceIdType.MESH
NX = 4
NY = 8
NZ = 8
PAIRS = NZ // 2
BANDS = 2 * NX
PEERS = NY * PAIRS
HEAD = 128
POSITIONS = 128
ROWS = 2 * POSITIONS
SHARE = POSITIONS // PEERS
DEPTH = 48
WIDTH = 384


def remote(src, dst, send_sem, recv_sem, device):
    return pltpu.make_async_remote_copy(
        src_ref=src,
        dst_ref=dst,
        send_sem=send_sem,
        recv_sem=recv_sem,
        device_id=device,
        device_id_type=MESH,
    )


def await_bytes(ref, sem):
    pltpu.make_async_copy(ref, ref, sem).wait()


def attend(queries, keys, values, bias):
    scores = lax.dot_general(
        queries, keys, (((1,), (1,)), ((), ())), preferred_element_type=jnp.float32
    ) * (HEAD**-0.5)
    if bias is not None:
        scores = scores + bias
    raised = jnp.exp(scores - jnp.max(scores, axis=-1, keepdims=True))
    probs = (raised / jnp.sum(raised, axis=-1, keepdims=True)).astype(jnp.bfloat16)
    return jnp.dot(probs, values, preferred_element_type=jnp.float32)


def wrap(value, size):
    return lax.rem(value + 8 * size, size)


def hops(size):
    return (size // 2, (size - 1) // 2)


def wander(place):
    if isinstance(place, int):
        return (place + 1) // 2 * (2 * (place % 2) - 1)
    return lax.div(place + 1, 2) * (2 * lax.rem(place, 2) - 1)


class Grid:
    def __init__(self, block, device, here, sizes, sign, sems):
        self.block = block
        self.device = device
        self.first, self.second = here
        self.n_first, self.n_second = sizes
        self.sign = sign
        self.send, self.recv1, self.recv2 = sems

    def turn(self, way, place):
        flip = 1 - 2 * (place // 2 if isinstance(place, int) else lax.div(place, 2))
        return (self.sign if way == 0 else -self.sign) * flip

    def to_second(self, block, way, step, place):
        there = wrap(self.second + self.turn(way, place), self.n_second)
        remote(
            block,
            block,
            self.send.at[1, way],
            self.recv2.at[way, step, place],
            self.device(self.first, there),
        ).start()

    def begin(self, src, dst, device):
        for way in range(2):
            there = wrap(self.second + self.turn(way, 0), self.n_second)
            remote(
                src,
                dst,
                self.send.at[1, way],
                self.recv2.at[way, 0, 0],
                device(self.first, there),
            ).start()
        for place in range(1, self.n_first):
            there = wrap(self.first + self.sign * wander(place), self.n_first)
            remote(
                src,
                dst,
                self.send.at[0, 0],
                self.recv1.at[place],
                device(there, self.second),
            ).start()

    def along_first(self, place):
        block = self.block(
            wrap(self.first - self.sign * wander(place), self.n_first), self.second
        )
        await_bytes(block, self.recv1.at[place])
        for way in range(2):
            self.to_second(block, way, 0, place)

    def along_second(self, step, place):
        for way in range(2):
            if step > hops(self.n_second)[way]:
                continue
            block = self.block(
                wrap(self.first - self.sign * wander(place), self.n_first),
                wrap(self.second - self.turn(way, place) * step, self.n_second),
            )
            await_bytes(block, self.recv2.at[way, step - 1, place])
            if step < hops(self.n_second)[way]:
                self.to_second(block, way, step, place)


def kernel(
    tokens,
    qkv,
    out_weight,
    kind_hbm,
    out,
    wbuf,
    obuf,
    tbuf,
    msg,
    fin,
    rmsg,
    rfin,
    cbuf,
    mbuf,
    sbuf,
    qkv_sum,
    total,
    by_peer,
    by_frame,
    bias,
    kind,
    cross,
    own_sem,
    z_send,
    z_recv,
    w_send,
    w_recv1,
    w_recv2,
    o_send,
    o_recv1,
    o_recv2,
    t_send,
    t_recv,
    s_send,
    s_recv,
    a_send,
    a_recv,
    m_send,
    m_recv,
    n_send,
    n_recv,
    f_send,
    f_recv,
):
    frame = lax.axis_index("frame")
    band = lax.axis_index("band")
    y, z = lax.div(frame, NZ), lax.rem(frame, NZ)
    x, core = lax.div(band, 2), lax.rem(band, 2)
    across = z + (y - z) * core
    along = y + (z - y) * core
    pair, odd = lax.div(across, 2), lax.rem(across, 2)
    other = 1 - odd
    sign = 1 - 2 * core
    sibling_band = 2 * x + 1 - core
    sibling = (frame, sibling_band)
    sibling_odd = lax.rem(y + (z - y) * core, 2)
    me = along * PAIRS + pair

    def frame_at(along_there, across_there):
        return along_there * (NZ - (NZ - 1) * core) + across_there * (1 + (NZ - 1) * core)

    beside = frame_at(along, 2 * pair + other)

    def band_at(step):
        return 2 * wrap(x + step, NX) + core

    def peer(index):
        return (frame_at(lax.div(index, PAIRS), 2 * lax.rem(index, PAIRS) + odd), band)

    def head_columns(which):
        return qkv.at[:, :, pl.ds(pl.multiple_of(which * HEAD, HEAD), HEAD)]

    own = [
        pltpu.make_async_copy(head_columns(odd), wbuf.at[:, along, pair, odd], own_sem.at[0]),
        pltpu.make_async_copy(out_weight.at[0:16], obuf.at[0, y, z], own_sem.at[1]),
        pltpu.make_async_copy(out_weight.at[16:32], obuf.at[1, z, y], own_sem.at[2]),
        pltpu.make_async_copy(tokens, tbuf.at[odd, band], own_sem.at[3]),
        pltpu.make_async_copy(kind_hbm, kind, own_sem.at[4]),
        pltpu.make_async_copy(head_columns(other), cross, own_sem.at[5]),
    ]
    for copy in own:
        copy.start()

    barrier = pltpu.get_barrier_semaphore()

    def greet(device):
        pl.semaphore_signal(barrier, inc=1, device_id=device, device_id_type=MESH)

    greet(sibling)
    greet((beside, sibling_band))
    for step in range(1, NY):
        greet((y * NZ + wrap(z + step, NZ), band))
        greet((wrap(y + step, NY) * NZ + z, band))
    for step in (1, -1):
        greet((frame_at(wrap(along + step, NY), 2 * pair + other), band))
    for step in range(1, NX):
        greet((frame, band_at(step)))

    pl.semaphore_wait(barrier, 2 + NY - 1 + NZ - 1 + 2 + NX - 1)

    own[0].wait()
    own[5].wait()

    grid = Grid(
        lambda first, second: wbuf.at[:, second, first],
        lambda first, second: (frame_at(second, 2 * first + odd), band),
        (pair, along),
        (PAIRS, NY),
        sign,
        (w_send, w_recv1, w_recv2),
    )

    def token_along_x(which, block):
        for step in (1, NX - 1):
            remote(
                block, block, t_send.at[which, step], t_recv.at[which, step], (frame, band_at(step))
            ).start()

    def token_passed_on(which, by):
        if which == 0:
            block = tbuf.at[odd, band_at(-by)]
        else:
            block = tbuf.at[other, 2 * wrap(x - by, NX) + which - 1]
        remote(
            block, block, t_send.at[which, 2], t_recv.at[which, 2], (frame, band_at(by))
        ).start()

    def token_to_sibling(hop):
        from_band = band_at(-hop)
        remote(
            tbuf.at[odd, from_band],
            tbuf.at[sibling_odd, from_band],
            s_send.at[hop],
            s_recv.at[hop],
            sibling,
        ).start()

    here = wbuf.at[:, along, pair, odd]
    grid.begin(here, here, grid.device)
    beside_z = y * NZ + z + 1 - 2 * lax.rem(z, 2)
    beside_y = (y + 1 - 2 * lax.rem(y, 2)) * NZ + z
    remote(
        tokens, tbuf.at[lax.rem(z, 2), band], z_send.at[1], z_recv.at[1 + core], (beside_z, 2 * x)
    ).start()
    remote(
        tokens, tbuf.at[lax.rem(y, 2), band], z_send.at[2], z_recv.at[1 + core], (beside_y, 2 * x + 1)
    ).start()
    grid.begin(
        cross, here, lambda first, second: (frame_at(second, 2 * first + other), band)
    )
    remote(cross, here, z_send.at[0], z_recv.at[0], (beside, band)).start()
    for copy in own[1:5]:
        copy.wait()
    token_along_x(0, tbuf.at[odd, band])
    remote(
        tbuf.at[odd, band], tbuf.at[sibling_odd, band], s_send.at[0], s_recv.at[0], sibling
    ).start()

    tall = lax.broadcasted_iota(jnp.int32, (ROWS, ROWS), 0)
    wide = lax.broadcasted_iota(jnp.int32, (ROWS, ROWS), 1)

    def origin(row):
        return (
            lax.rem(lax.div(row, SHARE), 2) * POSITIONS
            + lax.div(row, 2 * SHARE) * SHARE
            + lax.rem(row, SHARE)
        )

    qkv_sum[...] = jnp.zeros_like(qkv_sum)
    by_peer[...] = jnp.where(wide == origin(tall), 1.0, 0.0).astype(jnp.bfloat16)
    by_frame[...] = jnp.where(tall == origin(wide), 1.0, 0.0).astype(jnp.bfloat16)
    bias[...] = jnp.where(lax.rem(tall, SHARE) == lax.rem(wide, SHARE), 0.0, -1e30)

    for which in range(2):
        await_bytes(tbuf.at[other, 2 * x + which], z_recv.at[1 + which])
        token_along_x(1 + which, tbuf.at[other, 2 * x + which])

    def out_here(half):
        return (z, y) if half == 0 else (y, z)

    def out_device(half, first, second):
        return (second * NZ + first if half == 0 else first * NZ + second, band)

    def turn(way):
        return sign if way == 0 else -sign

    def out_send2(half, way, step, chunk, by=1):
        first, second = out_here(half)
        there = wrap(second + by * turn(way), NY)
        remote(
            chunk,
            chunk,
            o_send.at[half, 1, way],
            o_recv2.at[half, way, step],
            out_device(half, first, there),
        ).start()

    def out_to_first(half, block, by, sem):
        first, second = out_here(half)
        remote(
            block,
            block,
            o_send.at[half, 0, 0],
            o_recv1.at[half, sem],
            out_device(half, wrap(first + by, NY), second),
        ).start()

    def out_along_first():
        for half in range(2):
            first, second = out_here(half)
            block = obuf.at[half, second, first]
            out_to_first(half, block, 2 * sign, 0)
            out_to_first(half, block, -2 * sign, 1)
            out_to_first(half, block, sign, 2)
            out_to_first(half, block, -sign, 2)

    def out_beyond():
        for half in range(2):
            first, second = out_here(half)
            block = obuf.at[half, second, wrap(first - 2 * sign, NY)]
            await_bytes(block, o_recv1.at[half, 0])
            out_to_first(half, block, 2 * sign, 2)
            out_to_first(half, block, sign, 2)
            block = obuf.at[half, second, wrap(first + 2 * sign, NY)]
            await_bytes(block, o_recv1.at[half, 1])
            out_to_first(half, block, -sign, 2)

    def out_along_second(step):
        for half in range(2):
            first, second = out_here(half)
            for way in range(2):
                if step > hops(NY)[way]:
                    continue
                chunk = obuf.at[half, wrap(second - turn(way) * step, NY)]
                if step:
                    await_bytes(chunk, o_recv2.at[half, way, step - 1])
                if step < 3:
                    out_send2(half, way, step, chunk)
                if step == 2 and way == 0:
                    out_send2(half, way, 3, chunk, 2)

    out_along_first()
    for place in range(1, PAIRS):
        grid.along_first(place)

    def ring_step(step):
        def one(place, carry):
            grid.along_second(step, place)
            return carry

        lax.fori_loop(0, PAIRS, one, 0)

    ring_step(1)
    out_beyond()
    for hop in (1, NX - 1):
        await_bytes(tbuf.at[odd, band_at(-hop)], t_recv.at[0, hop])
    token_passed_on(0, sign)
    token_to_sibling(1)
    token_to_sibling(NX - 1)
    ring_step(2)
    for which, by in ((1, 1), (2, -1)):
        for hop in (1, NX - 1):
            await_bytes(
                tbuf.at[other, 2 * wrap(x - hop, NX) + which - 1], t_recv.at[which, hop]
            )
        token_passed_on(which, by)
    await_bytes(tbuf.at[odd, band_at(2)], t_recv.at[0, 2])
    token_to_sibling(2)
    ring_step(3)
    for hop in range(NX):
        from_band = 2 * wrap(x - hop, NX) + 1 - core
        await_bytes(tbuf.at[odd, from_band], s_recv.at[hop])
        if hop == 2:
            for which in range(2):
                await_bytes(
                    tbuf.at[other, 2 * wrap(x - hop, NX) + which], t_recv.at[1 + which, hop]
                )
    ring_step(4)
    await_bytes(wbuf.at[:, along, pair, other], z_recv.at[0])
    for half in range(2):
        await_bytes(obuf.at[half, out_here(half)[1], 0 : NY - 3], o_recv1.at[half, 2])
    out_along_second(0)

    chunk = 2 * NZ * DEPTH

    def project(step, right):
        at = pl.ds(pl.multiple_of(step * chunk, HEAD), chunk)
        qkv_sum[...] += jnp.dot(
            tbuf[:, :, :, at].reshape(ROWS, chunk),
            jnp.concatenate([right(slot) for slot in range(3)], axis=1),
            preferred_element_type=jnp.float32,
        )

    @pl.when(core == 0)
    def _():
        def one(step, carry):
            project(step, lambda slot: wbuf[slot, pl.ds(2 * step, 2)].reshape(chunk, HEAD))
            return carry

        lax.fori_loop(0, NY // 2, one, 0)

    @pl.when(core == 1)
    def _():
        def one(step, carry):
            project(
                step,
                lambda slot: jnp.concatenate(
                    [
                        wbuf[slot, :, step, parity].reshape(chunk // 2, HEAD)
                        for parity in range(2)
                    ],
                    axis=0,
                ),
            )
            return carry

        lax.fori_loop(0, NY // 2, one, 0)

    rounded = qkv_sum[...].astype(jnp.bfloat16)

    msg[...] = (
        jnp.dot(by_peer[...], rounded, preferred_element_type=jnp.float32)
        .reshape(msg.shape)
        .astype(jnp.bfloat16)
    )

    def exchange(stage, source, target):
        def send(step, carry):
            there = lax.rem(me + PEERS // 2 + wander(step) + PEERS, PEERS)
            remote(
                source.at[there], target.at[me], a_send.at[stage], a_recv.at[stage], peer(there)
            ).start()
            return carry

        pltpu.make_async_copy(source.at[me], target.at[me], a_recv.at[stage]).start()
        lax.fori_loop(0, PEERS - 1, send, 0)

    exchange(0, msg, fin)
    spatial = jnp.concatenate(
        [
            attend(
                rounded[at : at + POSITIONS, :HEAD],
                rounded[at : at + POSITIONS, HEAD : 2 * HEAD],
                rounded[at : at + POSITIONS, 2 * HEAD :],
                None,
            )
            for at in (0, POSITIONS)
        ],
        axis=0,
    ).astype(jnp.bfloat16)
    out_along_second(1)

    await_bytes(wbuf.at[:, 0, 0, 0], z_send.at[0])
    await_bytes(tbuf.at[0, 0], z_send.at[1])
    await_bytes(tbuf.at[0, 0], z_send.at[2])
    await_bytes(wbuf.at[:, 0, 0 : PAIRS - 1], w_send.at[0, 0])
    for way in range(2):
        await_bytes(wbuf.at[:, 0 : hops(NY)[way]], w_send.at[1, way])
        await_bytes(obuf.at[way, 0, 0 : NY - 1], o_send.at[way, 0, 0])
    for hop in range(NX):
        await_bytes(tbuf.at[0, 0], s_send.at[hop])
        if hop:
            for which in range(3):
                await_bytes(tbuf.at[0, 0], t_send.at[which, hop])
    await_bytes(fin, a_recv.at[0])
    laid = fin[...].reshape(ROWS, 3 * HEAD)
    mixed = attend(laid[:, :HEAD], laid[:, HEAD : 2 * HEAD], laid[:, 2 * HEAD :], bias[...])
    rmsg[...] = mixed.reshape(rmsg.shape).astype(jnp.bfloat16)
    exchange(1, rmsg, rfin)
    out_along_second(2)
    await_bytes(msg.at[0 : PEERS - 1], a_send.at[0])
    await_bytes(rfin, a_recv.at[1])
    back = jnp.dot(
        by_frame[...], rfin[...].reshape(ROWS, HEAD), preferred_element_type=jnp.float32
    ).astype(jnp.bfloat16)
    temporal = jnp.full((ROWS, HEAD), kind[odd], jnp.int32) == 1
    cbuf[...] = jnp.where(temporal, back, spatial).reshape(cbuf.shape)

    for which, step in ((1, 2), (1, 1), (1, NX - 1), (0, 2), (1, 0), (0, 1), (0, NX - 1)):
        remote(
            cbuf.at[odd if which == 0 else other],
            mbuf.at[band, odd],
            m_send.at[which, step],
            m_recv.at[which, step],
            (frame if which == 0 else beside, band_at(step)),
        ).start()
    remote(
        cbuf.at[odd], mbuf.at[band, odd], n_send.at[0, 0], n_recv.at[0, 0], sibling
    ).start()
    last = pltpu.make_async_copy(cbuf.at[odd], mbuf.at[band, odd], m_recv.at[0, 0])
    last.start()
    for which, hop in ((1, 0), (0, 1), (0, 3), (1, 1), (1, 3), (0, 2), (1, 2)):
        block = mbuf.at[band_at(-hop), odd if which == 0 else other]
        await_bytes(block, m_recv.at[which, hop])
        remote(block, block, n_send.at[which, hop], n_recv.at[which, hop], sibling).start()
    out_along_second(3)
    out_along_second(4)
    last.wait()

    def project_out(source):
        left = jnp.concatenate([mbuf[source, 0], mbuf[source, 1]], axis=1)
        right = jnp.stack([obuf[0, source], obuf[1, :, source]], axis=1).reshape(
            2 * HEAD, WIDTH
        )
        return jnp.dot(left, right, preferred_element_type=jnp.float32)

    def own_core(hop, carry):
        total[...] += project_out(band_at(-hop))
        return carry

    def other_core(hop, carry):
        source = 2 * wrap(x - hop, NX) + 1 - core
        for which in range(2):
            await_bytes(
                mbuf.at[source, sibling_odd if which == 0 else 1 - sibling_odd],
                n_recv.at[which, hop],
            )
        total[...] += project_out(source)
        return carry

    total[...] = jnp.zeros_like(total)
    lax.fori_loop(0, NX, own_core, 0)
    lax.fori_loop(0, NX, other_core, 0)
    sbuf[...] = total[...].astype(jnp.bfloat16).reshape(sbuf.shape)

    def columns(which):
        return out.at[:, pl.ds(pl.multiple_of(which * WIDTH, HEAD), WIDTH)]

    for step in range(1, BANDS):
        there = wrap(band + step, BANDS)
        remote(
            sbuf.at[there], columns(band), f_send.at[step], f_recv.at[step], (frame, there)
        ).start()
    last = pltpu.make_async_copy(sbuf.at[band], columns(band), f_send.at[0])
    last.start()
    for step in range(1, BANDS):
        await_bytes(columns(wrap(band - step, BANDS)), f_recv.at[step])
    last.wait()

    await_bytes(rmsg.at[0 : PEERS - 1], a_send.at[1])
    for which in range(2):
        for hop in range(NX):
            if hop or which:
                await_bytes(cbuf.at[0], m_send.at[which, hop])
            await_bytes(cbuf.at[0], n_send.at[which, hop])
    for half in range(2):
        for way in range(2):
            await_bytes(obuf.at[half, 0 : hops(NY)[way]], o_send.at[half, 1, way])
    for step in range(1, BANDS):
        await_bytes(sbuf.at[0], f_send.at[step])


def body(tokens, qkv_weight, out_weight, head_kind):
    bf16 = jnp.bfloat16
    dma = pltpu.SemaphoreType.DMA
    hbm = pl.BlockSpec(memory_space=pltpu.HBM)
    return pl.pallas_call(
        kernel,
        out_shape=jax.ShapeDtypeStruct(tokens.shape, tokens.dtype),
        in_specs=[hbm] * 4,
        out_specs=hbm,
        scratch_shapes=[
            pltpu.VMEM((3, NY, PAIRS, 2, DEPTH, HEAD), bf16),
            pltpu.VMEM((2, 8, 8, 16, WIDTH), bf16),
            pltpu.VMEM((2, BANDS) + tokens.shape, bf16),
            pltpu.VMEM((PEERS, 2 * SHARE, 3 * HEAD), bf16),
            pltpu.VMEM((PEERS, 2 * SHARE, 3 * HEAD), bf16),
            pltpu.VMEM((PEERS, 2 * SHARE, HEAD), bf16),
            pltpu.VMEM((PEERS, 2 * SHARE, HEAD), bf16),
            pltpu.VMEM((2, POSITIONS, HEAD), bf16),
            pltpu.VMEM((BANDS, 2, POSITIONS, HEAD), bf16),
            pltpu.VMEM((BANDS, 16, WIDTH), bf16),
            pltpu.VMEM((ROWS, 3 * HEAD), jnp.float32),
            pltpu.VMEM((POSITIONS, WIDTH), jnp.float32),
            pltpu.VMEM((ROWS, ROWS), bf16),
            pltpu.VMEM((ROWS, ROWS), bf16),
            pltpu.VMEM((ROWS, ROWS), jnp.float32),
            pltpu.SMEM((2,), jnp.int32),
            pltpu.VMEM((3, DEPTH, HEAD), bf16),
            dma((6,)),
            dma((3,)),
            dma((3,)),
            dma((2, 2)),
            dma((4,)),
            dma((2, 4, 4)),
            dma((2, 2, 2)),
            dma((2, 3)),
            dma((2, 2, 4)),
            dma((3, NX)),
            dma((3, NX)),
            dma((NX,)),
            dma((NX,)),
            dma((2,)),
            dma((2,)),
            dma((2, NX)),
            dma((2, NX)),
            dma((2, NX)),
            dma((2, NX)),
            dma((BANDS,)),
            dma((BANDS,)),
        ],
        compiler_params=pltpu.CompilerParams(
            collective_id=0, has_side_effects=True, vmem_limit_bytes=64 * 1024 * 1024
        ),
    )(tokens, qkv_weight.transpose(1, 0, 2), out_weight, head_kind)


def solution(mesh):
    return jax.shard_map(
        body,
        mesh=mesh,
        in_specs=(
            P(("frame", "band"), None),
            P("frame", None, "band"),
            P("frame", "band"),
            P("band"),
        ),
        out_specs=P(("frame", "band"), None),
        check_vma=False,
    )
```

```python
import jax
import jax.numpy as jnp
from jax import lax
from jax.experimental import pallas as pl
from jax.experimental.pallas import tpu as pltpu
from jax.sharding import PartitionSpec as P

MESH = pl.DeviceIdType.MESH
NX = 4
NY = 8
NZ = 8
PAIRS = NZ // 2
BANDS = 2 * NX
PEERS = NY * PAIRS
HEAD = 128
POSITIONS = 128
ROWS = 2 * POSITIONS
SHARE = POSITIONS // PEERS
DEPTH = 48
WIDTH = 384


def remote(src, dst, send_sem, recv_sem, device):
    return pltpu.make_async_remote_copy(
        src_ref=src,
        dst_ref=dst,
        send_sem=send_sem,
        recv_sem=recv_sem,
        device_id=device,
        device_id_type=MESH,
    )


def await_bytes(ref, sem):
    pltpu.make_async_copy(ref, ref, sem).wait()


def attend(queries, keys, values, bias):
    scores = lax.dot_general(
        queries, keys, (((1,), (1,)), ((), ())), preferred_element_type=jnp.float32
    ) * (HEAD**-0.5)
    if bias is not None:
        scores = scores + bias
    raised = jnp.exp(scores - jnp.max(scores, axis=-1, keepdims=True))
    probs = (raised / jnp.sum(raised, axis=-1, keepdims=True)).astype(jnp.bfloat16)
    return jnp.dot(probs, values, preferred_element_type=jnp.float32)


def wrap(value, size):
    return lax.rem(value + 8 * size, size)


def hops(size):
    return (size // 2, (size - 1) // 2)


def wander(place):
    if isinstance(place, int):
        return (place + 1) // 2 * (2 * (place % 2) - 1)
    return lax.div(place + 1, 2) * (2 * lax.rem(place, 2) - 1)


class Grid:
    def __init__(self, block, device, here, sizes, sign, sems):
        self.block = block
        self.device = device
        self.first, self.second = here
        self.n_first, self.n_second = sizes
        self.sign = sign
        self.send, self.recv1, self.recv2 = sems

    def turn(self, way, place):
        flip = 1 - 2 * (place // 2 if isinstance(place, int) else lax.div(place, 2))
        return (self.sign if way == 0 else -self.sign) * flip

    def to_second(self, block, way, step, place, by=1):
        there = wrap(self.second + by * self.turn(way, place), self.n_second)
        remote(
            block,
            block,
            self.send.at[1, way],
            self.recv2.at[way, step, place],
            self.device(self.first, there),
        ).start()

    def begin(self, src, dst, device):
        for way in range(2):
            there = wrap(self.second + self.turn(way, 0), self.n_second)
            remote(
                src,
                dst,
                self.send.at[1, way],
                self.recv2.at[way, 0, 0],
                device(self.first, there),
            ).start()
        for place in range(1, self.n_first):
            there = wrap(self.first + self.sign * wander(place), self.n_first)
            remote(
                src,
                dst,
                self.send.at[0, 0],
                self.recv1.at[place],
                device(there, self.second),
            ).start()

    def along_first(self, place):
        block = self.block(
            wrap(self.first - self.sign * wander(place), self.n_first), self.second
        )
        await_bytes(block, self.recv1.at[place])
        for way in range(2):
            self.to_second(block, way, 0, place)

    def along_second(self, step, place):
        for way in range(2):
            if step > hops(self.n_second)[way]:
                continue
            block = self.block(
                wrap(self.first - self.sign * wander(place), self.n_first),
                wrap(self.second - self.turn(way, place) * step, self.n_second),
            )
            await_bytes(block, self.recv2.at[way, step - 1, place])
            if step < 3:
                self.to_second(block, way, step, place)
            if step == 2 and way == 0:
                self.to_second(block, way, 3, place, 2)


def kernel(
    tokens,
    qkv,
    out_weight,
    kind_hbm,
    out,
    wbuf,
    obuf,
    tbuf,
    msg,
    fin,
    rmsg,
    rfin,
    cbuf,
    mbuf,
    sbuf,
    qkv_sum,
    total,
    by_peer,
    by_frame,
    bias,
    kind,
    cross,
    own_sem,
    z_send,
    z_recv,
    w_send,
    w_recv1,
    w_recv2,
    o_send,
    o_recv1,
    o_recv2,
    t_send,
    t_recv,
    s_send,
    s_recv,
    a_send,
    a_recv,
    m_send,
    m_recv,
    n_send,
    n_recv,
    f_send,
    f_recv,
):
    frame = lax.axis_index("frame")
    band = lax.axis_index("band")
    y, z = lax.div(frame, NZ), lax.rem(frame, NZ)
    x, core = lax.div(band, 2), lax.rem(band, 2)
    across = z + (y - z) * core
    along = y + (z - y) * core
    pair, odd = lax.div(across, 2), lax.rem(across, 2)
    other = 1 - odd
    sign = 1 - 2 * core
    sibling_band = 2 * x + 1 - core
    sibling = (frame, sibling_band)
    sibling_odd = lax.rem(y + (z - y) * core, 2)
    me = along * PAIRS + pair

    def frame_at(along_there, across_there):
        return along_there * (NZ - (NZ - 1) * core) + across_there * (1 + (NZ - 1) * core)

    beside = frame_at(along, 2 * pair + other)

    def band_at(step):
        return 2 * wrap(x + step, NX) + core

    def peer(index):
        return (frame_at(lax.div(index, PAIRS), 2 * lax.rem(index, PAIRS) + odd), band)

    def head_columns(which):
        return qkv.at[:, :, pl.ds(pl.multiple_of(which * HEAD, HEAD), HEAD)]

    own = [
        pltpu.make_async_copy(head_columns(odd), wbuf.at[:, along, pair, odd], own_sem.at[0]),
        pltpu.make_async_copy(out_weight.at[0:16], obuf.at[0, y, z], own_sem.at[1]),
        pltpu.make_async_copy(out_weight.at[16:32], obuf.at[1, z, y], own_sem.at[2]),
        pltpu.make_async_copy(tokens, tbuf.at[odd, band], own_sem.at[3]),
        pltpu.make_async_copy(kind_hbm, kind, own_sem.at[4]),
        pltpu.make_async_copy(head_columns(other), cross, own_sem.at[5]),
    ]
    for copy in own:
        copy.start()

    barrier = pltpu.get_barrier_semaphore()

    def greet(device):
        pl.semaphore_signal(barrier, inc=1, device_id=device, device_id_type=MESH)

    greet(sibling)
    greet((beside, sibling_band))
    for step in range(1, NY):
        greet((y * NZ + wrap(z + step, NZ), band))
        greet((wrap(y + step, NY) * NZ + z, band))
    for step in (1, -1):
        greet((frame_at(wrap(along + step, NY), 2 * pair + other), band))
    for step in range(1, NX):
        greet((frame, band_at(step)))

    pl.semaphore_wait(barrier, 2 + NY - 1 + NZ - 1 + 2 + NX - 1)

    own[0].wait()
    own[5].wait()

    grid = Grid(
        lambda first, second: wbuf.at[:, second, first],
        lambda first, second: (frame_at(second, 2 * first + odd), band),
        (pair, along),
        (PAIRS, NY),
        sign,
        (w_send, w_recv1, w_recv2),
    )

    def token_along_x(which, block):
        for step in (1, NX - 1):
            remote(
                block, block, t_send.at[which, step], t_recv.at[which, step], (frame, band_at(step))
            ).start()

    def token_passed_on(which, by):
        if which == 0:
            block = tbuf.at[odd, band_at(-by)]
        else:
            block = tbuf.at[other, 2 * wrap(x - by, NX) + which - 1]
        remote(
            block, block, t_send.at[which, 2], t_recv.at[which, 2], (frame, band_at(by))
        ).start()

    def token_to_sibling(hop):
        from_band = band_at(-hop)
        remote(
            tbuf.at[odd, from_band],
            tbuf.at[sibling_odd, from_band],
            s_send.at[hop],
            s_recv.at[hop],
            sibling,
        ).start()

    here = wbuf.at[:, along, pair, odd]
    grid.begin(here, here, grid.device)
    beside_z = y * NZ + z + 1 - 2 * lax.rem(z, 2)
    beside_y = (y + 1 - 2 * lax.rem(y, 2)) * NZ + z
    remote(
        tokens, tbuf.at[lax.rem(z, 2), band], z_send.at[1], z_recv.at[1 + core], (beside_z, 2 * x)
    ).start()
    remote(
        tokens, tbuf.at[lax.rem(y, 2), band], z_send.at[2], z_recv.at[1 + core], (beside_y, 2 * x + 1)
    ).start()
    grid.begin(
        cross, here, lambda first, second: (frame_at(second, 2 * first + other), band)
    )
    remote(cross, here, z_send.at[0], z_recv.at[0], (beside, band)).start()
    for copy in own[1:5]:
        copy.wait()
    token_along_x(0, tbuf.at[odd, band])
    remote(
        tbuf.at[odd, band], tbuf.at[sibling_odd, band], s_send.at[0], s_recv.at[0], sibling
    ).start()

    tall = lax.broadcasted_iota(jnp.int32, (ROWS, ROWS), 0)
    wide = lax.broadcasted_iota(jnp.int32, (ROWS, ROWS), 1)

    def origin(row):
        return (
            lax.rem(lax.div(row, SHARE), 2) * POSITIONS
            + lax.div(row, 2 * SHARE) * SHARE
            + lax.rem(row, SHARE)
        )

    qkv_sum[...] = jnp.zeros_like(qkv_sum)
    by_peer[...] = jnp.where(wide == origin(tall), 1.0, 0.0).astype(jnp.bfloat16)
    by_frame[...] = jnp.where(tall == origin(wide), 1.0, 0.0).astype(jnp.bfloat16)
    bias[...] = jnp.where(lax.rem(tall, SHARE) == lax.rem(wide, SHARE), 0.0, -1e30)

    for which in range(2):
        await_bytes(tbuf.at[other, 2 * x + which], z_recv.at[1 + which])
        token_along_x(1 + which, tbuf.at[other, 2 * x + which])

    def out_here(half):
        return (z, y) if half == 0 else (y, z)

    def out_device(half, first, second):
        return (second * NZ + first if half == 0 else first * NZ + second, band)

    def turn(way):
        return sign if way == 0 else -sign

    def out_send2(half, way, step, chunk, by=1):
        first, second = out_here(half)
        there = wrap(second + by * turn(way), NY)
        remote(
            chunk,
            chunk,
            o_send.at[half, 1, way],
            o_recv2.at[half, way, step],
            out_device(half, first, there),
        ).start()

    def out_to_first(half, block, by, sem):
        first, second = out_here(half)
        remote(
            block,
            block,
            o_send.at[half, 0, 0],
            o_recv1.at[half, sem],
            out_device(half, wrap(first + by, NY), second),
        ).start()

    def out_along_first():
        for half in range(2):
            first, second = out_here(half)
            block = obuf.at[half, second, first]
            out_to_first(half, block, 2 * sign, 0)
            out_to_first(half, block, -2 * sign, 1)
            out_to_first(half, block, sign, 2)
            out_to_first(half, block, -sign, 2)

    def out_beyond():
        for half in range(2):
            first, second = out_here(half)
            block = obuf.at[half, second, wrap(first - 2 * sign, NY)]
            await_bytes(block, o_recv1.at[half, 0])
            out_to_first(half, block, 2 * sign, 2)
            out_to_first(half, block, sign, 2)
            block = obuf.at[half, second, wrap(first + 2 * sign, NY)]
            await_bytes(block, o_recv1.at[half, 1])
            out_to_first(half, block, -sign, 2)

    def out_along_second(step):
        for half in range(2):
            first, second = out_here(half)
            for way in range(2):
                if step > hops(NY)[way]:
                    continue
                chunk = obuf.at[half, wrap(second - turn(way) * step, NY)]
                if step:
                    await_bytes(chunk, o_recv2.at[half, way, step - 1])
                if step < 3:
                    out_send2(half, way, step, chunk)
                if step == 2 and way == 0:
                    out_send2(half, way, 3, chunk, 2)

    out_along_first()
    for place in range(1, PAIRS):
        grid.along_first(place)

    def ring_step(step):
        def one(place, carry):
            grid.along_second(step, place)
            return carry

        lax.fori_loop(0, PAIRS, one, 0)

    ring_step(1)
    out_beyond()
    ring_step(2)
    for hop in (1, NX - 1):
        await_bytes(tbuf.at[odd, band_at(-hop)], t_recv.at[0, hop])
    token_passed_on(0, sign)
    token_to_sibling(1)
    token_to_sibling(NX - 1)
    for which, by in ((1, 1), (2, -1)):
        for hop in (1, NX - 1):
            await_bytes(
                tbuf.at[other, 2 * wrap(x - hop, NX) + which - 1], t_recv.at[which, hop]
            )
        token_passed_on(which, by)
    await_bytes(tbuf.at[odd, band_at(2)], t_recv.at[0, 2])
    token_to_sibling(2)
    ring_step(3)
    for hop in range(NX):
        from_band = 2 * wrap(x - hop, NX) + 1 - core
        await_bytes(tbuf.at[odd, from_band], s_recv.at[hop])
        if hop == 2:
            for which in range(2):
                await_bytes(
                    tbuf.at[other, 2 * wrap(x - hop, NX) + which], t_recv.at[1 + which, hop]
                )
    ring_step(4)
    await_bytes(wbuf.at[:, along, pair, other], z_recv.at[0])
    for half in range(2):
        await_bytes(obuf.at[half, out_here(half)[1], 0 : NY - 3], o_recv1.at[half, 2])
    out_along_second(0)

    chunk = 2 * NZ * DEPTH

    def project(step, right):
        at = pl.ds(pl.multiple_of(step * chunk, HEAD), chunk)
        qkv_sum[...] += jnp.dot(
            tbuf[:, :, :, at].reshape(ROWS, chunk),
            jnp.concatenate([right(slot) for slot in range(3)], axis=1),
            preferred_element_type=jnp.float32,
        )

    @pl.when(core == 0)
    def _():
        def one(step, carry):
            project(step, lambda slot: wbuf[slot, pl.ds(2 * step, 2)].reshape(chunk, HEAD))
            return carry

        lax.fori_loop(0, NY // 2, one, 0)

    @pl.when(core == 1)
    def _():
        def one(step, carry):
            project(
                step,
                lambda slot: jnp.concatenate(
                    [
                        wbuf[slot, :, step, parity].reshape(chunk // 2, HEAD)
                        for parity in range(2)
                    ],
                    axis=0,
                ),
            )
            return carry

        lax.fori_loop(0, NY // 2, one, 0)

    rounded = qkv_sum[...].astype(jnp.bfloat16)

    msg[...] = (
        jnp.dot(by_peer[...], rounded, preferred_element_type=jnp.float32)
        .reshape(msg.shape)
        .astype(jnp.bfloat16)
    )

    def exchange(stage, source, target):
        def send(step, carry):
            there = lax.rem(me + PEERS // 2 + wander(step) + PEERS, PEERS)
            remote(
                source.at[there], target.at[me], a_send.at[stage], a_recv.at[stage], peer(there)
            ).start()
            return carry

        pltpu.make_async_copy(source.at[me], target.at[me], a_recv.at[stage]).start()
        lax.fori_loop(0, PEERS - 1, send, 0)

    exchange(0, msg, fin)
    spatial = jnp.concatenate(
        [
            attend(
                rounded[at : at + POSITIONS, :HEAD],
                rounded[at : at + POSITIONS, HEAD : 2 * HEAD],
                rounded[at : at + POSITIONS, 2 * HEAD :],
                None,
            )
            for at in (0, POSITIONS)
        ],
        axis=0,
    ).astype(jnp.bfloat16)
    out_along_second(1)

    await_bytes(wbuf.at[:, 0, 0, 0], z_send.at[0])
    await_bytes(tbuf.at[0, 0], z_send.at[1])
    await_bytes(tbuf.at[0, 0], z_send.at[2])
    await_bytes(wbuf.at[:, 0, 0 : PAIRS - 1], w_send.at[0, 0])
    for way in range(2):
        await_bytes(wbuf.at[:, 0 : hops(NY)[way]], w_send.at[1, way])
        await_bytes(obuf.at[way, 0, 0 : NY - 1], o_send.at[way, 0, 0])
    for hop in range(NX):
        await_bytes(tbuf.at[0, 0], s_send.at[hop])
        if hop:
            for which in range(3):
                await_bytes(tbuf.at[0, 0], t_send.at[which, hop])
    await_bytes(fin, a_recv.at[0])
    laid = fin[...].reshape(ROWS, 3 * HEAD)
    mixed = attend(laid[:, :HEAD], laid[:, HEAD : 2 * HEAD], laid[:, 2 * HEAD :], bias[...])
    rmsg[...] = mixed.reshape(rmsg.shape).astype(jnp.bfloat16)
    exchange(1, rmsg, rfin)
    out_along_second(2)
    await_bytes(msg.at[0 : PEERS - 1], a_send.at[0])
    await_bytes(rfin, a_recv.at[1])
    back = jnp.dot(
        by_frame[...], rfin[...].reshape(ROWS, HEAD), preferred_element_type=jnp.float32
    ).astype(jnp.bfloat16)
    temporal = jnp.full((ROWS, HEAD), kind[odd], jnp.int32) == 1
    cbuf[...] = jnp.where(temporal, back, spatial).reshape(cbuf.shape)

    for which, step in ((1, 2), (1, 1), (1, NX - 1), (0, 2), (1, 0), (0, 1), (0, NX - 1)):
        remote(
            cbuf.at[odd if which == 0 else other],
            mbuf.at[band, odd],
            m_send.at[which, step],
            m_recv.at[which, step],
            (frame if which == 0 else beside, band_at(step)),
        ).start()
    remote(
        cbuf.at[odd], mbuf.at[band, odd], n_send.at[0, 0], n_recv.at[0, 0], sibling
    ).start()
    last = pltpu.make_async_copy(cbuf.at[odd], mbuf.at[band, odd], m_recv.at[0, 0])
    last.start()
    for which, hop in ((1, 0), (0, 1), (0, 3), (1, 1), (1, 3), (0, 2), (1, 2)):
        block = mbuf.at[band_at(-hop), odd if which == 0 else other]
        await_bytes(block, m_recv.at[which, hop])
        remote(block, block, n_send.at[which, hop], n_recv.at[which, hop], sibling).start()
    out_along_second(3)
    out_along_second(4)
    last.wait()

    def project_out(source):
        left = jnp.concatenate([mbuf[source, 0], mbuf[source, 1]], axis=1)
        right = jnp.stack([obuf[0, source], obuf[1, :, source]], axis=1).reshape(
            2 * HEAD, WIDTH
        )
        return jnp.dot(left, right, preferred_element_type=jnp.float32)

    def own_core(hop, carry):
        total[...] += project_out(band_at(-hop))
        return carry

    def other_core(hop, carry):
        source = 2 * wrap(x - hop, NX) + 1 - core
        for which in range(2):
            await_bytes(
                mbuf.at[source, sibling_odd if which == 0 else 1 - sibling_odd],
                n_recv.at[which, hop],
            )
        total[...] += project_out(source)
        return carry

    total[...] = jnp.zeros_like(total)
    lax.fori_loop(0, NX, own_core, 0)
    lax.fori_loop(0, NX, other_core, 0)
    sbuf[...] = total[...].astype(jnp.bfloat16).reshape(sbuf.shape)

    def columns(which):
        return out.at[:, pl.ds(pl.multiple_of(which * WIDTH, HEAD), WIDTH)]

    for step in range(1, BANDS):
        there = wrap(band + step, BANDS)
        remote(
            sbuf.at[there], columns(band), f_send.at[step], f_recv.at[step], (frame, there)
        ).start()
    last = pltpu.make_async_copy(sbuf.at[band], columns(band), f_send.at[0])
    last.start()
    for step in range(1, BANDS):
        await_bytes(columns(wrap(band - step, BANDS)), f_recv.at[step])
    last.wait()

    await_bytes(rmsg.at[0 : PEERS - 1], a_send.at[1])
    for which in range(2):
        for hop in range(NX):
            if hop or which:
                await_bytes(cbuf.at[0], m_send.at[which, hop])
            await_bytes(cbuf.at[0], n_send.at[which, hop])
    for half in range(2):
        for way in range(2):
            await_bytes(obuf.at[half, 0 : hops(NY)[way]], o_send.at[half, 1, way])
    for step in range(1, BANDS):
        await_bytes(sbuf.at[0], f_send.at[step])


def body(tokens, qkv_weight, out_weight, head_kind):
    bf16 = jnp.bfloat16
    dma = pltpu.SemaphoreType.DMA
    hbm = pl.BlockSpec(memory_space=pltpu.HBM)
    return pl.pallas_call(
        kernel,
        out_shape=jax.ShapeDtypeStruct(tokens.shape, tokens.dtype),
        in_specs=[hbm] * 4,
        out_specs=hbm,
        scratch_shapes=[
            pltpu.VMEM((3, NY, PAIRS, 2, DEPTH, HEAD), bf16),
            pltpu.VMEM((2, 8, 8, 16, WIDTH), bf16),
            pltpu.VMEM((2, BANDS) + tokens.shape, bf16),
            pltpu.VMEM((PEERS, 2 * SHARE, 3 * HEAD), bf16),
            pltpu.VMEM((PEERS, 2 * SHARE, 3 * HEAD), bf16),
            pltpu.VMEM((PEERS, 2 * SHARE, HEAD), bf16),
            pltpu.VMEM((PEERS, 2 * SHARE, HEAD), bf16),
            pltpu.VMEM((2, POSITIONS, HEAD), bf16),
            pltpu.VMEM((BANDS, 2, POSITIONS, HEAD), bf16),
            pltpu.VMEM((BANDS, 16, WIDTH), bf16),
            pltpu.VMEM((ROWS, 3 * HEAD), jnp.float32),
            pltpu.VMEM((POSITIONS, WIDTH), jnp.float32),
            pltpu.VMEM((ROWS, ROWS), bf16),
            pltpu.VMEM((ROWS, ROWS), bf16),
            pltpu.VMEM((ROWS, ROWS), jnp.float32),
            pltpu.SMEM((2,), jnp.int32),
            pltpu.VMEM((3, DEPTH, HEAD), bf16),
            dma((6,)),
            dma((3,)),
            dma((3,)),
            dma((2, 2)),
            dma((4,)),
            dma((2, 4, 4)),
            dma((2, 2, 2)),
            dma((2, 3)),
            dma((2, 2, 4)),
            dma((3, NX)),
            dma((3, NX)),
            dma((NX,)),
            dma((NX,)),
            dma((2,)),
            dma((2,)),
            dma((2, NX)),
            dma((2, NX)),
            dma((2, NX)),
            dma((2, NX)),
            dma((BANDS,)),
            dma((BANDS,)),
        ],
        compiler_params=pltpu.CompilerParams(
            collective_id=0, has_side_effects=True, vmem_limit_bytes=64 * 1024 * 1024
        ),
    )(tokens, qkv_weight.transpose(1, 0, 2), out_weight, head_kind)


def solution(mesh):
    return jax.shard_map(
        body,
        mesh=mesh,
        in_specs=(
            P(("frame", "band"), None),
            P("frame", None, "band"),
            P("frame", "band"),
            P("band"),
        ),
        out_specs=P(("frame", "band"), None),
        check_vma=False,
    )
```

```python
import jax
import jax.numpy as jnp
from jax import lax
from jax.experimental import pallas as pl
from jax.experimental.pallas import tpu as pltpu
from jax.sharding import PartitionSpec as P

MESH = pl.DeviceIdType.MESH
NX = 4
NY = 8
NZ = 8
PAIRS = NZ // 2
BANDS = 2 * NX
PEERS = NY * PAIRS
HEAD = 128
POSITIONS = 128
ROWS = 2 * POSITIONS
SHARE = POSITIONS // PEERS
DEPTH = 48
WIDTH = 384


def remote(src, dst, send_sem, recv_sem, device):
    return pltpu.make_async_remote_copy(
        src_ref=src,
        dst_ref=dst,
        send_sem=send_sem,
        recv_sem=recv_sem,
        device_id=device,
        device_id_type=MESH,
    )


def await_bytes(ref, sem):
    pltpu.make_async_copy(ref, ref, sem).wait()


def attend(queries, keys, values, bias):
    scores = lax.dot_general(
        queries, keys, (((1,), (1,)), ((), ())), preferred_element_type=jnp.float32
    ) * (HEAD**-0.5)
    if bias is not None:
        scores = scores + bias
    raised = jnp.exp(scores - jnp.max(scores, axis=-1, keepdims=True))
    probs = (raised / jnp.sum(raised, axis=-1, keepdims=True)).astype(jnp.bfloat16)
    return jnp.dot(probs, values, preferred_element_type=jnp.float32)


def wrap(value, size):
    return lax.rem(value + 8 * size, size)


def hops(size):
    return (size // 2, (size - 1) // 2)


def wander(place):
    if isinstance(place, int):
        return (place + 1) // 2 * (2 * (place % 2) - 1)
    return lax.div(place + 1, 2) * (2 * lax.rem(place, 2) - 1)


class Grid:
    def __init__(self, block, device, here, sizes, sign, sems):
        self.block = block
        self.device = device
        self.first, self.second = here
        self.n_first, self.n_second = sizes
        self.sign = sign
        self.send, self.recv1, self.recv2 = sems

    def turn(self, way, place):
        flip = 1 - 2 * (place // 2 if isinstance(place, int) else lax.div(place, 2))
        return (self.sign if way == 0 else -self.sign) * flip

    def to_second(self, block, way, step, place, by=1):
        there = wrap(self.second + by * self.turn(way, place), self.n_second)
        remote(
            block,
            block,
            self.send.at[1, way],
            self.recv2.at[way, step, place],
            self.device(self.first, there),
        ).start()

    def begin(self, src, dst, device):
        for way in range(2):
            there = wrap(self.second + self.turn(way, 0), self.n_second)
            remote(
                src,
                dst,
                self.send.at[1, way],
                self.recv2.at[way, 0, 0],
                device(self.first, there),
            ).start()
        for place in range(1, self.n_first):
            there = wrap(self.first + self.sign * wander(place), self.n_first)
            remote(
                src,
                dst,
                self.send.at[0, 0],
                self.recv1.at[place],
                device(there, self.second),
            ).start()

    def along_first(self, place):
        block = self.block(
            wrap(self.first - self.sign * wander(place), self.n_first), self.second
        )
        await_bytes(block, self.recv1.at[place])
        for way in range(2):
            self.to_second(block, way, 0, place)

    def along_second(self, step, place):
        for way in range(2):
            if step > hops(self.n_second)[way]:
                continue
            block = self.block(
                wrap(self.first - self.sign * wander(place), self.n_first),
                wrap(self.second - self.turn(way, place) * step, self.n_second),
            )
            await_bytes(block, self.recv2.at[way, step - 1, place])
            if step < 3:
                self.to_second(block, way, step, place)
            if step == 2 and way == 0:
                self.to_second(block, way, 3, place, 2)


def kernel(
    tokens,
    qkv,
    out_weight,
    kind_hbm,
    out,
    wbuf,
    obuf,
    tbuf,
    msg,
    fin,
    rmsg,
    rfin,
    cbuf,
    mbuf,
    sbuf,
    qkv_sum,
    total,
    by_peer,
    by_frame,
    bias,
    kind,
    cross,
    own_sem,
    z_send,
    z_recv,
    w_send,
    w_recv1,
    w_recv2,
    o_send,
    o_recv1,
    o_recv2,
    t_send,
    t_recv,
    s_send,
    s_recv,
    a_send,
    a_recv,
    m_send,
    m_recv,
    n_send,
    n_recv,
    f_send,
    f_recv,
):
    frame = lax.axis_index("frame")
    band = lax.axis_index("band")
    y, z = lax.div(frame, NZ), lax.rem(frame, NZ)
    x, core = lax.div(band, 2), lax.rem(band, 2)
    across = z + (y - z) * core
    along = y + (z - y) * core
    pair, odd = lax.div(across, 2), lax.rem(across, 2)
    other = 1 - odd
    sign = 1 - 2 * core
    sibling_band = 2 * x + 1 - core
    sibling = (frame, sibling_band)
    sibling_odd = lax.rem(y + (z - y) * core, 2)
    me = along * PAIRS + pair

    def frame_at(along_there, across_there):
        return along_there * (NZ - (NZ - 1) * core) + across_there * (1 + (NZ - 1) * core)

    beside = frame_at(along, 2 * pair + other)

    def band_at(step):
        return 2 * wrap(x + step, NX) + core

    def peer(index):
        return (frame_at(lax.div(index, PAIRS), 2 * lax.rem(index, PAIRS) + odd), band)

    def head_columns(which):
        return qkv.at[:, :, pl.ds(pl.multiple_of(which * HEAD, HEAD), HEAD)]

    own = [
        pltpu.make_async_copy(head_columns(odd), wbuf.at[:, along, pair, odd], own_sem.at[0]),
        pltpu.make_async_copy(out_weight.at[0:16], obuf.at[0, y, z], own_sem.at[1]),
        pltpu.make_async_copy(out_weight.at[16:32], obuf.at[1, z, y], own_sem.at[2]),
        pltpu.make_async_copy(tokens, tbuf.at[odd, band], own_sem.at[3]),
        pltpu.make_async_copy(kind_hbm, kind, own_sem.at[4]),
        pltpu.make_async_copy(head_columns(other), cross, own_sem.at[5]),
    ]
    for copy in own:
        copy.start()

    barrier = pltpu.get_barrier_semaphore()

    def greet(device):
        pl.semaphore_signal(barrier, inc=1, device_id=device, device_id_type=MESH)

    greet(sibling)
    greet((beside, sibling_band))
    for step in range(1, NY):
        greet((y * NZ + wrap(z + step, NZ), band))
        greet((wrap(y + step, NY) * NZ + z, band))
    for step in (1, -1):
        greet((frame_at(wrap(along + step, NY), 2 * pair + other), band))
    for step in range(1, NX):
        greet((frame, band_at(step)))

    pl.semaphore_wait(barrier, 2 + NY - 1 + NZ - 1 + 2 + NX - 1)

    own[0].wait()
    own[5].wait()

    grid = Grid(
        lambda first, second: wbuf.at[:, second, first],
        lambda first, second: (frame_at(second, 2 * first + odd), band),
        (pair, along),
        (PAIRS, NY),
        sign,
        (w_send, w_recv1, w_recv2),
    )

    def token_along_x(which, block):
        for step in (1, NX - 1):
            remote(
                block, block, t_send.at[which, step], t_recv.at[which, step], (frame, band_at(step))
            ).start()

    def token_passed_on(which, by):
        if which == 0:
            block = tbuf.at[odd, band_at(-by)]
        else:
            block = tbuf.at[other, 2 * wrap(x - by, NX) + which - 1]
        remote(
            block, block, t_send.at[which, 2], t_recv.at[which, 2], (frame, band_at(by))
        ).start()

    def token_to_sibling(hop):
        from_band = band_at(-hop)
        remote(
            tbuf.at[odd, from_band],
            tbuf.at[sibling_odd, from_band],
            s_send.at[hop],
            s_recv.at[hop],
            sibling,
        ).start()

    here = wbuf.at[:, along, pair, odd]
    grid.begin(here, here, grid.device)
    beside_z = y * NZ + z + 1 - 2 * lax.rem(z, 2)
    beside_y = (y + 1 - 2 * lax.rem(y, 2)) * NZ + z
    remote(
        tokens, tbuf.at[lax.rem(z, 2), band], z_send.at[1], z_recv.at[1 + core], (beside_z, 2 * x)
    ).start()
    remote(
        tokens, tbuf.at[lax.rem(y, 2), band], z_send.at[2], z_recv.at[1 + core], (beside_y, 2 * x + 1)
    ).start()
    grid.begin(
        cross, here, lambda first, second: (frame_at(second, 2 * first + other), band)
    )
    remote(cross, here, z_send.at[0], z_recv.at[0], (beside, band)).start()
    for copy in own[1:5]:
        copy.wait()
    token_along_x(0, tbuf.at[odd, band])
    remote(
        tbuf.at[odd, band], tbuf.at[sibling_odd, band], s_send.at[0], s_recv.at[0], sibling
    ).start()

    tall = lax.broadcasted_iota(jnp.int32, (ROWS, ROWS), 0)
    wide = lax.broadcasted_iota(jnp.int32, (ROWS, ROWS), 1)

    def origin(row):
        return (
            lax.rem(lax.div(row, SHARE), 2) * POSITIONS
            + lax.div(row, 2 * SHARE) * SHARE
            + lax.rem(row, SHARE)
        )

    qkv_sum[...] = jnp.zeros_like(qkv_sum)
    by_peer[...] = jnp.where(wide == origin(tall), 1.0, 0.0).astype(jnp.bfloat16)
    by_frame[...] = jnp.where(tall == origin(wide), 1.0, 0.0).astype(jnp.bfloat16)
    bias[...] = jnp.where(lax.rem(tall, SHARE) == lax.rem(wide, SHARE), 0.0, -1e30)

    for which in range(2):
        await_bytes(tbuf.at[other, 2 * x + which], z_recv.at[1 + which])
        token_along_x(1 + which, tbuf.at[other, 2 * x + which])

    def out_here(half):
        return (z, y) if half == 0 else (y, z)

    def out_device(half, first, second):
        return (second * NZ + first if half == 0 else first * NZ + second, band)

    def turn(way):
        return sign if way == 0 else -sign

    def out_send2(half, way, step, chunk, by=1):
        first, second = out_here(half)
        there = wrap(second + by * turn(way), NY)
        remote(
            chunk,
            chunk,
            o_send.at[half, 1, way],
            o_recv2.at[half, way, step],
            out_device(half, first, there),
        ).start()

    def out_to_first(half, block, by, sem):
        first, second = out_here(half)
        remote(
            block,
            block,
            o_send.at[half, 0, 0],
            o_recv1.at[half, sem],
            out_device(half, wrap(first + by, NY), second),
        ).start()

    def out_along_first():
        for half in range(2):
            first, second = out_here(half)
            block = obuf.at[half, second, first]
            out_to_first(half, block, 2 * sign, 0)
            out_to_first(half, block, -2 * sign, 1)
            out_to_first(half, block, sign, 2)
            out_to_first(half, block, -sign, 2)

    def out_beyond():
        for half in range(2):
            first, second = out_here(half)
            block = obuf.at[half, second, wrap(first - 2 * sign, NY)]
            await_bytes(block, o_recv1.at[half, 0])
            out_to_first(half, block, 2 * sign, 2)
            out_to_first(half, block, sign, 2)
            block = obuf.at[half, second, wrap(first + 2 * sign, NY)]
            await_bytes(block, o_recv1.at[half, 1])
            out_to_first(half, block, -sign, 2)

    def out_along_second(step):
        for half in range(2):
            first, second = out_here(half)
            for way in range(2):
                if step > hops(NY)[way]:
                    continue
                chunk = obuf.at[half, wrap(second - turn(way) * step, NY)]
                if step:
                    await_bytes(chunk, o_recv2.at[half, way, step - 1])
                if step < 3:
                    out_send2(half, way, step, chunk)
                if step == 2 and way == 0:
                    out_send2(half, way, 3, chunk, 2)

    out_along_first()
    for place in range(1, PAIRS):
        grid.along_first(place)

    def ring_step(step):
        def one(place, carry):
            grid.along_second(step, place)
            return carry

        lax.fori_loop(0, PAIRS, one, 0)

    ring_step(1)
    out_beyond()
    for hop in (1, NX - 1):
        await_bytes(tbuf.at[odd, band_at(-hop)], t_recv.at[0, hop])
    token_passed_on(0, sign)
    token_to_sibling(1)
    token_to_sibling(NX - 1)
    ring_step(2)
    for which, by in ((1, 1), (2, -1)):
        for hop in (1, NX - 1):
            await_bytes(
                tbuf.at[other, 2 * wrap(x - hop, NX) + which - 1], t_recv.at[which, hop]
            )
        token_passed_on(which, by)
    await_bytes(tbuf.at[odd, band_at(2)], t_recv.at[0, 2])
    token_to_sibling(2)
    ring_step(3)
    for hop in range(NX):
        from_band = 2 * wrap(x - hop, NX) + 1 - core
        await_bytes(tbuf.at[odd, from_band], s_recv.at[hop])
        if hop == 2:
            for which in range(2):
                await_bytes(
                    tbuf.at[other, 2 * wrap(x - hop, NX) + which], t_recv.at[1 + which, hop]
                )
    ring_step(4)
    await_bytes(wbuf.at[:, along, pair, other], z_recv.at[0])

    chunk = 2 * NZ * DEPTH

    def project(step, right):
        at = pl.ds(pl.multiple_of(step * chunk, HEAD), chunk)
        qkv_sum[...] += jnp.dot(
            tbuf[:, :, :, at].reshape(ROWS, chunk),
            jnp.concatenate([right(slot) for slot in range(3)], axis=1),
            preferred_element_type=jnp.float32,
        )

    @pl.when(core == 0)
    def _():
        def one(step, carry):
            project(step, lambda slot: wbuf[slot, pl.ds(2 * step, 2)].reshape(chunk, HEAD))
            return carry

        lax.fori_loop(0, NY // 2, one, 0)

    @pl.when(core == 1)
    def _():
        def one(step, carry):
            project(
                step,
                lambda slot: jnp.concatenate(
                    [
                        wbuf[slot, :, step, parity].reshape(chunk // 2, HEAD)
                        for parity in range(2)
                    ],
                    axis=0,
                ),
            )
            return carry

        lax.fori_loop(0, NY // 2, one, 0)

    for half in range(2):
        await_bytes(obuf.at[half, out_here(half)[1], 0 : NY - 3], o_recv1.at[half, 2])
    out_along_second(0)
    rounded = qkv_sum[...].astype(jnp.bfloat16)

    msg[...] = (
        jnp.dot(by_peer[...], rounded, preferred_element_type=jnp.float32)
        .reshape(msg.shape)
        .astype(jnp.bfloat16)
    )

    def exchange(stage, source, target):
        def send(step, carry):
            there = lax.rem(me + PEERS // 2 + wander(step) + PEERS, PEERS)
            remote(
                source.at[there], target.at[me], a_send.at[stage], a_recv.at[stage], peer(there)
            ).start()
            return carry

        pltpu.make_async_copy(source.at[me], target.at[me], a_recv.at[stage]).start()
        lax.fori_loop(0, PEERS - 1, send, 0)

    exchange(0, msg, fin)
    spatial = jnp.concatenate(
        [
            attend(
                rounded[at : at + POSITIONS, :HEAD],
                rounded[at : at + POSITIONS, HEAD : 2 * HEAD],
                rounded[at : at + POSITIONS, 2 * HEAD :],
                None,
            )
            for at in (0, POSITIONS)
        ],
        axis=0,
    ).astype(jnp.bfloat16)
    out_along_second(1)

    await_bytes(wbuf.at[:, 0, 0, 0], z_send.at[0])
    await_bytes(tbuf.at[0, 0], z_send.at[1])
    await_bytes(tbuf.at[0, 0], z_send.at[2])
    await_bytes(wbuf.at[:, 0, 0 : PAIRS - 1], w_send.at[0, 0])
    for way in range(2):
        await_bytes(wbuf.at[:, 0 : hops(NY)[way]], w_send.at[1, way])
        await_bytes(obuf.at[way, 0, 0 : NY - 1], o_send.at[way, 0, 0])
    for hop in range(NX):
        await_bytes(tbuf.at[0, 0], s_send.at[hop])
        if hop:
            for which in range(3):
                await_bytes(tbuf.at[0, 0], t_send.at[which, hop])
    await_bytes(fin, a_recv.at[0])
    laid = fin[...].reshape(ROWS, 3 * HEAD)
    mixed = attend(laid[:, :HEAD], laid[:, HEAD : 2 * HEAD], laid[:, 2 * HEAD :], bias[...])
    rmsg[...] = mixed.reshape(rmsg.shape).astype(jnp.bfloat16)
    exchange(1, rmsg, rfin)
    out_along_second(2)
    await_bytes(msg.at[0 : PEERS - 1], a_send.at[0])
    await_bytes(rfin, a_recv.at[1])
    back = jnp.dot(
        by_frame[...], rfin[...].reshape(ROWS, HEAD), preferred_element_type=jnp.float32
    ).astype(jnp.bfloat16)
    temporal = jnp.full((ROWS, HEAD), kind[odd], jnp.int32) == 1
    cbuf[...] = jnp.where(temporal, back, spatial).reshape(cbuf.shape)

    for which, step in ((1, 2), (1, 1), (1, NX - 1), (0, 2), (1, 0), (0, 1), (0, NX - 1)):
        remote(
            cbuf.at[odd if which == 0 else other],
            mbuf.at[band, odd],
            m_send.at[which, step],
            m_recv.at[which, step],
            (frame if which == 0 else beside, band_at(step)),
        ).start()
    remote(
        cbuf.at[odd], mbuf.at[band, odd], n_send.at[0, 0], n_recv.at[0, 0], sibling
    ).start()
    last = pltpu.make_async_copy(cbuf.at[odd], mbuf.at[band, odd], m_recv.at[0, 0])
    last.start()
    for which, hop in ((1, 0), (0, 1), (0, 3), (1, 1), (1, 3), (0, 2), (1, 2)):
        block = mbuf.at[band_at(-hop), odd if which == 0 else other]
        await_bytes(block, m_recv.at[which, hop])
        remote(block, block, n_send.at[which, hop], n_recv.at[which, hop], sibling).start()
    out_along_second(3)
    out_along_second(4)
    last.wait()

    def project_out(source):
        left = jnp.concatenate([mbuf[source, 0], mbuf[source, 1]], axis=1)
        right = jnp.stack([obuf[0, source], obuf[1, :, source]], axis=1).reshape(
            2 * HEAD, WIDTH
        )
        return jnp.dot(left, right, preferred_element_type=jnp.float32)

    def own_core(hop, carry):
        total[...] += project_out(band_at(-hop))
        return carry

    def other_core(hop, carry):
        source = 2 * wrap(x - hop, NX) + 1 - core
        for which in range(2):
            await_bytes(
                mbuf.at[source, sibling_odd if which == 0 else 1 - sibling_odd],
                n_recv.at[which, hop],
            )
        total[...] += project_out(source)
        return carry

    total[...] = jnp.zeros_like(total)
    lax.fori_loop(0, NX, own_core, 0)
    lax.fori_loop(0, NX, other_core, 0)
    sbuf[...] = total[...].astype(jnp.bfloat16).reshape(sbuf.shape)

    def columns(which):
        return out.at[:, pl.ds(pl.multiple_of(which * WIDTH, HEAD), WIDTH)]

    for step in (4, 5, 3, 6, 2, 7, 1):
        there = wrap(band + step, BANDS)
        remote(
            sbuf.at[there], columns(band), f_send.at[step], f_recv.at[step], (frame, there)
        ).start()
    last = pltpu.make_async_copy(sbuf.at[band], columns(band), f_send.at[0])
    last.start()
    for step in range(1, BANDS):
        await_bytes(columns(wrap(band - step, BANDS)), f_recv.at[step])
    last.wait()

    await_bytes(rmsg.at[0 : PEERS - 1], a_send.at[1])
    for which in range(2):
        for hop in range(NX):
            if hop or which:
                await_bytes(cbuf.at[0], m_send.at[which, hop])
            await_bytes(cbuf.at[0], n_send.at[which, hop])
    for half in range(2):
        for way in range(2):
            await_bytes(obuf.at[half, 0 : hops(NY)[way]], o_send.at[half, 1, way])
    for step in range(1, BANDS):
        await_bytes(sbuf.at[0], f_send.at[step])


def body(tokens, qkv_weight, out_weight, head_kind):
    bf16 = jnp.bfloat16
    dma = pltpu.SemaphoreType.DMA
    hbm = pl.BlockSpec(memory_space=pltpu.HBM)
    return pl.pallas_call(
        kernel,
        out_shape=jax.ShapeDtypeStruct(tokens.shape, tokens.dtype),
        in_specs=[hbm] * 4,
        out_specs=hbm,
        scratch_shapes=[
            pltpu.VMEM((3, NY, PAIRS, 2, DEPTH, HEAD), bf16),
            pltpu.VMEM((2, 8, 8, 16, WIDTH), bf16),
            pltpu.VMEM((2, BANDS) + tokens.shape, bf16),
            pltpu.VMEM((PEERS, 2 * SHARE, 3 * HEAD), bf16),
            pltpu.VMEM((PEERS, 2 * SHARE, 3 * HEAD), bf16),
            pltpu.VMEM((PEERS, 2 * SHARE, HEAD), bf16),
            pltpu.VMEM((PEERS, 2 * SHARE, HEAD), bf16),
            pltpu.VMEM((2, POSITIONS, HEAD), bf16),
            pltpu.VMEM((BANDS, 2, POSITIONS, HEAD), bf16),
            pltpu.VMEM((BANDS, 16, WIDTH), bf16),
            pltpu.VMEM((ROWS, 3 * HEAD), jnp.float32),
            pltpu.VMEM((POSITIONS, WIDTH), jnp.float32),
            pltpu.VMEM((ROWS, ROWS), bf16),
            pltpu.VMEM((ROWS, ROWS), bf16),
            pltpu.VMEM((ROWS, ROWS), jnp.float32),
            pltpu.SMEM((2,), jnp.int32),
            pltpu.VMEM((3, DEPTH, HEAD), bf16),
            dma((6,)),
            dma((3,)),
            dma((3,)),
            dma((2, 2)),
            dma((4,)),
            dma((2, 4, 4)),
            dma((2, 2, 2)),
            dma((2, 3)),
            dma((2, 2, 4)),
            dma((3, NX)),
            dma((3, NX)),
            dma((NX,)),
            dma((NX,)),
            dma((2,)),
            dma((2,)),
            dma((2, NX)),
            dma((2, NX)),
            dma((2, NX)),
            dma((2, NX)),
            dma((BANDS,)),
            dma((BANDS,)),
        ],
        compiler_params=pltpu.CompilerParams(
            collective_id=0, has_side_effects=True, vmem_limit_bytes=64 * 1024 * 1024
        ),
    )(tokens, qkv_weight.transpose(1, 0, 2), out_weight, head_kind)


def solution(mesh):
    return jax.shard_map(
        body,
        mesh=mesh,
        in_specs=(
            P(("frame", "band"), None),
            P("frame", None, "band"),
            P("frame", "band"),
            P("band"),
        ),
        out_specs=P(("frame", "band"), None),
        check_vma=False,
    )
```
